32 devices in a mesh: groups: 2 (over y), tiles: 4 (over z), freq: 2 (over x), field: 2 (over core).
Axes of the slice: x: 2, y: 2, z: 4, core: 2. Of those that a mesh axis runs over, the one named last changes fastest.
Arguments:
- fields: bfloat16 [2, 4, 512, 1024], P('field', 'tiles', ('groups', 'freq')), parts along dimension 2, may hold values from -7.5 to 7.5
- slot_tile_ids: int32 [4], replicated, may hold values from 0 to 3, each once
- neighbour_tile_ids: int32 [4, 4], replicated, may hold values from 0 to 3
- neighbour_rotation_code: int32 [4, 4], replicated, may hold values from 0 to 7
- paired_tile_ids: int32 [4, 2], P('tiles'), may hold values from 0 to 3
Outputs:
- csd: float32 [8, 2, 2, 32, 128, 128], P(('groups', 'tiles'), None, None, ('freq', 'field')), parts along dimension 0
The draws below stay inside these ranges and needn't reach their ends.
There are 2 independent parts, one for each index of `groups`. The reference program is written for one: setup_inputs(seed, part) draws one part's arguments, and reference() takes and returns one part's arrays. A program takes and returns all parts, laid end to end along the dimension named above; an argument that names none is the same for every part. Nothing has to cross between parts.
All inputs are finite; a program needn't handle non-finite values.
Results may differ from the reference program's by a relative error of at most 0.0095.
Values may be sent and summed in bfloat16 or wider, within the bound.
No kernel may reach another device: no remote copies, remote signals or barrier semaphores. Data moves between devices by JAX's collectives and lax.ppermute only.
A program may use at most 64 MiB of HBM per device.

```python
import math
import jax
import jax.numpy as jnp
from jax import lax

SIDE = 32
PARTNERS_EACH = 2
SEGLEN = 64
SMOOTH = 2
SLOT_COUNT = 4
SEGS = 4
TIME_SAMPLES = 256
TILE_CELLS = 1024


def draw_fields(key, part):
    leading = (2, SLOT_COUNT, TIME_SAMPLES, 1)
    streams = jax.random.split(jax.random.fold_in(key, 17), 4)
    cell_index = jnp.arange(TILE_CELLS, dtype=jnp.int32)
    row_index = cell_index // SIDE
    col_index = cell_index % SIDE
    row_sign = (1 - 2 * (row_index % 2)).astype(jnp.float32)
    col_sign = (1 - 2 * (col_index % 2)).astype(jnp.float32)
    row_cos = jnp.where(row_index % 2 == 0, 1 - row_index % 4, 0).astype(jnp.float32)
    row_sin = jnp.where(row_index % 2 == 1, 2 - row_index % 4, 0).astype(jnp.float32)
    col_cos = jnp.where(col_index % 2 == 0, 1 - col_index % 4, 0).astype(jnp.float32)
    col_sin = jnp.where(col_index % 2 == 1, 2 - col_index % 4, 0).astype(jnp.float32)
    wave_shape = (2, SLOT_COUNT, TIME_SAMPLES, 4)
    jitter_shape = (2, SLOT_COUNT, TIME_SAMPLES, TILE_CELLS)
    row_amp = 1.2 * jax.random.truncated_normal(streams[0], -1.7, 1.7, leading, jnp.float32)
    col_amp = 1.2 * jax.random.truncated_normal(streams[1], -1.7, 1.7, leading, jnp.float32)
    wave_amp = jax.random.truncated_normal(streams[2], -1.7, 1.7, wave_shape, jnp.float32)
    jitter_part = 0.35 * jax.random.truncated_normal(streams[3], -3.0, 3.0, jitter_shape, jnp.float32)
    wave_part = wave_amp[..., 0:1] * (row_cos * col_cos) + wave_amp[..., 1:2] * (row_cos * col_sin)
    wave_part = wave_part + wave_amp[..., 2:3] * (row_sin * col_cos) + wave_amp[..., 3:4] * (row_sin * col_sin)
    values = row_amp * row_sign + col_amp * col_sign + wave_part + jitter_part
    return values.astype(jnp.bfloat16)


def place_ends(array, own_key, low, largest):
    longest = array.shape.index(max(array.shape))
    spots = []
    for shift in (0, 1):
        where = [jax.random.randint(jax.random.fold_in(own_key, axis), (), 0, length) for axis, length in enumerate(array.shape)]
        where[longest] = (where[longest] + shift) % array.shape[longest]
        spots.append(tuple(where))
    return array.at[spots[0]].set(low).at[spots[1]].set(largest)


def setup_inputs(seed: int = 0, part: int = 0) -> dict:
    splits = jax.random.split(jax.random.key(seed), 6)
    part_keys = jax.random.split(jax.random.fold_in(splits[5], part), 6)
    return {
        "fields": draw_fields(jax.random.fold_in(jax.random.fold_in(splits[5], part), 71), part),
        "slot_tile_ids": jax.random.permutation(splits[1], SLOT_COUNT).astype(jnp.int32),
        "neighbour_tile_ids": place_ends(jax.random.randint(splits[2], (SLOT_COUNT, 4), 0, SLOT_COUNT), jax.random.fold_in(splits[2], 1), 0, SLOT_COUNT - 1).astype(jnp.int32),
        "neighbour_rotation_code": place_ends(jax.random.randint(splits[3], (SLOT_COUNT, 4), 0, 8), jax.random.fold_in(splits[3], 1), 0, 7).astype(jnp.int32),
        "paired_tile_ids": place_ends(jax.random.randint(splits[4], (SLOT_COUNT, PARTNERS_EACH), 0, SLOT_COUNT), jax.random.fold_in(splits[4], 1), 0, SLOT_COUNT - 1).astype(jnp.int32),
    }


diffusion = 0.25


def slot_lookup(slot_tile_ids, tile_ids):
    matches = (slot_tile_ids[None, :] == tile_ids.reshape(-1)[:, None]).astype(jnp.int32)
    positions = jnp.sum(matches * jnp.arange(slot_tile_ids.shape[0], dtype=jnp.int32)[None, :], axis=1)
    return positions.reshape(tile_ids.shape).astype(jnp.int32)


def tile_edges(field, tile_side):
    cell_count = field.shape[-1]
    north = field[..., :tile_side]
    east = field[..., tile_side - 1::tile_side]
    south = field[..., cell_count - tile_side:]
    west = field[..., ::tile_side]
    return jnp.stack([north, east, south, west], axis=-3)


def pick_rims(all_edges, near_slots, codes):
    chosen = all_edges[near_slots, codes % 4]
    flipped = chosen[..., ::-1]
    return jnp.where((codes // 4 == 1)[:, :, None, None], flipped, chosen)


def smooth_step(field, rims, tile_side):
    cell_count = field.shape[-1]
    values = field.astype(jnp.float32)
    edge_vals = rims.astype(jnp.float32)
    above_row = jnp.concatenate([edge_vals[:, 0], values[..., :cell_count - tile_side]], axis=-1)
    below_row = jnp.concatenate([values[..., tile_side:], edge_vals[:, 2]], axis=-1)
    column_pos = jnp.arange(cell_count, dtype=jnp.int32) % tile_side
    west_full = jnp.repeat(edge_vals[:, 3], tile_side, axis=-1)
    east_full = jnp.repeat(edge_vals[:, 1], tile_side, axis=-1)
    leftward = jnp.where(column_pos == 0, west_full, jnp.roll(values, 1, axis=-1))
    rightward = jnp.where(column_pos == tile_side - 1, east_full, jnp.roll(values, -1, axis=-1))
    laplace = above_row + below_row + leftward + rightward - 4.0 * values
    return (values + diffusion * laplace).astype(jnp.bfloat16)


def coarse_sums(field, tile_side):
    leading = field.shape[:-1]
    blocks = field.astype(jnp.float32).reshape(leading + (tile_side // 2, 2, tile_side // 4, 4))
    return jnp.sum(blocks, axis=(-3, -1)).reshape(leading + ((tile_side // 2) * (tile_side // 4),))


def window_table(seg_length):
    samples = jnp.arange(seg_length, dtype=jnp.int32)
    frequency = jnp.arange(seg_length // 2, dtype=jnp.int32)
    products = (frequency[:, None] * samples[None, :]) % seg_length
    angles = (2.0 * math.pi / seg_length) * products.astype(jnp.float32)
    window = 0.5 - 0.5 * jnp.cos((2.0 * math.pi / seg_length) * samples.astype(jnp.float32))
    dft_table = jnp.stack([window[None, :] * jnp.cos(angles), -window[None, :] * jnp.sin(angles)])
    return dft_table, jnp.sum(window * window)


def segment_spectra(coarse, dft_table):
    leading = coarse.shape[0]
    segments = coarse.reshape(leading, -1, dft_table.shape[-1], coarse.shape[-1])
    spectra = jnp.einsum("cft,nstp->nscfp", dft_table, segments, precision=lax.Precision.HIGHEST)
    return spectra.astype(jnp.bfloat16)


def reference(fields, slot_tile_ids, neighbour_tile_ids, neighbour_rotation_code, paired_tile_ids):
    near_slots = slot_lookup(slot_tile_ids, neighbour_tile_ids)
    partner_slots = slot_lookup(slot_tile_ids, paired_tile_ids)
    dft_table, window_power = window_table(SEGLEN)
    spectra = []
    for field_index in range(2):
        field = fields[field_index]
        for sweep_index in range(SMOOTH):
            rims = pick_rims(tile_edges(field, SIDE), near_slots, neighbour_rotation_code)
            field = smooth_step(field, rims, SIDE)
        spectra.append(segment_spectra(coarse_sums(field, SIDE), dft_table))
    height = spectra[0].astype(jnp.float32)
    partner = spectra[1][partner_slots].astype(jnp.float32)
    rotated = jnp.stack([height[:, :, 1], -height[:, :, 0]], axis=2)
    stacked = jnp.stack([height, rotated], axis=1)
    cross = jnp.einsum("noscfi,nkscfj->nkofij", stacked, partner, precision=lax.Precision.HIGHEST)
    return cross / (SEGS * window_power)
```

```python
import functools
import math

import jax
import jax.numpy as jnp
import ml_dtypes
import numpy as np
from jax import lax
from jax.experimental import pallas as pl
from jax.experimental.pallas import tpu as pltpu
from jax.sharding import PartitionSpec as P

SIDE = 32
SEGLEN = 64
LANES = 128
BLOCKS = SIDE // 2
CORNER_ROWS = 16
FREQS = SEGLEN // 2

NORTH, EAST, SOUTH, WEST = range(4)
EDGE_CORNERS = ((0, 1), (1, 3), (2, 3), (0, 2))
END_RIMS = (
    ((WEST, 0), (EAST, 0)),
    ((NORTH, 1), (SOUTH, 1)),
    ((WEST, 1), (EAST, 1)),
    ((NORTH, 0), (SOUTH, 0)),
)


def split_bf16(values):
    high = values.astype(ml_dtypes.bfloat16)
    low = (values - high.astype(np.float64)).astype(ml_dtypes.bfloat16)
    return high, low


@functools.lru_cache(maxsize=None)
def cell_tables():
    cells = SIDE * SIDE

    def at(row, column):
        return row * SIDE + column

    near = np.zeros((cells, cells))
    pool = np.zeros((cells, LANES))
    for row in range(SIDE):
        for column in range(SIDE):
            pool[at(row, column), (row // 2) * (SIDE // 4) + column // 4] = 1
            for down, right in ((1, 0), (-1, 0), (0, 1), (0, -1)):
                if 0 <= row + down < SIDE and 0 <= column + right < SIDE:
                    near[at(row + down, column + right), at(row, column)] = 1
    last = SIDE - 1
    outer = [[at(0, i), at(i, last), at(last, i), at(i, 0)] for i in range(SIDE)]
    inner = [[at(1, i), at(i, last - 1), at(last - 1, i), at(i, 1)] for i in range(SIDE)]
    carried = np.zeros((cells, 4 * BLOCKS))
    sums = np.zeros((cells, 4 * BLOCKS))
    for edge in range(4):
        for i in range(SIDE):
            block = edge * BLOCKS + i // 2
            sums[outer[i][edge], block] += 1
            carried[outer[i][edge], block] += 1
            carried[inner[i][edge], block] += 1
            if i > 0:
                carried[outer[i - 1][edge], block] += 2
            if i < last:
                carried[outer[i + 1][edge], block] += 2
    cell_map = np.concatenate([near @ near @ pool, carried, sums], axis=1)
    first_corners = np.zeros((CORNER_ROWS, LANES))
    last_corners = np.zeros((CORNER_ROWS, LANES))
    first_corners[0, 0] = 1
    first_corners[1, last] = 1
    last_corners[2, LANES - SIDE] = 1
    last_corners[3, LANES - 1] = 1
    to_bf16 = lambda table: table.astype(ml_dtypes.bfloat16)
    return to_bf16(cell_map), to_bf16(first_corners), to_bf16(last_corners)


@functools.lru_cache(maxsize=None)
def time_tables(bands, samples):
    per_band = FREQS // bands
    segments = samples // SEGLEN
    time = np.arange(SEGLEN)
    frequency = np.arange(FREQS)
    angles = 2.0 * math.pi / SEGLEN * (frequency[:, None] * time[None, :] % SEGLEN)
    window = 0.5 - 0.5 * np.cos(2.0 * math.pi / SEGLEN * time)
    waves = np.stack([window * np.cos(angles), -window * np.sin(angles)]) / 16.0
    table = np.zeros((bands, segments, 2, per_band, segments, SEGLEN))
    for segment in range(segments):
        table[:, segment, :, :, segment, :] = waves.reshape(2, bands, per_band, SEGLEN).transpose(1, 0, 2, 3)
    table = table.reshape(bands * segments * 2 * per_band, samples)
    high, low = split_bf16(table)
    return high, low, np.ascontiguousarray(high.T), np.ascontiguousarray(low.T)


def dot(left, right):
    return jnp.dot(left, right, preferred_element_type=jnp.float32)


def transform_kernel(
    devices, place_ref, x_ref, cells_ref, first_ref, last_ref, high_ref, low_ref, high_t_ref, low_t_ref, *rest
):
    outs, spectra_ref = rest[:devices], rest[devices]
    place = place_ref[0]
    rows = high_ref.shape[0] // devices
    x = x_ref[...]
    sums = dot(x, cells_ref[...])
    sums_high = sums.astype(jnp.bfloat16)
    sums_low = (sums - sums_high.astype(jnp.float32)).astype(jnp.bfloat16)
    high = high_ref[...]
    spectra_ref[...] = dot(high, sums_high) + (dot(high, sums_low) + dot(low_ref[...], sums_high))
    across = (((1,), (1,)), ((), ()))
    corners = lax.dot_general(first_ref[...], x[:, :LANES], across, preferred_element_type=jnp.float32)
    corners += lax.dot_general(
        last_ref[...], x[:, SIDE * SIDE - LANES :], across, preferred_element_type=jnp.float32
    )
    corners = corners.astype(jnp.bfloat16)
    corner_spectra = dot(corners, high_t_ref[...]) + dot(corners, low_t_ref[...])
    field, half = place % 2, place // 2
    lane_start = field * (LANES // 2) + half * rows
    lane = lax.broadcasted_iota(jnp.int32, (CORNER_ROWS, LANES), 1)
    mine = (lane >= lane_start) & (lane < lane_start + rows)
    for step in range(devices):
        band = jnp.bitwise_xor(place, step)
        start = pl.multiple_of(band * rows, rows)
        block = spectra_ref[pl.ds(start, rows), :].astype(jnp.bfloat16)
        outs[step][0:rows, :] = block[:, :LANES]
        outs[step][rows : 2 * rows, :] = block[:, LANES:]
        turned = pltpu.roll(corner_spectra, lax.rem(lane_start - start + LANES, LANES), 1)
        outs[step][2 * rows : 2 * rows + CORNER_ROWS, :] = jnp.where(mine, turned, 0.0).astype(jnp.bfloat16)


def collect_kernel(devices, place_ref, *rest):
    blocks, (band_ref, height_ref, held_ref) = rest[:devices], rest[devices:]
    place = place_ref[0]
    rows = (blocks[0].shape[0] - CORNER_ROWS) // 2
    total = height_ref.shape[0]
    corners = jnp.zeros((CORNER_ROWS, LANES), jnp.float32)
    for step in range(devices):
        source = jnp.bitwise_xor(place, step)
        field, half = source % 2, source // 2
        start = pl.multiple_of(field * total + half * rows, rows)
        held_ref[pl.ds(start, rows), :] = blocks[step][0:rows, :]
        held_ref[pl.ds(2 * total + start, rows), :] = blocks[step][rows : 2 * rows, :]
        corners += blocks[step][2 * rows :, :].astype(jnp.float32)
    height_ref[...] = held_ref[0:total, :]
    band_ref[0 : 3 * total, :] = held_ref[total : 4 * total, :]
    band_ref[3 * total :, :] = corners.astype(jnp.bfloat16)


def placement_kernel(
    tile_ref, ids_ref, near_ids_ref, codes_ref, paired_ref, map_ref, corner_map_ref, slot_ref, wide_ref, corner_ref
):
    slots = ids_ref.shape[0]
    tile = tile_ref[0]

    def invert(slot, carry):
        slot_ref[ids_ref[slot]] = slot
        return carry

    lax.fori_loop(0, slots, invert, 0, unroll=slots <= 8)
    wide_ref[...] = jnp.zeros_like(wide_ref)
    corner_ref[...] = jnp.zeros_like(corner_ref)
    block = lax.broadcasted_iota(jnp.int32, (BLOCKS, LANES), 0)
    cell = lax.broadcasted_iota(jnp.int32, (BLOCKS, LANES), 1)
    corner_row = lax.broadcasted_iota(jnp.int32, (CORNER_ROWS, LANES), 0)
    corner_cell = lax.broadcasted_iota(jnp.int32, (CORNER_ROWS, LANES), 1)

    def target(edge, position):
        if edge == NORTH:
            return position // 2
        if edge == EAST:
            return position * (SIDE // 4) + SIDE // 4 - 1
        if edge == SOUTH:
            return LANES - SIDE // 4 + position // 2
        return position * (SIDE // 4)

    def turn(position, reverse):
        return position + reverse * (BLOCKS - 1 - 2 * position)

    partners = paired_ref.shape[1]
    wanted = [tile] + [slot_ref[paired_ref[0, partner]] for partner in range(partners)]
    for index, slot in enumerate(wanted):
        columns = slice(index * LANES, (index + 1) * LANES)
        for edge in range(4):
            near = slot_ref[near_ids_ref[slot, edge]]
            code = codes_ref[slot, edge]
            touching, reverse = code % 4, code // 4
            pattern = (cell == target(edge, turn(block, reverse))).astype(jnp.float32)
            start = pl.multiple_of(jnp.bitwise_xor(tile, near) * LANES + touching * BLOCKS, BLOCKS)
            wide_ref[pl.ds(start, BLOCKS), columns] += pattern
            beyond = slot_ref[near_ids_ref[near, touching]]
            beyond_code = codes_ref[near, touching]
            reverse_both = jnp.bitwise_xor(reverse, beyond_code // 4)
            pattern = (cell == target(edge, turn(block, reverse_both))).astype(jnp.float32)
            start = pl.multiple_of(
                jnp.bitwise_xor(tile, beyond) * LANES + 4 * BLOCKS + (beyond_code % 4) * BLOCKS, BLOCKS
            )
            wide_ref[pl.ds(start, BLOCKS), columns] += pattern
            for end in range(2):
                rim_edge = jnp.int32(0)
                rim_end = jnp.int32(0)
                for option in range(4):
                    rim_edge = jnp.where(touching == option, END_RIMS[option][end][0], rim_edge)
                    rim_end = jnp.where(touching == option, END_RIMS[option][end][1], rim_end)
                other = slot_ref[near_ids_ref[near, rim_edge]]
                other_code = codes_ref[near, rim_edge]
                other_end = jnp.bitwise_xor(rim_end, other_code // 4)
                corner = jnp.int32(0)
                for option in range(4):
                    for which in range(2):
                        corner = jnp.where(
                            (other_code % 4 == option) & (other_end == which), EDGE_CORNERS[option][which], corner
                        )
                position = turn((BLOCKS - 1) * end, reverse)
                hit = (corner_row == corner) & (corner_cell == target(edge, position))
                start = pl.multiple_of(jnp.bitwise_xor(tile, other) * CORNER_ROWS, CORNER_ROWS)
                corner_ref[pl.ds(start, CORNER_ROWS), columns] += hit.astype(jnp.float32)
    map_ref[...] = wide_ref[...].astype(jnp.bfloat16)
    corner_map_ref[...] = corner_ref[...].astype(jnp.bfloat16)


def density_kernel(
    tiles, scale, per_band, tile_ref, ids_ref, paired_ref, height_ref, map_ref, corner_map_ref, *rest
):
    bands, (out_ref, turned_ref, partner_ref) = rest[:tiles], rest[tiles:]
    total = height_ref.shape[0]
    partners = paired_ref.shape[1]
    step_freqs = out_ref.shape[3]

    @pl.when(pl.program_id(0) == 0)
    def _():
        tile = tile_ref[0]
        height_rims = jnp.concatenate([band[total : 2 * total, :] for band in bands], axis=1)
        velocity_rims = jnp.concatenate([band[2 * total : 3 * total, :] for band in bands], axis=1)
        corners = jnp.concatenate([band[3 * total :, :] for band in bands], axis=0)
        corner_part = lax.dot_general(
            corners, corner_map_ref[...], (((0,), (0,)), ((), ())), preferred_element_type=jnp.float32
        )
        height = height_ref[...].astype(jnp.float32) + dot(height_rims, map_ref[:, :LANES])
        height = height + corner_part[:total, :LANES]
        velocity = dot(velocity_rims, map_ref[:, LANES:]) + corner_part[total:, LANES:]
        own = []
        for partner in range(partners):
            slot = jnp.int32(0)
            for candidate in range(ids_ref.shape[0]):
                slot = jnp.where(ids_ref[candidate] == paired_ref[0, partner], candidate, slot)
            wanted = jnp.bitwise_xor(tile, slot)
            chosen = bands[0][0:total, :]
            for step in range(1, tiles):
                chosen = jnp.where(wanted == step, bands[step][0:total, :], chosen)
            own.append(chosen.astype(jnp.float32))
        velocity = velocity + jnp.concatenate(own, axis=1)
        partner_ref[...] = velocity.astype(jnp.bfloat16)
        height = height.astype(jnp.bfloat16).astype(jnp.float32)
        row = lax.broadcasted_iota(jnp.int32, height.shape, 0)
        rotated = jnp.where(
            (row // per_band) % 2 == 0,
            pltpu.roll(height, total - per_band, 0),
            -pltpu.roll(height, per_band, 0),
        )
        turned_ref[0:LANES, :] = height.T
        turned_ref[LANES:, :] = rotated.T

    lane = lax.broadcasted_iota(jnp.int32, turned_ref.shape, 1)
    for offset in range(step_freqs):
        frequency = pl.program_id(0) * step_freqs + offset
        left = jnp.where(lane % per_band == frequency, turned_ref[...], 0.0).astype(jnp.bfloat16)
        cross = dot(left, partner_ref[...]) * scale
        for partner in range(partners):
            for part in range(2):
                out_ref[0, partner, part, offset] = cross[
                    part * LANES : (part + 1) * LANES, partner * LANES : (partner + 1) * LANES
                ]


SMEM = pl.BlockSpec(memory_space=pltpu.SMEM)
VMEM = pl.BlockSpec(memory_space=pltpu.VMEM)


def shards(tiles, freqs, field_count, fields, slot_tile_ids, neighbour_tile_ids, neighbour_rotation_code, paired_tile_ids):
    field = fields.reshape(fields.shape[2], fields.shape[3])
    samples = field.shape[0]
    devices = freqs * field_count
    per_band = FREQS // devices
    rows = samples // SEGLEN * 2 * per_band
    total = freqs * rows
    partners = paired_tile_ids.shape[1]
    tile = lax.axis_index("tiles").astype(jnp.int32).reshape(1)
    place = (lax.axis_index("freq") * field_count + lax.axis_index("field")).astype(jnp.int32).reshape(1)

    def swap(value, axes, count, step):
        return lax.ppermute(value, axes, [(i, i ^ step) for i in range(count)])

    piece = jax.ShapeDtypeStruct((2 * rows + CORNER_ROWS, LANES), jnp.bfloat16)
    pieces = pl.pallas_call(
        functools.partial(transform_kernel, devices),
        out_shape=[piece] * devices,
        in_specs=[SMEM] + [VMEM] * 8,
        out_specs=[VMEM] * devices,
        scratch_shapes=[pltpu.VMEM((samples, 2 * LANES), jnp.float32)],
        name="transform",
    )(place, field, *cell_tables(), *time_tables(devices, samples))
    pieces = [pieces[0]] + [
        swap(pieces[step], ("freq", "field"), devices, step) for step in range(1, devices)
    ]

    cell_map, corner_map = pl.pallas_call(
        placement_kernel,
        out_shape=[
            jax.ShapeDtypeStruct((tiles * LANES, (1 + partners) * LANES), jnp.bfloat16),
            jax.ShapeDtypeStruct((tiles * CORNER_ROWS, (1 + partners) * LANES), jnp.bfloat16),
        ],
        in_specs=[SMEM] * 5,
        out_specs=[VMEM] * 2,
        scratch_shapes=[
            pltpu.SMEM((tiles,), jnp.int32),
            pltpu.VMEM((tiles * LANES, (1 + partners) * LANES), jnp.float32),
            pltpu.VMEM((tiles * CORNER_ROWS, (1 + partners) * LANES), jnp.float32),
        ],
        name="placement",
    )(tile, slot_tile_ids, neighbour_tile_ids, neighbour_rotation_code, paired_tile_ids)

    band, height = pl.pallas_call(
        functools.partial(collect_kernel, devices),
        out_shape=[
            jax.ShapeDtypeStruct((3 * total + CORNER_ROWS, LANES), jnp.bfloat16),
            jax.ShapeDtypeStruct((total, LANES), jnp.bfloat16),
        ],
        in_specs=[SMEM] + [VMEM] * devices,
        out_specs=[VMEM] * 2,
        scratch_shapes=[pltpu.VMEM((4 * total, LANES), jnp.bfloat16)],
        name="collect",
    )(place, *pieces)
    bands = [band] + [swap(band, "tiles", tiles, step) for step in range(1, tiles)]

    segments = freqs * samples // SEGLEN
    scale = 1.0 / (segments * SEGLEN * 0.375)
    step_freqs = 2
    block = (1, partners, 2, step_freqs, LANES, LANES)
    return pl.pallas_call(
        functools.partial(density_kernel, tiles, scale, per_band),
        out_shape=jax.ShapeDtypeStruct((1, partners, 2, per_band, LANES, LANES), jnp.float32),
        grid=(per_band // step_freqs,),
        in_specs=[SMEM] * 3 + [VMEM] * (3 + tiles),
        out_specs=pl.BlockSpec(block, lambda i: (0, 0, 0, i, 0, 0)),
        scratch_shapes=[
            pltpu.VMEM((2 * LANES, total), jnp.float32),
            pltpu.VMEM((total, partners * LANES), jnp.bfloat16),
        ],
        name="density",
    )(tile, slot_tile_ids, paired_tile_ids, height, cell_map, corner_map, *bands)


def solution(mesh):
    placed = (P("field", "tiles", ("groups", "freq"), None), P(), P(), P(), P("tiles", None))
    return jax.shard_map(
        functools.partial(shards, mesh.shape["tiles"], mesh.shape["freq"], mesh.shape["field"]),
        mesh=mesh,
        in_specs=placed,
        out_specs=P(("groups", "tiles"), None, None, ("freq", "field"), None, None),
        check_vma=False,
    )
```

```python
import functools
import math

import jax
import jax.numpy as jnp
import ml_dtypes
import numpy as np
from jax import lax
from jax.experimental import pallas as pl
from jax.experimental.pallas import tpu as pltpu
from jax.sharding import PartitionSpec as P

SIDE = 32
SEGLEN = 64
LANES = 128
BLOCKS = SIDE // 2
CORNER_ROWS = 16
FREQS = SEGLEN // 2

NORTH, EAST, SOUTH, WEST = range(4)
EDGE_CORNERS = ((0, 1), (1, 3), (2, 3), (0, 2))
END_RIMS = (
    ((WEST, 0), (EAST, 0)),
    ((NORTH, 1), (SOUTH, 1)),
    ((WEST, 1), (EAST, 1)),
    ((NORTH, 0), (SOUTH, 0)),
)


def split_bf16(values):
    high = values.astype(ml_dtypes.bfloat16)
    low = (values - high.astype(np.float64)).astype(ml_dtypes.bfloat16)
    return high, low


@functools.lru_cache(maxsize=None)
def cell_tables():
    cells = SIDE * SIDE

    def at(row, column):
        return row * SIDE + column

    near = np.zeros((cells, cells))
    pool = np.zeros((cells, LANES))
    for row in range(SIDE):
        for column in range(SIDE):
            pool[at(row, column), (row // 2) * (SIDE // 4) + column // 4] = 1
            for down, right in ((1, 0), (-1, 0), (0, 1), (0, -1)):
                if 0 <= row + down < SIDE and 0 <= column + right < SIDE:
                    near[at(row + down, column + right), at(row, column)] = 1
    last = SIDE - 1
    outer = [[at(0, i), at(i, last), at(last, i), at(i, 0)] for i in range(SIDE)]
    inner = [[at(1, i), at(i, last - 1), at(last - 1, i), at(i, 1)] for i in range(SIDE)]
    carried = np.zeros((cells, 4 * BLOCKS))
    sums = np.zeros((cells, 4 * BLOCKS))
    for edge in range(4):
        for i in range(SIDE):
            block = edge * BLOCKS + i // 2
            sums[outer[i][edge], block] += 1
            carried[outer[i][edge], block] += 1
            carried[inner[i][edge], block] += 1
            if i > 0:
                carried[outer[i - 1][edge], block] += 2
            if i < last:
                carried[outer[i + 1][edge], block] += 2
    cell_map = np.concatenate([near @ near @ pool, carried, sums], axis=1)
    first_corners = np.zeros((CORNER_ROWS, LANES))
    last_corners = np.zeros((CORNER_ROWS, LANES))
    first_corners[0, 0] = 1
    first_corners[1, last] = 1
    last_corners[2, LANES - SIDE] = 1
    last_corners[3, LANES - 1] = 1
    to_bf16 = lambda table: table.astype(ml_dtypes.bfloat16)
    return to_bf16(cell_map), to_bf16(first_corners), to_bf16(last_corners)


@functools.lru_cache(maxsize=None)
def time_tables(bands, samples):
    per_band = FREQS // bands
    segments = samples // SEGLEN
    time = np.arange(SEGLEN)
    frequency = np.arange(FREQS)
    angles = 2.0 * math.pi / SEGLEN * (frequency[:, None] * time[None, :] % SEGLEN)
    window = 0.5 - 0.5 * np.cos(2.0 * math.pi / SEGLEN * time)
    waves = np.stack([window * np.cos(angles), -window * np.sin(angles)]) / 16.0
    table = np.zeros((bands, segments, 2, per_band, segments, SEGLEN))
    for segment in range(segments):
        table[:, segment, :, :, segment, :] = waves.reshape(2, bands, per_band, SEGLEN).transpose(1, 0, 2, 3)
    table = table.reshape(bands * segments * 2 * per_band, samples)
    high, low = split_bf16(table)
    return high, low, np.ascontiguousarray(high.T), np.ascontiguousarray(low.T)


def dot(left, right):
    return jnp.dot(left, right, preferred_element_type=jnp.float32)


def transform_kernel(
    devices, place_ref, x_ref, cells_ref, first_ref, last_ref, high_ref, low_ref, high_t_ref, low_t_ref, *rest
):
    outs, spectra_ref = rest[:devices], rest[devices]
    place = place_ref[0]
    rows = high_ref.shape[0] // devices
    x = x_ref[...]
    sums = dot(x, cells_ref[...])
    sums_high = sums.astype(jnp.bfloat16)
    sums_low = (sums - sums_high.astype(jnp.float32)).astype(jnp.bfloat16)
    high = high_ref[...]
    spectra_ref[...] = dot(high, sums_high) + (dot(high, sums_low) + dot(low_ref[...], sums_high))
    across = (((1,), (1,)), ((), ()))
    corners = lax.dot_general(first_ref[...], x[:, :LANES], across, preferred_element_type=jnp.float32)
    corners += lax.dot_general(
        last_ref[...], x[:, SIDE * SIDE - LANES :], across, preferred_element_type=jnp.float32
    )
    corners = corners.astype(jnp.bfloat16)
    corner_spectra = dot(corners, high_t_ref[...]) + dot(corners, low_t_ref[...])
    field, half = place % 2, place // 2
    lane_start = field * (LANES // 2) + half * rows
    lane = lax.broadcasted_iota(jnp.int32, (CORNER_ROWS, LANES), 1)
    mine = (lane >= lane_start) & (lane < lane_start + rows)
    for step in range(devices):
        band = jnp.bitwise_xor(place, step)
        start = pl.multiple_of(band * rows, rows)
        block = spectra_ref[pl.ds(start, rows), :].astype(jnp.bfloat16)
        outs[step][0:rows, :] = block[:, :LANES]
        outs[step][rows : 2 * rows, :] = block[:, LANES:]
        turned = pltpu.roll(corner_spectra, lax.rem(lane_start - start + LANES, LANES), 1)
        outs[step][2 * rows : 2 * rows + CORNER_ROWS, :] = jnp.where(mine, turned, 0.0).astype(jnp.bfloat16)


def collect_kernel(devices, place_ref, *rest):
    blocks, (band_ref, height_ref, held_ref) = rest[:devices], rest[devices:]
    place = place_ref[0]
    rows = (blocks[0].shape[0] - CORNER_ROWS) // 2
    total = height_ref.shape[0]
    corners = jnp.zeros((CORNER_ROWS, LANES), jnp.float32)
    for step in range(devices):
        source = jnp.bitwise_xor(place, step)
        field, half = source % 2, source // 2
        start = pl.multiple_of(field * total + half * rows, rows)
        held_ref[pl.ds(start, rows), :] = blocks[step][0:rows, :]
        held_ref[pl.ds(2 * total + start, rows), :] = blocks[step][rows : 2 * rows, :]
        corners += blocks[step][2 * rows :, :].astype(jnp.float32)
    height_ref[...] = held_ref[0:total, :]
    band_ref[0 : 3 * total, :] = held_ref[total : 4 * total, :]
    band_ref[3 * total :, :] = corners.astype(jnp.bfloat16)


def placement_kernel(
    tile_ref, ids_ref, near_ids_ref, codes_ref, paired_ref, map_ref, corner_map_ref, slot_ref, wide_ref, corner_ref
):
    slots = ids_ref.shape[0]
    tile = tile_ref[0]

    def invert(slot, carry):
        slot_ref[ids_ref[slot]] = slot
        return carry

    lax.fori_loop(0, slots, invert, 0, unroll=slots <= 8)
    wide_ref[...] = jnp.zeros_like(wide_ref)
    corner_ref[...] = jnp.zeros_like(corner_ref)
    block = lax.broadcasted_iota(jnp.int32, (BLOCKS, LANES), 0)
    cell = lax.broadcasted_iota(jnp.int32, (BLOCKS, LANES), 1)
    corner_row = lax.broadcasted_iota(jnp.int32, (CORNER_ROWS, LANES), 0)
    corner_cell = lax.broadcasted_iota(jnp.int32, (CORNER_ROWS, LANES), 1)

    def target(edge, position):
        if edge == NORTH:
            return position // 2
        if edge == EAST:
            return position * (SIDE // 4) + SIDE // 4 - 1
        if edge == SOUTH:
            return LANES - SIDE // 4 + position // 2
        return position * (SIDE // 4)

    def turn(position, reverse):
        return position + reverse * (BLOCKS - 1 - 2 * position)

    partners = paired_ref.shape[1]
    wanted = [tile] + [slot_ref[paired_ref[0, partner]] for partner in range(partners)]
    for index, slot in enumerate(wanted):
        columns = slice(index * LANES, (index + 1) * LANES)
        for edge in range(4):
            near = slot_ref[near_ids_ref[slot, edge]]
            code = codes_ref[slot, edge]
            touching, reverse = code % 4, code // 4
            pattern = (cell == target(edge, turn(block, reverse))).astype(jnp.float32)
            start = pl.multiple_of(jnp.bitwise_xor(tile, near) * LANES + touching * BLOCKS, BLOCKS)
            wide_ref[pl.ds(start, BLOCKS), columns] += pattern
            beyond = slot_ref[near_ids_ref[near, touching]]
            beyond_code = codes_ref[near, touching]
            reverse_both = jnp.bitwise_xor(reverse, beyond_code // 4)
            pattern = (cell == target(edge, turn(block, reverse_both))).astype(jnp.float32)
            start = pl.multiple_of(
                jnp.bitwise_xor(tile, beyond) * LANES + 4 * BLOCKS + (beyond_code % 4) * BLOCKS, BLOCKS
            )
            wide_ref[pl.ds(start, BLOCKS), columns] += pattern
            for end in range(2):
                rim_edge = jnp.int32(0)
                rim_end = jnp.int32(0)
                for option in range(4):
                    rim_edge = jnp.where(touching == option, END_RIMS[option][end][0], rim_edge)
                    rim_end = jnp.where(touching == option, END_RIMS[option][end][1], rim_end)
                other = slot_ref[near_ids_ref[near, rim_edge]]
                other_code = codes_ref[near, rim_edge]
                other_end = jnp.bitwise_xor(rim_end, other_code // 4)
                corner = jnp.int32(0)
                for option in range(4):
                    for which in range(2):
                        corner = jnp.where(
                            (other_code % 4 == option) & (other_end == which), EDGE_CORNERS[option][which], corner
                        )
                position = turn((BLOCKS - 1) * end, reverse)
                hit = (corner_row == corner) & (corner_cell == target(edge, position))
                start = pl.multiple_of(jnp.bitwise_xor(tile, other) * CORNER_ROWS, CORNER_ROWS)
                corner_ref[pl.ds(start, CORNER_ROWS), columns] += hit.astype(jnp.float32)
    map_ref[...] = wide_ref[...].astype(jnp.bfloat16)
    corner_map_ref[...] = corner_ref[...].astype(jnp.bfloat16)


def density_kernel(
    tiles, scale, per_band, tile_ref, ids_ref, paired_ref, height_ref, map_ref, corner_map_ref, *rest
):
    bands, (out_ref, turned_ref, partner_ref) = rest[:tiles], rest[tiles:]
    total = height_ref.shape[0]
    partners = paired_ref.shape[1]
    step_freqs = out_ref.shape[3]

    @pl.when(pl.program_id(0) == 0)
    def _():
        tile = tile_ref[0]
        height_rims = jnp.concatenate([band[total : 2 * total, :] for band in bands], axis=1)
        velocity_rims = jnp.concatenate([band[2 * total : 3 * total, :] for band in bands], axis=1)
        corners = jnp.concatenate([band[3 * total :, :] for band in bands], axis=0)
        corner_part = lax.dot_general(
            corners, corner_map_ref[...], (((0,), (0,)), ((), ())), preferred_element_type=jnp.float32
        )
        height = height_ref[...].astype(jnp.float32) + dot(height_rims, map_ref[:, :LANES])
        height = height + corner_part[:total, :LANES]
        velocity = dot(velocity_rims, map_ref[:, LANES:]) + corner_part[total:, LANES:]
        own = []
        for partner in range(partners):
            slot = jnp.int32(0)
            for candidate in range(ids_ref.shape[0]):
                slot = jnp.where(ids_ref[candidate] == paired_ref[0, partner], candidate, slot)
            wanted = jnp.bitwise_xor(tile, slot)
            chosen = bands[0][0:total, :]
            for step in range(1, tiles):
                chosen = jnp.where(wanted == step, bands[step][0:total, :], chosen)
            own.append(chosen.astype(jnp.float32))
        velocity = velocity + jnp.concatenate(own, axis=1)
        partner_ref[...] = velocity.astype(jnp.bfloat16)
        height = height.astype(jnp.bfloat16).astype(jnp.float32)
        row = lax.broadcasted_iota(jnp.int32, height.shape, 0)
        rotated = jnp.where(
            (row // per_band) % 2 == 0,
            pltpu.roll(height, total - per_band, 0),
            -pltpu.roll(height, per_band, 0),
        )
        turned_ref[0:LANES, :] = height.T
        turned_ref[LANES:, :] = rotated.T

    lane = lax.broadcasted_iota(jnp.int32, turned_ref.shape, 1)
    for offset in range(step_freqs):
        frequency = pl.program_id(0) * step_freqs + offset
        left = jnp.where(lane % per_band == frequency, turned_ref[...], 0.0).astype(jnp.bfloat16)
        cross = dot(left, partner_ref[...]) * scale
        for partner in range(partners):
            for part in range(2):
                out_ref[0, partner, part, offset] = cross[
                    part * LANES : (part + 1) * LANES, partner * LANES : (partner + 1) * LANES
                ]


SMEM = pl.BlockSpec(memory_space=pltpu.SMEM)
VMEM = pl.BlockSpec(memory_space=pltpu.VMEM)


def shards(tiles, freqs, field_count, fields, slot_tile_ids, neighbour_tile_ids, neighbour_rotation_code, paired_tile_ids):
    field = fields.reshape(fields.shape[2], fields.shape[3])
    samples = field.shape[0]
    devices = freqs * field_count
    per_band = FREQS // devices
    rows = samples // SEGLEN * 2 * per_band
    total = freqs * rows
    partners = paired_tile_ids.shape[1]
    tile = lax.axis_index("tiles").astype(jnp.int32).reshape(1)
    place = (lax.axis_index("freq") * field_count + lax.axis_index("field")).astype(jnp.int32).reshape(1)

    def swap(value, axes, count, step):
        return lax.ppermute(value, axes, [(i, i ^ step) for i in range(count)])

    piece = pltpu.VMEM((2 * rows + CORNER_ROWS, LANES), jnp.bfloat16)
    pieces = pl.pallas_call(
        functools.partial(transform_kernel, devices),
        out_shape=[piece] * devices,
        in_specs=[SMEM] + [VMEM] * 8,
        out_specs=[VMEM] * devices,
        scratch_shapes=[pltpu.VMEM((samples, 2 * LANES), jnp.float32)],
        name="transform",
    )(place, field, *cell_tables(), *time_tables(devices, samples))
    pieces = [pieces[0]] + [
        swap(pieces[step], ("freq", "field"), devices, step) for step in range(1, devices)
    ]

    cell_map, corner_map = pl.pallas_call(
        placement_kernel,
        out_shape=[
            pltpu.VMEM((tiles * LANES, (1 + partners) * LANES), jnp.bfloat16),
            pltpu.VMEM((tiles * CORNER_ROWS, (1 + partners) * LANES), jnp.bfloat16),
        ],
        in_specs=[SMEM] * 5,
        out_specs=[VMEM] * 2,
        scratch_shapes=[
            pltpu.SMEM((tiles,), jnp.int32),
            pltpu.VMEM((tiles * LANES, (1 + partners) * LANES), jnp.float32),
            pltpu.VMEM((tiles * CORNER_ROWS, (1 + partners) * LANES), jnp.float32),
        ],
        name="placement",
    )(tile, slot_tile_ids, neighbour_tile_ids, neighbour_rotation_code, paired_tile_ids)

    band, height = pl.pallas_call(
        functools.partial(collect_kernel, devices),
        out_shape=[
            pltpu.VMEM((3 * total + CORNER_ROWS, LANES), jnp.bfloat16),
            pltpu.VMEM((total, LANES), jnp.bfloat16),
        ],
        in_specs=[SMEM] + [VMEM] * devices,
        out_specs=[VMEM] * 2,
        scratch_shapes=[pltpu.VMEM((4 * total, LANES), jnp.bfloat16)],
        name="collect",
    )(place, *map(near, pieces))
    bands = [band] + [swap(band, "tiles", tiles, step) for step in range(1, tiles)]

    segments = freqs * samples // SEGLEN
    scale = 1.0 / (segments * SEGLEN * 0.375)
    step_freqs = 2
    block = (1, partners, 2, step_freqs, LANES, LANES)
    return pl.pallas_call(
        functools.partial(density_kernel, tiles, scale, per_band),
        out_shape=jax.ShapeDtypeStruct((1, partners, 2, per_band, LANES, LANES), jnp.float32),
        grid=(per_band // step_freqs,),
        in_specs=[SMEM] * 3 + [VMEM] * (3 + tiles),
        out_specs=pl.BlockSpec(block, lambda i: (0, 0, 0, i, 0, 0)),
        scratch_shapes=[
            pltpu.VMEM((2 * LANES, total), jnp.float32),
            pltpu.VMEM((total, partners * LANES), jnp.bfloat16),
        ],
        name="density",
    )(tile, slot_tile_ids, paired_tile_ids, *map(near, (height, cell_map, corner_map, *bands)))


def near(value):
    return pltpu.with_memory_space_constraint(value, pltpu.VMEM)


def solution(mesh):
    placed = (P("field", "tiles", ("groups", "freq"), None), P(), P(), P(), P("tiles", None))
    return jax.shard_map(
        functools.partial(shards, mesh.shape["tiles"], mesh.shape["freq"], mesh.shape["field"]),
        mesh=mesh,
        in_specs=placed,
        out_specs=P(("groups", "tiles"), None, None, ("freq", "field"), None, None),
        check_vma=False,
    )
```

```python
import functools
import math

import jax
import jax.numpy as jnp
import ml_dtypes
import numpy as np
from jax import lax
from jax.experimental import pallas as pl
from jax.experimental.pallas import tpu as pltpu
from jax.sharding import PartitionSpec as P

SIDE = 32
SEGLEN = 64
LANES = 128
BLOCKS = SIDE // 2
CORNER_ROWS = 16
FREQS = SEGLEN // 2

NORTH, EAST, SOUTH, WEST = range(4)
EDGE_CORNERS = ((0, 1), (1, 3), (2, 3), (0, 2))
END_RIMS = (
    ((WEST, 0), (EAST, 0)),
    ((NORTH, 1), (SOUTH, 1)),
    ((WEST, 1), (EAST, 1)),
    ((NORTH, 0), (SOUTH, 0)),
)


def split_bf16(values):
    high = values.astype(ml_dtypes.bfloat16)
    low = (values - high.astype(np.float64)).astype(ml_dtypes.bfloat16)
    return high, low


@functools.lru_cache(maxsize=None)
def cell_tables():
    cells = SIDE * SIDE

    def at(row, column):
        return row * SIDE + column

    near = np.zeros((cells, cells))
    pool = np.zeros((cells, LANES))
    for row in range(SIDE):
        for column in range(SIDE):
            pool[at(row, column), (row // 2) * (SIDE // 4) + column // 4] = 1
            for down, right in ((1, 0), (-1, 0), (0, 1), (0, -1)):
                if 0 <= row + down < SIDE and 0 <= column + right < SIDE:
                    near[at(row + down, column + right), at(row, column)] = 1
    last = SIDE - 1
    outer = [[at(0, i), at(i, last), at(last, i), at(i, 0)] for i in range(SIDE)]
    inner = [[at(1, i), at(i, last - 1), at(last - 1, i), at(i, 1)] for i in range(SIDE)]
    carried = np.zeros((cells, 4 * BLOCKS))
    sums = np.zeros((cells, 4 * BLOCKS))
    for edge in range(4):
        for i in range(SIDE):
            block = edge * BLOCKS + i // 2
            sums[outer[i][edge], block] += 1
            carried[outer[i][edge], block] += 1
            carried[inner[i][edge], block] += 1
            if i > 0:
                carried[outer[i - 1][edge], block] += 2
            if i < last:
                carried[outer[i + 1][edge], block] += 2
    cell_map = np.concatenate([near @ near @ pool, carried, sums], axis=1)
    first_corners = np.zeros((CORNER_ROWS, LANES))
    last_corners = np.zeros((CORNER_ROWS, LANES))
    first_corners[0, 0] = 1
    first_corners[1, last] = 1
    last_corners[2, LANES - SIDE] = 1
    last_corners[3, LANES - 1] = 1
    to_bf16 = lambda table: table.astype(ml_dtypes.bfloat16)
    return to_bf16(cell_map), to_bf16(first_corners), to_bf16(last_corners)


@functools.lru_cache(maxsize=None)
def time_tables(bands, samples):
    per_band = FREQS // bands
    segments = samples // SEGLEN
    time = np.arange(SEGLEN)
    frequency = np.arange(FREQS)
    angles = 2.0 * math.pi / SEGLEN * (frequency[:, None] * time[None, :] % SEGLEN)
    window = 0.5 - 0.5 * np.cos(2.0 * math.pi / SEGLEN * time)
    waves = np.stack([window * np.cos(angles), -window * np.sin(angles)]) / 16.0
    table = np.zeros((bands, segments, 2, per_band, segments, SEGLEN))
    for segment in range(segments):
        table[:, segment, :, :, segment, :] = waves.reshape(2, bands, per_band, SEGLEN).transpose(1, 0, 2, 3)
    table = table.reshape(bands * segments * 2 * per_band, samples)
    high, low = split_bf16(table)
    return high, low


def dot(left, right):
    return jnp.dot(left, right, preferred_element_type=jnp.float32)


def transform_kernel(devices, place_ref, x_ref, cells_ref, first_ref, last_ref, high_ref, low_ref, *outs):
    place = place_ref[0]
    rows = high_ref.shape[0] // devices
    starts = [pl.multiple_of(jnp.bitwise_xor(place, step) * rows, rows) for step in range(devices)]
    high = jnp.concatenate([high_ref[pl.ds(start, rows), :] for start in starts], axis=0)
    low = jnp.concatenate([low_ref[pl.ds(start, rows), :] for start in starts], axis=0)
    across = (((1,), (1,)), ((), ()))
    x = x_ref[...]
    corners = lax.dot_general(first_ref[...], x[:, :LANES], across, preferred_element_type=jnp.float32)
    corners += lax.dot_general(
        last_ref[...], x[:, SIDE * SIDE - LANES :], across, preferred_element_type=jnp.float32
    )
    corners = corners.astype(jnp.bfloat16)
    corner_spectra = lax.dot_general(corners, high, across, preferred_element_type=jnp.float32)
    corner_spectra += lax.dot_general(corners, low, across, preferred_element_type=jnp.float32)
    sums = dot(x, cells_ref[...])
    sums_high = sums.astype(jnp.bfloat16)
    sums_low = (sums - sums_high.astype(jnp.float32)).astype(jnp.bfloat16)
    spectra = dot(high, sums_high) + (dot(high, sums_low) + dot(low, sums_high))
    spectra = spectra.astype(jnp.bfloat16)
    lane_start = (place % 2) * (LANES // 2) + (place // 2) * rows
    lane = lax.broadcasted_iota(jnp.int32, (CORNER_ROWS, LANES), 1)
    mine = (lane >= lane_start) & (lane < lane_start + rows)
    for step in range(devices):
        block = spectra[step * rows : (step + 1) * rows]
        outs[step][0:rows, :] = block[:, :LANES]
        outs[step][rows : 2 * rows, :] = block[:, LANES:]
        turned = pltpu.roll(corner_spectra, lax.rem(lane_start - step * rows + LANES, LANES), 1)
        outs[step][2 * rows : 2 * rows + CORNER_ROWS, :] = jnp.where(mine, turned, 0.0).astype(jnp.bfloat16)


def collect_kernel(devices, place_ref, *rest):
    blocks, (band_ref, height_ref, held_ref) = rest[:devices], rest[devices:]
    place = place_ref[0]
    rows = (blocks[0].shape[0] - CORNER_ROWS) // 2
    total = height_ref.shape[0]
    corners = jnp.zeros((CORNER_ROWS, LANES), jnp.float32)
    for step in range(devices):
        source = jnp.bitwise_xor(place, step)
        field, half = source % 2, source // 2
        start = pl.multiple_of(field * total + half * rows, rows)
        held_ref[pl.ds(start, rows), :] = blocks[step][0:rows, :]
        held_ref[pl.ds(2 * total + start, rows), :] = blocks[step][rows : 2 * rows, :]
        corners += blocks[step][2 * rows :, :].astype(jnp.float32)
    height_ref[...] = held_ref[0:total, :]
    band_ref[0 : 3 * total, :] = held_ref[total : 4 * total, :]
    band_ref[3 * total :, :] = corners.astype(jnp.bfloat16)


def placement_kernel(
    tile_ref,
    ids_ref,
    near_ids_ref,
    codes_ref,
    paired_ref,
    map_ref,
    corner_map_ref,
    chosen_ref,
    slot_ref,
    wide_ref,
    corner_ref,
):
    slots = ids_ref.shape[0]
    tile = tile_ref[0]

    def invert(slot, carry):
        slot_ref[ids_ref[slot]] = slot
        return carry

    lax.fori_loop(0, slots, invert, 0, unroll=slots <= 8)
    wide_ref[...] = jnp.zeros_like(wide_ref)
    corner_ref[...] = jnp.zeros_like(corner_ref)
    block = lax.broadcasted_iota(jnp.int32, (BLOCKS, LANES), 0)
    cell = lax.broadcasted_iota(jnp.int32, (BLOCKS, LANES), 1)
    corner_row = lax.broadcasted_iota(jnp.int32, (CORNER_ROWS, LANES), 0)
    corner_cell = lax.broadcasted_iota(jnp.int32, (CORNER_ROWS, LANES), 1)

    def target(edge, position):
        if edge == NORTH:
            return position // 2
        if edge == EAST:
            return position * (SIDE // 4) + SIDE // 4 - 1
        if edge == SOUTH:
            return LANES - SIDE // 4 + position // 2
        return position * (SIDE // 4)

    def turn(position, reverse):
        return position + reverse * (BLOCKS - 1 - 2 * position)

    partners = paired_ref.shape[1]
    wanted = [tile] + [slot_ref[paired_ref[0, partner]] for partner in range(partners)]
    for index, slot in enumerate(wanted):
        columns = slice(index * LANES, (index + 1) * LANES)
        for edge in range(4):
            near = slot_ref[near_ids_ref[slot, edge]]
            code = codes_ref[slot, edge]
            touching, reverse = code % 4, code // 4
            pattern = (cell == target(edge, turn(block, reverse))).astype(jnp.float32)
            start = pl.multiple_of(jnp.bitwise_xor(tile, near) * LANES + touching * BLOCKS, BLOCKS)
            wide_ref[pl.ds(start, BLOCKS), columns] += pattern
            beyond = slot_ref[near_ids_ref[near, touching]]
            beyond_code = codes_ref[near, touching]
            reverse_both = jnp.bitwise_xor(reverse, beyond_code // 4)
            pattern = (cell == target(edge, turn(block, reverse_both))).astype(jnp.float32)
            start = pl.multiple_of(
                jnp.bitwise_xor(tile, beyond) * LANES + 4 * BLOCKS + (beyond_code % 4) * BLOCKS, BLOCKS
            )
            wide_ref[pl.ds(start, BLOCKS), columns] += pattern
            for end in range(2):
                rim_edge = jnp.int32(0)
                rim_end = jnp.int32(0)
                for option in range(4):
                    rim_edge = jnp.where(touching == option, END_RIMS[option][end][0], rim_edge)
                    rim_end = jnp.where(touching == option, END_RIMS[option][end][1], rim_end)
                other = slot_ref[near_ids_ref[near, rim_edge]]
                other_code = codes_ref[near, rim_edge]
                other_end = jnp.bitwise_xor(rim_end, other_code // 4)
                corner = jnp.int32(0)
                for option in range(4):
                    for which in range(2):
                        corner = jnp.where(
                            (other_code % 4 == option) & (other_end == which), EDGE_CORNERS[option][which], corner
                        )
                position = turn((BLOCKS - 1) * end, reverse)
                hit = (corner_row == corner) & (corner_cell == target(edge, position))
                start = pl.multiple_of(jnp.bitwise_xor(tile, other) * CORNER_ROWS, CORNER_ROWS)
                corner_ref[pl.ds(start, CORNER_ROWS), columns] += hit.astype(jnp.float32)
    step = lax.broadcasted_iota(jnp.int32, (chosen_ref.shape[0], LANES), 0)
    for partner in range(partners):
        wanted_step = jnp.bitwise_xor(tile, wanted[1 + partner])
        chosen_ref[:, partner * LANES : (partner + 1) * LANES] = (step == wanted_step).astype(jnp.float32)
    map_ref[...] = wide_ref[...].astype(jnp.bfloat16)
    corner_map_ref[...] = corner_ref[...].astype(jnp.bfloat16)


def density_kernel(
    tiles, partners, scale, per_band, height_ref, map_ref, corner_map_ref, chosen_ref, *rest
):
    bands, (out_ref, cross_ref, sent) = rest[:tiles], rest[tiles:]
    total = height_ref.shape[0]
    height_rims = jnp.concatenate([band[total : 2 * total, :] for band in bands], axis=1)
    velocity_rims = jnp.concatenate([band[2 * total : 3 * total, :] for band in bands], axis=1)
    corners = jnp.concatenate([band[3 * total :, :] for band in bands], axis=0)
    corner_part = lax.dot_general(
        corners, corner_map_ref[...], (((0,), (0,)), ((), ())), preferred_element_type=jnp.float32
    )
    height = height_ref[...].astype(jnp.float32) + dot(height_rims, map_ref[:, :LANES])
    height = height + corner_part[:total, :LANES]
    velocity = dot(velocity_rims, map_ref[:, LANES:]) + corner_part[total:, LANES:]
    for step in range(tiles):
        own = bands[step][0:total, :].astype(jnp.float32)
        velocity += jnp.concatenate([own] * partners, axis=1) * chosen_ref[step : step + 1, :]
    velocity = velocity.astype(jnp.bfloat16)
    height = height.astype(jnp.bfloat16).astype(jnp.float32)
    row = lax.broadcasted_iota(jnp.int32, height.shape, 0)
    rotated = jnp.where(
        (row // per_band) % 2 == 0,
        pltpu.roll(height, total - per_band, 0),
        -pltpu.roll(height, per_band, 0),
    )
    turned = jnp.concatenate([height.T, rotated.T], axis=0)
    lane = lax.broadcasted_iota(jnp.int32, turned.shape, 1)
    copies = []
    for frequency in range(per_band):
        left = jnp.where(lane % per_band == frequency, turned, 0.0).astype(jnp.bfloat16)
        cross = dot(left, velocity) * scale
        for partner in range(partners):
            for part in range(2):
                index = (partner * 2 + part) * per_band + frequency
                rows = pl.ds(index * LANES, LANES)
                cross_ref[rows, :] = cross[
                    part * LANES : (part + 1) * LANES, partner * LANES : (partner + 1) * LANES
                ]
                copies.append(pltpu.make_async_copy(cross_ref.at[rows], out_ref.at[rows], sent.at[index]))
                copies[-1].start()
    for copy in copies:
        copy.wait()


SMEM = pl.BlockSpec(memory_space=pltpu.SMEM)
VMEM = pl.BlockSpec(memory_space=pltpu.VMEM)


def kept(shape, dtype):
    return pltpu.VMEM(shape, dtype)


def near(value):
    return pltpu.with_memory_space_constraint(value, pltpu.VMEM)


def shards(tiles, freqs, field_count, fields, slot_tile_ids, neighbour_tile_ids, neighbour_rotation_code, paired_tile_ids):
    field = fields.reshape(fields.shape[2], fields.shape[3])
    samples = field.shape[0]
    devices = freqs * field_count
    per_band = FREQS // devices
    rows = samples // SEGLEN * 2 * per_band
    total = freqs * rows
    partners = paired_tile_ids.shape[1]
    tile = lax.axis_index("tiles").astype(jnp.int32).reshape(1)
    place = (lax.axis_index("freq") * field_count + lax.axis_index("field")).astype(jnp.int32).reshape(1)

    def swap(value, axes, count, step):
        return lax.ppermute(value, axes, [(i, i ^ step) for i in range(count)])

    piece = kept((2 * rows + CORNER_ROWS, LANES), jnp.bfloat16)
    pieces = pl.pallas_call(
        functools.partial(transform_kernel, devices),
        out_shape=[piece] * devices,
        in_specs=[SMEM] + [VMEM] * 6,
        out_specs=[VMEM] * devices,
        name="transform",
    )(place, field, *cell_tables(), *time_tables(devices, samples))
    pieces = [pieces[0]] + [
        swap(pieces[step], ("freq", "field"), devices, step) for step in range(1, devices)
    ]

    cell_map, corner_map, chosen = pl.pallas_call(
        placement_kernel,
        out_shape=[
            kept((tiles * LANES, (1 + partners) * LANES), jnp.bfloat16),
            kept((tiles * CORNER_ROWS, (1 + partners) * LANES), jnp.bfloat16),
            kept((tiles + -tiles % 8, partners * LANES), jnp.float32),
        ],
        in_specs=[SMEM] * 5,
        out_specs=[VMEM] * 3,
        scratch_shapes=[
            pltpu.SMEM((tiles,), jnp.int32),
            pltpu.VMEM((tiles * LANES, (1 + partners) * LANES), jnp.float32),
            pltpu.VMEM((tiles * CORNER_ROWS, (1 + partners) * LANES), jnp.float32),
        ],
        name="placement",
    )(tile, slot_tile_ids, neighbour_tile_ids, neighbour_rotation_code, paired_tile_ids)

    band, height = pl.pallas_call(
        functools.partial(collect_kernel, devices),
        out_shape=[
            kept((3 * total + CORNER_ROWS, LANES), jnp.bfloat16),
            kept((total, LANES), jnp.bfloat16),
        ],
        in_specs=[SMEM] + [VMEM] * devices,
        out_specs=[VMEM] * 2,
        scratch_shapes=[pltpu.VMEM((4 * total, LANES), jnp.bfloat16)],
        name="collect",
    )(place, *map(near, pieces))
    bands = [band] + [swap(band, "tiles", tiles, step) for step in range(1, tiles)]

    segments = freqs * samples // SEGLEN
    scale = 1.0 / (segments * SEGLEN * 0.375)
    blocks = partners * 2 * per_band
    density = pl.pallas_call(
        functools.partial(density_kernel, tiles, partners, scale, per_band),
        out_shape=jax.ShapeDtypeStruct((blocks * LANES, LANES), jnp.float32),
        in_specs=[VMEM] * (4 + tiles),
        out_specs=pl.BlockSpec(memory_space=pl.ANY),
        scratch_shapes=[
            pltpu.VMEM((blocks * LANES, LANES), jnp.float32),
            pltpu.SemaphoreType.DMA((blocks,)),
        ],
        name="density",
    )(*map(near, (height, cell_map, corner_map, chosen, *bands)))
    return density.reshape(1, partners, 2, per_band, LANES, LANES)


def solution(mesh):
    placed = (P("field", "tiles", ("groups", "freq"), None), P(), P(), P(), P("tiles", None))
    return jax.shard_map(
        functools.partial(shards, mesh.shape["tiles"], mesh.shape["freq"], mesh.shape["field"]),
        mesh=mesh,
        in_specs=placed,
        out_specs=P(("groups", "tiles"), None, None, ("freq", "field"), None, None),
        check_vma=False,
    )
```

```python
import functools
import math

import jax
import jax.numpy as jnp
import ml_dtypes
import numpy as np
from jax import lax
from jax.experimental import pallas as pl
from jax.experimental.pallas import tpu as pltpu
from jax.sharding import PartitionSpec as P

SIDE = 32
SEGLEN = 64
LANES = 128
BLOCKS = SIDE // 2
CORNER_ROWS = 16
FREQS = SEGLEN // 2

NORTH, EAST, SOUTH, WEST = range(4)
EDGE_CORNERS = ((0, 1), (1, 3), (2, 3), (0, 2))
END_RIMS = (
    ((WEST, 0), (EAST, 0)),
    ((NORTH, 1), (SOUTH, 1)),
    ((WEST, 1), (EAST, 1)),
    ((NORTH, 0), (SOUTH, 0)),
)

BAND_ROUTES = ((1, 3, 0, 2), (3, 2, 1, 0), (2, 0, 3, 1))
TILE_ROUTES = ((1, 2, 0, 3), (2, 3, 1, 0), (3, 0, 2, 1), (0, 1, 3, 2))


def routes_for(count, preferred):
    if len(preferred[0]) == count:
        return preferred
    return tuple(tuple(i ^ step for i in range(count)) for step in range(1, count))


def senders(route):
    return tuple(route.index(i) for i in range(len(route)))


def look_up(table, index):
    value = jnp.int32(table[0])
    for i in range(1, len(table)):
        value = jnp.where(index == i, table[i], value)
    return value


def split_bf16(values):
    high = values.astype(ml_dtypes.bfloat16)
    low = (values - high.astype(np.float64)).astype(ml_dtypes.bfloat16)
    return high, low


@functools.lru_cache(maxsize=None)
def cell_tables():
    cells = SIDE * SIDE

    def at(row, column):
        return row * SIDE + column

    near = np.zeros((cells, cells))
    pool = np.zeros((cells, LANES))
    for row in range(SIDE):
        for column in range(SIDE):
            pool[at(row, column), (row // 2) * (SIDE // 4) + column // 4] = 1
            for down, right in ((1, 0), (-1, 0), (0, 1), (0, -1)):
                if 0 <= row + down < SIDE and 0 <= column + right < SIDE:
                    near[at(row + down, column + right), at(row, column)] = 1
    last = SIDE - 1
    outer = [[at(0, i), at(i, last), at(last, i), at(i, 0)] for i in range(SIDE)]
    inner = [[at(1, i), at(i, last - 1), at(last - 1, i), at(i, 1)] for i in range(SIDE)]
    carried = np.zeros((cells, 4 * BLOCKS))
    sums = np.zeros((cells, 4 * BLOCKS))
    for edge in range(4):
        for i in range(SIDE):
            block = edge * BLOCKS + i // 2
            sums[outer[i][edge], block] += 1
            carried[outer[i][edge], block] += 1
            carried[inner[i][edge], block] += 1
            if i > 0:
                carried[outer[i - 1][edge], block] += 2
            if i < last:
                carried[outer[i + 1][edge], block] += 2
    cell_map = np.concatenate([near @ near @ pool, carried, sums], axis=1)
    first_corners = np.zeros((CORNER_ROWS, LANES))
    last_corners = np.zeros((CORNER_ROWS, LANES))
    first_corners[0, 0] = 1
    first_corners[1, last] = 1
    last_corners[2, LANES - SIDE] = 1
    last_corners[3, LANES - 1] = 1
    to_bf16 = lambda table: table.astype(ml_dtypes.bfloat16)
    return to_bf16(cell_map), to_bf16(first_corners), to_bf16(last_corners)


@functools.lru_cache(maxsize=None)
def time_tables(bands, samples):
    per_band = FREQS // bands
    segments = samples // SEGLEN
    time = np.arange(SEGLEN)
    frequency = np.arange(FREQS)
    angles = 2.0 * math.pi / SEGLEN * (frequency[:, None] * time[None, :] % SEGLEN)
    window = 0.5 - 0.5 * np.cos(2.0 * math.pi / SEGLEN * time)
    waves = np.stack([window * np.cos(angles), -window * np.sin(angles)]) / 16.0
    table = np.zeros((bands, segments, 2, per_band, segments, SEGLEN))
    for segment in range(segments):
        table[:, segment, :, :, segment, :] = waves.reshape(2, bands, per_band, SEGLEN).transpose(1, 0, 2, 3)
    table = table.reshape(bands * segments * 2 * per_band, samples)
    high, low = split_bf16(table)
    return np.concatenate([high, high, low], axis=1)


def dot(left, right):
    return jnp.dot(left, right, preferred_element_type=jnp.float32)


def transform_kernel(routes, place_ref, x_ref, cells_ref, first_ref, last_ref, waves_ref, *outs):
    place = place_ref[0]
    devices = len(outs)
    rows = waves_ref.shape[0] // devices
    bands = [place] + [look_up(route, place) for route in routes]
    waves = jnp.concatenate(
        [waves_ref[pl.ds(pl.multiple_of(band * rows, rows), rows), :] for band in bands], axis=0
    )
    across = (((1,), (1,)), ((), ()))
    x = x_ref[...]
    samples = x.shape[0]
    corners = lax.dot_general(first_ref[...], x[:, :LANES], across, preferred_element_type=jnp.float32)
    corners += lax.dot_general(
        last_ref[...], x[:, SIDE * SIDE - LANES :], across, preferred_element_type=jnp.float32
    )
    corners = corners.astype(jnp.bfloat16)
    corners = jnp.concatenate([corners, corners], axis=1)
    corner_spectra = lax.dot_general(corners, waves[:, samples:], across, preferred_element_type=jnp.float32)
    sums = dot(x, cells_ref[...])
    sums_high = sums.astype(jnp.bfloat16)
    sums_low = (sums - sums_high.astype(jnp.float32)).astype(jnp.bfloat16)
    spectra = dot(waves, jnp.concatenate([sums_low, sums_high, sums_high], axis=0))
    spectra = spectra.astype(jnp.bfloat16)
    lane_start = (place % 2) * (LANES // 2) + (place // 2) * rows
    lane = lax.broadcasted_iota(jnp.int32, (CORNER_ROWS, LANES), 1)
    mine = (lane >= lane_start) & (lane < lane_start + rows)
    for step in range(devices):
        block = spectra[step * rows : (step + 1) * rows]
        outs[step][0:rows, :] = block[:, :LANES]
        outs[step][rows : 2 * rows, :] = block[:, LANES:]
        turned = pltpu.roll(corner_spectra, lax.rem(lane_start - step * rows + LANES, LANES), 1)
        outs[step][2 * rows : 2 * rows + CORNER_ROWS, :] = jnp.where(mine, turned, 0.0).astype(jnp.bfloat16)


def collect_kernel(routes, place_ref, *rest):
    devices = len(routes) + 1
    blocks, (band_ref, height_ref, held_ref) = rest[:devices], rest[devices:]
    place = place_ref[0]
    rows = (blocks[0].shape[0] - CORNER_ROWS) // 2
    total = height_ref.shape[0]
    corners = jnp.zeros((CORNER_ROWS, LANES), jnp.float32)
    for step in range(devices):
        source = look_up(senders(routes[step - 1]), place) if step else place
        field, half = source % 2, source // 2
        start = pl.multiple_of(field * total + half * rows, rows)
        held_ref[pl.ds(start, rows), :] = blocks[step][0:rows, :]
        held_ref[pl.ds(2 * total + start, rows), :] = blocks[step][rows : 2 * rows, :]
        corners += blocks[step][2 * rows :, :].astype(jnp.float32)
    height_ref[...] = held_ref[0:total, :]
    band_ref[0 : 3 * total, :] = held_ref[total : 4 * total, :]
    band_ref[3 * total :, :] = corners.astype(jnp.bfloat16)


def placement_kernel(
    routes,
    tile_ref,
    ids_ref,
    near_ids_ref,
    codes_ref,
    paired_ref,
    map_ref,
    corner_map_ref,
    chosen_ref,
    slot_ref,
    arrival_ref,
    wide_ref,
    corner_ref,
):
    slots = ids_ref.shape[0]
    tile = tile_ref[0]

    def invert(slot, carry):
        slot_ref[ids_ref[slot]] = slot
        return carry

    lax.fori_loop(0, slots, invert, 0, unroll=slots <= 8)
    for sender in range(len(routes[0])):
        steps = [0] * len(routes[0])
        for step, route in enumerate(routes):
            if route[sender] != sender:
                steps[route[sender]] = step + 1
        arrival_ref[sender] = look_up(steps, tile)
    wide_ref[...] = jnp.zeros_like(wide_ref)
    corner_ref[...] = jnp.zeros_like(corner_ref)
    block = lax.broadcasted_iota(jnp.int32, (BLOCKS, LANES), 0)
    cell = lax.broadcasted_iota(jnp.int32, (BLOCKS, LANES), 1)
    corner_row = lax.broadcasted_iota(jnp.int32, (CORNER_ROWS, LANES), 0)
    corner_cell = lax.broadcasted_iota(jnp.int32, (CORNER_ROWS, LANES), 1)

    def target(edge, position):
        if edge == NORTH:
            return position // 2
        if edge == EAST:
            return position * (SIDE // 4) + SIDE // 4 - 1
        if edge == SOUTH:
            return LANES - SIDE // 4 + position // 2
        return position * (SIDE // 4)

    def turn(position, reverse):
        return position + reverse * (BLOCKS - 1 - 2 * position)

    partners = paired_ref.shape[1]
    wanted = [tile] + [slot_ref[paired_ref[0, partner]] for partner in range(partners)]
    for index, slot in enumerate(wanted):
        columns = slice(index * LANES, (index + 1) * LANES)
        for edge in range(4):
            near = slot_ref[near_ids_ref[slot, edge]]
            code = codes_ref[slot, edge]
            touching, reverse = code % 4, code // 4
            pattern = (cell == target(edge, turn(block, reverse))).astype(jnp.float32)
            start = pl.multiple_of(arrival_ref[near] * LANES + touching * BLOCKS, BLOCKS)
            wide_ref[pl.ds(start, BLOCKS), columns] += pattern
            beyond = slot_ref[near_ids_ref[near, touching]]
            beyond_code = codes_ref[near, touching]
            reverse_both = jnp.bitwise_xor(reverse, beyond_code // 4)
            pattern = (cell == target(edge, turn(block, reverse_both))).astype(jnp.float32)
            start = pl.multiple_of(
                arrival_ref[beyond] * LANES + 4 * BLOCKS + (beyond_code % 4) * BLOCKS, BLOCKS
            )
            wide_ref[pl.ds(start, BLOCKS), columns] += pattern
            for end in range(2):
                rim_edge = jnp.int32(0)
                rim_end = jnp.int32(0)
                for option in range(4):
                    rim_edge = jnp.where(touching == option, END_RIMS[option][end][0], rim_edge)
                    rim_end = jnp.where(touching == option, END_RIMS[option][end][1], rim_end)
                other = slot_ref[near_ids_ref[near, rim_edge]]
                other_code = codes_ref[near, rim_edge]
                other_end = jnp.bitwise_xor(rim_end, other_code // 4)
                corner = jnp.int32(0)
                for option in range(4):
                    for which in range(2):
                        corner = jnp.where(
                            (other_code % 4 == option) & (other_end == which), EDGE_CORNERS[option][which], corner
                        )
                position = turn((BLOCKS - 1) * end, reverse)
                hit = (corner_row == corner) & (corner_cell == target(edge, position))
                start = pl.multiple_of(arrival_ref[other] * CORNER_ROWS, CORNER_ROWS)
                corner_ref[pl.ds(start, CORNER_ROWS), columns] += hit.astype(jnp.float32)
    step = lax.broadcasted_iota(jnp.int32, (chosen_ref.shape[0], LANES), 0)
    for partner in range(partners):
        wanted_step = arrival_ref[wanted[1 + partner]]
        chosen_ref[:, partner * LANES : (partner + 1) * LANES] = (step == wanted_step).astype(jnp.float32)
    map_ref[...] = wide_ref[...].astype(jnp.bfloat16)
    corner_map_ref[...] = corner_ref[...].astype(jnp.bfloat16)


def density_kernel(
    arrivals, partners, scale, per_band, height_ref, map_ref, corner_map_ref, chosen_ref, *rest
):
    bands, (out_ref, cross_ref, sent) = (rest[0], *rest[arrivals - 1 : 0 : -1]), rest[arrivals:]
    total = height_ref.shape[0]
    height_rims = jnp.concatenate([band[total : 2 * total, :] for band in bands], axis=1)
    velocity_rims = jnp.concatenate([band[2 * total : 3 * total, :] for band in bands], axis=1)
    corners = jnp.concatenate([band[3 * total :, :] for band in bands], axis=0)
    corner_part = lax.dot_general(
        corners, corner_map_ref[...], (((0,), (0,)), ((), ())), preferred_element_type=jnp.float32
    )
    height = height_ref[...].astype(jnp.float32) + dot(height_rims, map_ref[:, :LANES])
    height = height + corner_part[:total, :LANES]
    velocity = dot(velocity_rims, map_ref[:, LANES:]) + corner_part[total:, LANES:]
    for step in range(arrivals):
        own = bands[step][0:total, :].astype(jnp.float32)
        velocity += jnp.concatenate([own] * partners, axis=1) * chosen_ref[step : step + 1, :]
    velocity = velocity.astype(jnp.bfloat16)
    height = height.astype(jnp.bfloat16).astype(jnp.float32)
    row = lax.broadcasted_iota(jnp.int32, height.shape, 0)
    rotated = jnp.where(
        (row // per_band) % 2 == 0,
        pltpu.roll(height, total - per_band, 0),
        -pltpu.roll(height, per_band, 0),
    )
    turned = jnp.concatenate([height.T, rotated.T], axis=0)
    lane = lax.broadcasted_iota(jnp.int32, turned.shape, 1)
    copies = []
    for frequency in range(per_band):
        left = jnp.where(lane % per_band == frequency, turned, 0.0).astype(jnp.bfloat16)
        cross = dot(left, velocity) * scale
        for partner in range(partners):
            for part in range(2):
                index = (partner * 2 + part) * per_band + frequency
                rows = pl.ds(index * LANES, LANES)
                cross_ref[rows, :] = cross[
                    part * LANES : (part + 1) * LANES, partner * LANES : (partner + 1) * LANES
                ]
                copies.append(pltpu.make_async_copy(cross_ref.at[rows], out_ref.at[rows], sent.at[index]))
                copies[-1].start()
    for copy in copies:
        copy.wait()


SMEM = pl.BlockSpec(memory_space=pltpu.SMEM)
VMEM = pl.BlockSpec(memory_space=pltpu.VMEM)


def kept(shape, dtype):
    return pltpu.VMEM(shape, dtype)


def near(value):
    return pltpu.with_memory_space_constraint(value, pltpu.VMEM)


def shards(tiles, freqs, field_count, fields, slot_tile_ids, neighbour_tile_ids, neighbour_rotation_code, paired_tile_ids):
    field = fields.reshape(fields.shape[2], fields.shape[3])
    samples = field.shape[0]
    devices = freqs * field_count
    per_band = FREQS // devices
    rows = samples // SEGLEN * 2 * per_band
    total = freqs * rows
    partners = paired_tile_ids.shape[1]
    tile = lax.axis_index("tiles").astype(jnp.int32).reshape(1)
    place = (lax.axis_index("freq") * field_count + lax.axis_index("field")).astype(jnp.int32).reshape(1)

    band_routes = routes_for(devices, BAND_ROUTES)
    tile_routes = routes_for(tiles, TILE_ROUTES)
    arrivals = len(tile_routes) + 1

    piece = kept((2 * rows + CORNER_ROWS, LANES), jnp.bfloat16)
    pieces = pl.pallas_call(
        functools.partial(transform_kernel, band_routes),
        out_shape=[piece] * devices,
        in_specs=[SMEM] + [VMEM] * 5,
        out_specs=[VMEM] * devices,
        name="transform",
    )(place, field, *cell_tables(), time_tables(devices, samples))
    pieces = [pieces[0]] + [
        lax.ppermute(piece, ("freq", "field"), list(enumerate(route)))
        for piece, route in zip(pieces[1:], band_routes)
    ]

    cell_map, corner_map, chosen = pl.pallas_call(
        functools.partial(placement_kernel, tile_routes),
        out_shape=[
            kept((arrivals * LANES, (1 + partners) * LANES), jnp.bfloat16),
            kept((arrivals * CORNER_ROWS, (1 + partners) * LANES), jnp.bfloat16),
            kept((arrivals + -arrivals % 8, partners * LANES), jnp.float32),
        ],
        in_specs=[SMEM] * 5,
        out_specs=[VMEM] * 3,
        scratch_shapes=[
            pltpu.SMEM((tiles,), jnp.int32),
            pltpu.SMEM((tiles,), jnp.int32),
            pltpu.VMEM((arrivals * LANES, (1 + partners) * LANES), jnp.float32),
            pltpu.VMEM((arrivals * CORNER_ROWS, (1 + partners) * LANES), jnp.float32),
        ],
        name="placement",
    )(tile, slot_tile_ids, neighbour_tile_ids, neighbour_rotation_code, paired_tile_ids)

    band, height = pl.pallas_call(
        functools.partial(collect_kernel, band_routes),
        out_shape=[
            kept((3 * total + CORNER_ROWS, LANES), jnp.bfloat16),
            kept((total, LANES), jnp.bfloat16),
        ],
        in_specs=[SMEM] + [VMEM] * devices,
        out_specs=[VMEM] * 2,
        scratch_shapes=[pltpu.VMEM((4 * total, LANES), jnp.bfloat16)],
        name="collect",
    )(place, *map(near, pieces))
    bands = [band]
    for route in tile_routes[::-1]:
        pairs = []
        for sender, receiver in enumerate(route):
            for core in range(field_count):
                there = receiver * field_count + (core if receiver != sender else field_count - 1 - core)
                pairs.append((sender * field_count + core, there))
        bands.append(lax.ppermute(band, ("tiles", "field"), pairs))

    segments = freqs * samples // SEGLEN
    scale = 1.0 / (segments * SEGLEN * 0.375)
    blocks = partners * 2 * per_band
    density = pl.pallas_call(
        functools.partial(density_kernel, arrivals, partners, scale, per_band),
        out_shape=jax.ShapeDtypeStruct((blocks * LANES, LANES), jnp.float32),
        in_specs=[VMEM] * (4 + arrivals),
        out_specs=pl.BlockSpec(memory_space=pl.ANY),
        scratch_shapes=[
            pltpu.VMEM((blocks * LANES, LANES), jnp.float32),
            pltpu.SemaphoreType.DMA((blocks,)),
        ],
        name="density",
    )(*map(near, (height, cell_map, corner_map, chosen, *bands)))
    return density.reshape(1, partners, 2, per_band, LANES, LANES)


def solution(mesh):
    placed = (P("field", "tiles", ("groups", "freq"), None), P(), P(), P(), P("tiles", None))
    return jax.shard_map(
        functools.partial(shards, mesh.shape["tiles"], mesh.shape["freq"], mesh.shape["field"]),
        mesh=mesh,
        in_specs=placed,
        out_specs=P(("groups", "tiles"), None, None, ("freq", "field"), None, None),
        check_vma=False,
    )
```

```python
import functools
import math

import jax
import jax.numpy as jnp
import ml_dtypes
import numpy as np
from jax import lax
from jax.experimental import pallas as pl
from jax.experimental.pallas import tpu as pltpu
from jax.sharding import PartitionSpec as P

SIDE = 32
SEGLEN = 64
LANES = 128
BLOCKS = SIDE // 2
CORNER_ROWS = 16
FREQS = SEGLEN // 2

NORTH, EAST, SOUTH, WEST = range(4)
HALF = LANES // 2
RIM_LANES = (0, SIDE // 4, SIDE // 4 + BLOCKS, SIDE // 2 + BLOCKS)
CORNER_LANE = SIDE // 2 + 2 * BLOCKS
EDGE_CORNERS = ((0, 1), (1, 3), (2, 3), (0, 2))
END_RIMS = (
    ((WEST, 0), (EAST, 0)),
    ((NORTH, 1), (SOUTH, 1)),
    ((WEST, 1), (EAST, 1)),
    ((NORTH, 0), (SOUTH, 0)),
)

BAND_ROUTES = ((1, 3, 0, 2), (3, 2, 1, 0), (2, 0, 3, 1))
TILE_ROUTES = ((1, 2, 0, 3), (2, 3, 1, 0), (3, 0, 2, 1), (0, 1, 3, 2))


def routes_for(count, preferred):
    if len(preferred[0]) == count:
        return preferred
    return tuple(tuple(i ^ step for i in range(count)) for step in range(1, count))


def senders(route):
    return tuple(route.index(i) for i in range(len(route)))


def look_up(table, index, dtype=jnp.int32):
    value = dtype(table[0])
    for i in range(1, len(table)):
        value = jnp.where(index == i, dtype(table[i]), value)
    return value


def split_bf16(values):
    high = values.astype(ml_dtypes.bfloat16)
    low = (values - high.astype(np.float64)).astype(ml_dtypes.bfloat16)
    return high, low


@functools.lru_cache(maxsize=None)
def cell_tables():
    cells = SIDE * SIDE

    def at(row, column):
        return row * SIDE + column

    near = np.zeros((cells, cells))
    pool = np.zeros((cells, LANES))
    for row in range(SIDE):
        for column in range(SIDE):
            pool[at(row, column), (row // 2) * (SIDE // 4) + column // 4] = 1
            for down, right in ((1, 0), (-1, 0), (0, 1), (0, -1)):
                if 0 <= row + down < SIDE and 0 <= column + right < SIDE:
                    near[at(row + down, column + right), at(row, column)] = 1
    last = SIDE - 1
    outer = [[at(0, i), at(i, last), at(last, i), at(i, 0)] for i in range(SIDE)]
    inner = [[at(1, i), at(i, last - 1), at(last - 1, i), at(i, 1)] for i in range(SIDE)]
    carried = np.zeros((cells, 4 * BLOCKS))
    sums = np.zeros((cells, 4 * BLOCKS))
    for edge in range(4):
        for i in range(SIDE):
            block = edge * BLOCKS + i // 2
            sums[outer[i][edge], block] += 1
            carried[outer[i][edge], block] += 1
            carried[inner[i][edge], block] += 1
            if i > 0:
                carried[outer[i - 1][edge], block] += 2
            if i < last:
                carried[outer[i + 1][edge], block] += 2
    cell_map = np.concatenate([near @ near @ pool, carried, sums], axis=1)
    first_corners = np.zeros((CORNER_ROWS, LANES))
    last_corners = np.zeros((CORNER_ROWS, LANES))
    first_corners[0, 0] = 1
    first_corners[1, last] = 1
    last_corners[2, LANES - SIDE] = 1
    last_corners[3, LANES - 1] = 1
    to_bf16 = lambda table: table.astype(ml_dtypes.bfloat16)
    return to_bf16(cell_map), to_bf16(first_corners), to_bf16(last_corners)


@functools.lru_cache(maxsize=None)
def time_tables(bands, samples):
    per_band = FREQS // bands
    segments = samples // SEGLEN
    time = np.arange(SEGLEN)
    frequency = np.arange(FREQS)
    angles = 2.0 * math.pi / SEGLEN * (frequency[:, None] * time[None, :] % SEGLEN)
    window = 0.5 - 0.5 * np.cos(2.0 * math.pi / SEGLEN * time)
    waves = np.stack([window * np.cos(angles), -window * np.sin(angles)]) / 16.0
    table = np.zeros((bands, segments, 2, per_band, segments, SEGLEN))
    for segment in range(segments):
        table[:, segment, :, :, segment, :] = waves.reshape(2, bands, per_band, SEGLEN).transpose(1, 0, 2, 3)
    table = table.reshape(bands * segments * 2 * per_band, samples)
    return split_bf16(table)


def dot(left, right):
    return jnp.dot(left, right, preferred_element_type=jnp.float32)


def transform_kernel(
    routes,
    place_ref,
    ids_ref,
    near_ids_ref,
    codes_ref,
    paired_ref,
    x_ref,
    cells_ref,
    first_ref,
    last_ref,
    high_ref,
    low_ref,
    near_ref,
    kept_codes_ref,
    partner_ref,
    *rest,
):
    outs, slot_ref = rest[:-1], rest[-1]
    place = place_ref[0]
    devices = len(outs)
    rows = high_ref.shape[0] // devices
    x = x_ref[...]
    sums = dot(x, cells_ref[...])
    bands = [place] + [look_up(route, place) for route in routes]
    starts = [pl.multiple_of(band * rows, rows) for band in bands]
    high = jnp.concatenate([high_ref[pl.ds(start, rows), :] for start in starts], axis=0)
    low = jnp.concatenate([low_ref[pl.ds(start, rows), :] for start in starts], axis=0)
    across = (((1,), (1,)), ((), ()))
    corners = lax.dot_general(first_ref[...], x[:, :LANES], across, preferred_element_type=jnp.float32)
    corners += lax.dot_general(
        last_ref[...], x[:, SIDE * SIDE - LANES :], across, preferred_element_type=jnp.float32
    )
    corners = corners.astype(jnp.bfloat16)
    corner_spectra = lax.dot_general(corners, high, across, preferred_element_type=jnp.float32)
    corner_spectra += lax.dot_general(corners, low, across, preferred_element_type=jnp.float32)
    sums_high = sums.astype(jnp.bfloat16)
    sums_low = (sums - sums_high.astype(jnp.float32)).astype(jnp.bfloat16)
    spectra = dot(
        jnp.concatenate([high, high, low], axis=1), jnp.concatenate([sums_high, sums_low, sums_high], axis=0)
    )
    spectra = spectra.astype(jnp.bfloat16)
    lane_start = (place % 2) * (LANES // 2) + (place // 2) * rows
    lane = lax.broadcasted_iota(jnp.int32, (CORNER_ROWS, LANES), 1)
    mine = (lane >= lane_start) & (lane < lane_start + rows)
    for step in range(devices):
        block = spectra[step * rows : (step + 1) * rows]
        outs[step][0:rows, :] = block[:, :LANES]
        outs[step][rows : 2 * rows, :] = block[:, LANES:]
        turned = pltpu.roll(corner_spectra, lax.rem(lane_start - step * rows + LANES, LANES), 1)
        outs[step][2 * rows : 2 * rows + CORNER_ROWS, :] = jnp.where(mine, turned, 0.0).astype(jnp.bfloat16)
    fill_slots(ids_ref, near_ids_ref, codes_ref, slot_ref, near_ref, kept_codes_ref)
    for partner in range(paired_ref.shape[1]):
        partner_ref[0, partner] = slot_ref[paired_ref[0, partner]]


def collect_kernel(band_routes, tile_routes, place_ref, tile_ref, rim_map_ref, corner_map_ref, *rest):
    devices, arrivals = len(band_routes) + 1, len(tile_routes) + 1
    blocks, rest = rest[:devices], rest[devices:]
    bands, (height_ref, held_ref, rim_ref) = rest[:arrivals], rest[arrivals:]
    place = place_ref[0]
    rows = (blocks[0].shape[0] - CORNER_ROWS) // 2
    total = height_ref.shape[0]
    corners = jnp.zeros((CORNER_ROWS, LANES), jnp.float32)
    for step in range(devices):
        source = look_up(senders(band_routes[step - 1]), place) if step else place
        field, half = source % 2, source // 2
        start = pl.multiple_of(field * total + half * rows, rows)
        held_ref[pl.ds(start, rows), :] = blocks[step][0:rows, :]
        held_ref[pl.ds(2 * total + start, rows), :] = blocks[step][rows : 2 * rows, :]
        corners += blocks[step][2 * rows :, :].astype(jnp.float32)
    corners = corners.astype(jnp.bfloat16)
    height_ref[...] = held_ref[0:total, :]
    row = lax.broadcasted_iota(jnp.int32, (CORNER_ROWS, LANES), 0)
    lane = lax.broadcasted_iota(jnp.int32, (CORNER_ROWS, LANES), 1)
    spread = (lane % HALF == row + CORNER_LANE) & (row < 4)
    spread = jnp.where(spread, 1.0, 0.0).astype(jnp.bfloat16)
    maps = jnp.concatenate([corner_map_ref[...], spread], axis=1)
    corner_part = lax.dot_general(corners, maps, (((0,), (0,)), ((), ())), preferred_element_type=jnp.float32)
    width = rim_map_ref.shape[1]
    rims = dot(held_ref[2 * total : 3 * total, :], rim_map_ref[...]) + corner_part[:total, :width]
    corner_part = corner_part[total:, width:]
    rim_ref[...] = rims
    lane = lax.broadcasted_iota(jnp.int32, (total // 2, LANES), 1)
    for step in range(arrivals):
        bands[step][0:total, :] = held_ref[total : 2 * total, :]
        bands[step][total : 2 * total, :] = held_ref[3 * total : 4 * total, :]
        receiver = look_up(tile_routes[step - 1], tile_ref[0]) if step else tile_ref[0]
        part = rim_ref[:, pl.ds(pl.multiple_of(receiver * LANES, LANES), LANES)] + corner_part
        packed = jnp.where(lane < HALF, part[: total // 2], part[total // 2 :])
        bands[step][2 * total :, :] = packed.astype(jnp.bfloat16)


def rim_lane(edge, position):
    return RIM_LANES[edge] + (position // 2 if edge in (NORTH, SOUTH) else position)


def rim_cell(edge, position):
    across = SIDE // 4
    if edge == NORTH:
        return position
    if edge == EAST:
        return position * across + across - 1
    if edge == SOUTH:
        return LANES - across + position
    return position * across


def turn(position, reverse):
    return position + reverse * (BLOCKS - 1 - 2 * position)


def fill_slots(ids_ref, near_ids_ref, codes_ref, slot_ref, near_ref, kept_codes_ref):
    slots = ids_ref.shape[0]

    def invert(slot, carry):
        slot_ref[ids_ref[slot]] = slot
        return carry

    def find(slot, carry):
        for edge in range(4):
            near_ref[slot, edge] = slot_ref[near_ids_ref[slot, edge]]
            kept_codes_ref[slot, edge] = codes_ref[slot, edge]
        return carry

    lax.fori_loop(0, slots, invert, 0, unroll=slots <= 8)
    lax.fori_loop(0, slots, find, 0, unroll=slots <= 8)


def edge_terms(slot, edge, near_ref, codes_ref):
    near = near_ref[slot, edge]
    code = codes_ref[slot, edge]
    touching, reverse = code % 4, code // 4
    beyond_code = codes_ref[near, touching]
    carried = (near, touching, reverse)
    summed = (near_ref[near, touching], beyond_code % 4, jnp.bitwise_xor(reverse, beyond_code // 4))
    ends = []
    for end in range(2):
        rim_edge = look_up([END_RIMS[option][end][0] for option in range(4)], touching)
        rim_end = look_up([END_RIMS[option][end][1] for option in range(4)], touching)
        other_code = codes_ref[near, rim_edge]
        other_end = jnp.bitwise_xor(rim_end, other_code // 4)
        corner = look_up([EDGE_CORNERS[i // 2][i % 2] for i in range(8)], other_code % 4 * 2 + other_end)
        ends.append((near_ref[near, rim_edge], corner, turn((BLOCKS - 1) * end, reverse)))
    return carried, summed, ends


def rim_map_kernel(tile_ref, near_ref, codes_ref, rim_map_ref, corner_map_ref, wide_ref, corner_ref):
    tile = tile_ref[0]
    wide_ref[...] = jnp.zeros_like(wide_ref)
    corner_ref[...] = jnp.zeros_like(corner_ref)
    block = lax.broadcasted_iota(jnp.int32, (BLOCKS, LANES), 0)
    lane = lax.broadcasted_iota(jnp.int32, (BLOCKS, LANES), 1) % HALF
    corner_row = lax.broadcasted_iota(jnp.int32, (CORNER_ROWS, LANES), 0)
    corner_lane = lax.broadcasted_iota(jnp.int32, (CORNER_ROWS, LANES), 1) % HALF

    def fill(slot, carry):
        columns = pl.ds(pl.multiple_of(slot * LANES, LANES), LANES)
        for edge in range(4):
            carried, summed, ends = edge_terms(slot, edge, near_ref, codes_ref)
            for base, (source, source_edge, reverse) in ((0, carried), (4 * BLOCKS, summed)):
                hit = (lane == rim_lane(edge, turn(block, reverse))) & (source == tile)
                start = pl.multiple_of(base + source_edge * BLOCKS, BLOCKS)
                wide_ref[pl.ds(start, BLOCKS), columns] += hit.astype(jnp.float32)
            for source, corner, position in ends:
                hit = (corner_row == corner) & (corner_lane == rim_lane(edge, position)) & (source == tile)
                corner_ref[:, columns] += hit.astype(jnp.float32)
        return carry

    slots = near_ref.shape[0]
    lax.fori_loop(0, slots, fill, 0, unroll=slots <= 8)
    rim_map_ref[...] = wide_ref[...].astype(jnp.bfloat16)
    corner_map_ref[...] = corner_ref[...].astype(jnp.bfloat16)


def partner_map_kernel(
    routes,
    tile_ref,
    near_ref,
    codes_ref,
    partner_ref,
    velocity_map_ref,
    rim_map_ref,
    chosen_ref,
    arrival_ref,
    wide_ref,
    rim_ref,
):
    tile = tile_ref[0]
    row = lax.broadcasted_iota(jnp.int32, (LANES, LANES), 0) % HALF
    cell = lax.broadcasted_iota(jnp.int32, (LANES, LANES), 1)
    placed = jnp.zeros((LANES, LANES), jnp.bool_)
    for edge in range(4):
        count = SIDE // 4 if edge in (NORTH, SOUTH) else BLOCKS
        position = row - RIM_LANES[edge]
        placed |= (position >= 0) & (position < count) & (cell == rim_cell(edge, position))
    placed = placed.astype(jnp.float32)
    wide_ref[...] = jnp.zeros_like(wide_ref)
    rim_ref[...] = jnp.zeros_like(rim_ref)
    rim_ref[0:LANES, 0:LANES] = placed
    for step, route in enumerate(routes):
        sent = look_up([float(receiver != sender) for sender, receiver in enumerate(route)], tile, jnp.float32)
        rim_ref[(step + 1) * LANES : (step + 2) * LANES, 0:LANES] = placed * sent
    for sender in range(len(routes[0])):
        steps = [0] * len(routes[0])
        for step, route in enumerate(routes):
            if route[sender] != sender:
                steps[route[sender]] = step + 1
        arrival_ref[sender] = look_up(steps, tile)
    block = lax.broadcasted_iota(jnp.int32, (BLOCKS, LANES), 0)
    cell = lax.broadcasted_iota(jnp.int32, (BLOCKS, LANES), 1)
    corner_row = lax.broadcasted_iota(jnp.int32, (8, LANES), 0)
    corner_cell = lax.broadcasted_iota(jnp.int32, (8, LANES), 1)
    step = lax.broadcasted_iota(jnp.int32, (chosen_ref.shape[0], LANES), 0)

    def target(edge, position):
        return rim_cell(edge, position // 2 if edge in (NORTH, SOUTH) else position)

    for partner in range(partner_ref.shape[1]):
        slot = partner_ref[0, partner]
        columns = slice(partner * LANES, (partner + 1) * LANES)
        rim_columns = slice((partner + 1) * LANES, (partner + 2) * LANES)
        chosen_ref[:, columns] = (step == arrival_ref[slot]).astype(jnp.float32)
        for edge in range(4):
            carried, summed, ends = edge_terms(slot, edge, near_ref, codes_ref)
            for base, (source, source_edge, reverse) in ((0, carried), (4 * BLOCKS, summed)):
                hit = cell == target(edge, turn(block, reverse))
                start = pl.multiple_of(arrival_ref[source] * LANES + base + source_edge * BLOCKS, BLOCKS)
                wide_ref[pl.ds(start, BLOCKS), columns] += hit.astype(jnp.float32)
            for source, corner, position in ends:
                hit = (corner_row == corner) & (corner_cell == target(edge, position))
                for base in (CORNER_LANE, HALF + CORNER_LANE):
                    start = pl.multiple_of(arrival_ref[source] * LANES + base, 8)
                    rim_ref[pl.ds(start, 8), rim_columns] += hit.astype(jnp.float32)
    velocity_map_ref[...] = wide_ref[...].astype(jnp.bfloat16)
    rim_map_ref[...] = rim_ref[...].astype(jnp.bfloat16)


def density_kernel(
    arrivals, partners, scale, per_band, height_ref, velocity_map_ref, rim_map_ref, chosen_ref, *rest
):
    bands, (out_ref, cross_ref, sent) = rest[:arrivals], rest[arrivals:]
    total = height_ref.shape[0]
    rims = jnp.concatenate([band[2 * total :, :] for band in bands], axis=1)
    first_half = lax.broadcasted_iota(jnp.int32, rims.shape, 1) % LANES < HALF
    rims = rims.astype(jnp.float32)
    rims = jnp.concatenate([jnp.where(first_half, rims, 0.0), jnp.where(first_half, 0.0, rims)], axis=0)
    rims = dot(rims.astype(jnp.bfloat16), rim_map_ref[...])
    height = height_ref[...].astype(jnp.float32) + rims[:, :LANES]
    velocity = dot(jnp.concatenate([band[total : 2 * total, :] for band in bands], axis=1), velocity_map_ref[...])
    velocity += rims[:, LANES:]
    for step in range(arrivals):
        own = bands[step][0:total, :].astype(jnp.float32)
        velocity += jnp.concatenate([own] * partners, axis=1) * chosen_ref[step : step + 1, :]
    velocity = velocity.astype(jnp.bfloat16)
    height = height.astype(jnp.bfloat16).astype(jnp.float32)
    row = lax.broadcasted_iota(jnp.int32, height.shape, 0)
    rotated = jnp.where(
        (row // per_band) % 2 == 0,
        pltpu.roll(height, total - per_band, 0),
        -pltpu.roll(height, per_band, 0),
    )
    turned = jnp.concatenate([height.T, rotated.T], axis=0)
    lane = lax.broadcasted_iota(jnp.int32, turned.shape, 1)
    copies = []
    for frequency in range(per_band):
        left = jnp.where(lane % per_band == frequency, turned, 0.0).astype(jnp.bfloat16)
        cross = dot(left, velocity) * scale
        for partner in range(partners):
            for part in range(2):
                index = (partner * 2 + part) * per_band + frequency
                rows = pl.ds(index * LANES, LANES)
                cross_ref[rows, :] = cross[
                    part * LANES : (part + 1) * LANES, partner * LANES : (partner + 1) * LANES
                ]
                copies.append(pltpu.make_async_copy(cross_ref.at[rows], out_ref.at[rows], sent.at[index]))
                copies[-1].start()
    for copy in copies:
        copy.wait()


SMEM = pl.BlockSpec(memory_space=pltpu.SMEM)
VMEM = pl.BlockSpec(memory_space=pltpu.VMEM)


def kept(shape, dtype):
    return pltpu.VMEM(shape, dtype)


def scalars(shape, dtype):
    return pltpu.SMEM(shape, dtype)


def near_scalars(value):
    return pltpu.with_memory_space_constraint(value, pltpu.SMEM)


def near(value):
    return pltpu.with_memory_space_constraint(value, pltpu.VMEM)


def shards(tiles, freqs, field_count, fields, slot_tile_ids, neighbour_tile_ids, neighbour_rotation_code, paired_tile_ids):
    field = fields.reshape(fields.shape[2], fields.shape[3])
    samples = field.shape[0]
    devices = freqs * field_count
    per_band = FREQS // devices
    rows = samples // SEGLEN * 2 * per_band
    total = freqs * rows
    partners = paired_tile_ids.shape[1]
    tile = lax.axis_index("tiles").astype(jnp.int32).reshape(1)
    place = (lax.axis_index("freq") * field_count + lax.axis_index("field")).astype(jnp.int32).reshape(1)

    band_routes = routes_for(devices, BAND_ROUTES)
    tile_routes = routes_for(tiles, TILE_ROUTES)
    arrivals = len(tile_routes) + 1

    piece = kept((2 * rows + CORNER_ROWS, LANES), jnp.bfloat16)
    slots = slot_tile_ids.shape[0]
    near_slots, codes, partner_slots, *pieces = pl.pallas_call(
        functools.partial(transform_kernel, band_routes),
        out_shape=[
            scalars((slots, 4), jnp.int32),
            scalars((slots, 4), jnp.int32),
            scalars((1, partners), jnp.int32),
        ]
        + [piece] * devices,
        in_specs=[SMEM] * 5 + [VMEM] * 6,
        out_specs=[SMEM] * 3 + [VMEM] * devices,
        scratch_shapes=[pltpu.SMEM((slots,), jnp.int32)],
        name="transform",
    )(
        place,
        slot_tile_ids,
        neighbour_tile_ids,
        neighbour_rotation_code,
        paired_tile_ids,
        field,
        *cell_tables(),
        *time_tables(devices, samples),
    )
    near_slots, codes, partner_slots = map(near_scalars, (near_slots, codes, partner_slots))
    pieces = [pieces[0]] + [
        lax.ppermute(piece, ("freq", "field"), list(enumerate(route)))
        for piece, route in zip(pieces[1:], band_routes)
    ]

    rim_map, corner_map = pl.pallas_call(
        rim_map_kernel,
        out_shape=[
            kept((LANES, slots * LANES), jnp.bfloat16),
            kept((CORNER_ROWS, slots * LANES), jnp.bfloat16),
        ],
        in_specs=[SMEM] * 3,
        out_specs=[VMEM] * 2,
        scratch_shapes=[
            pltpu.VMEM((LANES, slots * LANES), jnp.float32),
            pltpu.VMEM((CORNER_ROWS, slots * LANES), jnp.float32),
        ],
        name="rim_map",
    )(tile, near_slots, codes)

    *sent, height = pl.pallas_call(
        functools.partial(collect_kernel, band_routes, tile_routes),
        out_shape=[kept((5 * total // 2, LANES), jnp.bfloat16)] * arrivals + [kept((total, LANES), jnp.bfloat16)],
        in_specs=[SMEM] * 2 + [VMEM] * (2 + devices),
        out_specs=[VMEM] * (arrivals + 1),
        scratch_shapes=[
            pltpu.VMEM((4 * total, LANES), jnp.bfloat16),
            pltpu.VMEM((total, slots * LANES), jnp.float32),
        ],
        name="collect",
    )(place, tile, *map(near, (rim_map, corner_map, *pieces)))

    velocity_map, rim_map, chosen = pl.pallas_call(
        functools.partial(partner_map_kernel, tile_routes),
        out_shape=[
            kept((arrivals * LANES, partners * LANES), jnp.bfloat16),
            kept((arrivals * LANES, (1 + partners) * LANES), jnp.bfloat16),
            kept((arrivals + -arrivals % 8, partners * LANES), jnp.float32),
        ],
        in_specs=[SMEM] * 4,
        out_specs=[VMEM] * 3,
        scratch_shapes=[
            pltpu.SMEM((slots,), jnp.int32),
            pltpu.VMEM((arrivals * LANES, partners * LANES), jnp.float32),
            pltpu.VMEM((arrivals * LANES, (1 + partners) * LANES), jnp.float32),
        ],
        name="partner_map",
    )(tile, near_slots, codes, partner_slots)

    bands = [sent[0]]
    for band, route in zip(sent[1:], tile_routes):
        pairs = []
        for sender, receiver in enumerate(route):
            for core in range(field_count):
                there = receiver * field_count + (core if receiver != sender else field_count - 1 - core)
                pairs.append((sender * field_count + core, there))
        bands.append(lax.ppermute(band, ("tiles", "field"), pairs))

    segments = freqs * samples // SEGLEN
    scale = 1.0 / (segments * SEGLEN * 0.375)
    blocks = partners * 2 * per_band
    density = pl.pallas_call(
        functools.partial(density_kernel, arrivals, partners, scale, per_band),
        out_shape=jax.ShapeDtypeStruct((blocks * LANES, LANES), jnp.float32),
        in_specs=[VMEM] * (4 + arrivals),
        out_specs=pl.BlockSpec(memory_space=pl.ANY),
        scratch_shapes=[
            pltpu.VMEM((blocks * LANES, LANES), jnp.float32),
            pltpu.SemaphoreType.DMA((blocks,)),
        ],
        name="density",
    )(*map(near, (height, velocity_map, rim_map, chosen, *bands)))
    return density.reshape(1, partners, 2, per_band, LANES, LANES)


def solution(mesh):
    placed = (P("field", "tiles", ("groups", "freq"), None), P(), P(), P(), P("tiles", None))
    return jax.shard_map(
        functools.partial(shards, mesh.shape["tiles"], mesh.shape["freq"], mesh.shape["field"]),
        mesh=mesh,
        in_specs=placed,
        out_specs=P(("groups", "tiles"), None, None, ("freq", "field"), None, None),
        check_vma=False,
    )
```

```python
import functools
import math

import jax
import jax.numpy as jnp
import ml_dtypes
import numpy as np
from jax import lax
from jax.experimental import pallas as pl
from jax.experimental.pallas import tpu as pltpu
from jax.sharding import PartitionSpec as P

SIDE = 32
SEGLEN = 64
LANES = 128
BLOCKS = SIDE // 2
CORNER_ROWS = 16
FREQS = SEGLEN // 2

NORTH, EAST, SOUTH, WEST = range(4)
HALF = LANES // 2
RIM_LANES = (0, SIDE // 4, SIDE // 4 + BLOCKS, SIDE // 2 + BLOCKS)
CORNER_LANE = SIDE // 2 + 2 * BLOCKS
HEIGHT_CORNER_LANE = CORNER_LANE + 8
EDGE_CORNERS = ((0, 1), (1, 3), (2, 3), (0, 2))
END_RIMS = (
    ((WEST, 0), (EAST, 0)),
    ((NORTH, 1), (SOUTH, 1)),
    ((WEST, 1), (EAST, 1)),
    ((NORTH, 0), (SOUTH, 0)),
)

BAND_ROUTES = ((1, 3, 0, 2), (3, 2, 1, 0), (2, 0, 3, 1))
TILE_ROUTES = ((1, 3, 2, 0), (2, 1, 0, 3), (3, 0, 1, 2), (0, 2, 3, 1))


def routes_for(count, preferred):
    if len(preferred[0]) == count:
        return preferred
    return tuple(tuple(i ^ step for i in range(count)) for step in range(1, count))


def senders(route):
    return tuple(route.index(i) for i in range(len(route)))


def look_up(table, index, dtype=jnp.int32):
    value = dtype(table[0])
    for i in range(1, len(table)):
        value = jnp.where(index == i, dtype(table[i]), value)
    return value


def split_bf16(values):
    high = values.astype(ml_dtypes.bfloat16)
    low = (values - high.astype(np.float64)).astype(ml_dtypes.bfloat16)
    return high, low


@functools.lru_cache(maxsize=None)
def cell_tables():
    cells = SIDE * SIDE

    def at(row, column):
        return row * SIDE + column

    near = np.zeros((cells, cells))
    pool = np.zeros((cells, LANES))
    for row in range(SIDE):
        for column in range(SIDE):
            pool[at(row, column), (row // 2) * (SIDE // 4) + column // 4] = 1
            for down, right in ((1, 0), (-1, 0), (0, 1), (0, -1)):
                if 0 <= row + down < SIDE and 0 <= column + right < SIDE:
                    near[at(row + down, column + right), at(row, column)] = 1
    last = SIDE - 1
    outer = [[at(0, i), at(i, last), at(last, i), at(i, 0)] for i in range(SIDE)]
    inner = [[at(1, i), at(i, last - 1), at(last - 1, i), at(i, 1)] for i in range(SIDE)]
    carried = np.zeros((cells, 4 * BLOCKS))
    sums = np.zeros((cells, 4 * BLOCKS))
    for edge in range(4):
        for i in range(SIDE):
            block = edge * BLOCKS + i // 2
            sums[outer[i][edge], block] += 1
            carried[outer[i][edge], block] += 1
            carried[inner[i][edge], block] += 1
            if i > 0:
                carried[outer[i - 1][edge], block] += 2
            if i < last:
                carried[outer[i + 1][edge], block] += 2
    cell_map = np.concatenate([near @ near @ pool, carried, sums], axis=1)
    first_corners = np.zeros((CORNER_ROWS, LANES))
    last_corners = np.zeros((CORNER_ROWS, LANES))
    first_corners[0, 0] = 1
    first_corners[1, last] = 1
    last_corners[2, LANES - SIDE] = 1
    last_corners[3, LANES - 1] = 1
    to_bf16 = lambda table: table.astype(ml_dtypes.bfloat16)
    return cell_map.astype(ml_dtypes.float8_e4m3fn), to_bf16(first_corners), to_bf16(last_corners)


@functools.lru_cache(maxsize=None)
def time_tables(bands, samples):
    per_band = FREQS // bands
    segments = samples // SEGLEN
    time = np.arange(SEGLEN)
    frequency = np.arange(FREQS)
    angles = 2.0 * math.pi / SEGLEN * (frequency[:, None] * time[None, :] % SEGLEN)
    window = 0.5 - 0.5 * np.cos(2.0 * math.pi / SEGLEN * time)
    waves = np.stack([window * np.cos(angles), -window * np.sin(angles)]) / 16.0
    table = np.zeros((bands, segments, 2, per_band, segments, SEGLEN))
    for segment in range(segments):
        table[:, segment, :, :, segment, :] = waves.reshape(2, bands, per_band, SEGLEN).transpose(1, 0, 2, 3)
    table = table.reshape(bands * segments * 2 * per_band, samples)
    return split_bf16(table)


def dot(left, right):
    return jnp.dot(left, right, preferred_element_type=jnp.float32)


def transform_kernel(
    routes,
    place_ref,
    ids_ref,
    near_ids_ref,
    codes_ref,
    paired_ref,
    x_ref,
    cells_ref,
    first_ref,
    last_ref,
    high_ref,
    low_ref,
    near_ref,
    kept_codes_ref,
    partner_ref,
    *rest,
):
    outs, slot_ref = rest[:-1], rest[-1]
    place = place_ref[0]
    devices = len(outs)
    rows = high_ref.shape[0] // devices
    x = x_ref[...]
    sums = dot(x, cells_ref[...].astype(jnp.bfloat16))
    bands = [place] + [look_up(route, place) for route in routes]
    starts = [pl.multiple_of(band * rows, rows) for band in bands]
    high = jnp.concatenate([high_ref[pl.ds(start, rows), :] for start in starts], axis=0)
    low = jnp.concatenate([low_ref[pl.ds(start, rows), :] for start in starts], axis=0)
    across = (((1,), (1,)), ((), ()))
    corners = lax.dot_general(first_ref[...], x[:, :LANES], across, preferred_element_type=jnp.float32)
    corners += lax.dot_general(
        last_ref[...], x[:, SIDE * SIDE - LANES :], across, preferred_element_type=jnp.float32
    )
    corners = corners.astype(jnp.bfloat16)
    corner_spectra = lax.dot_general(corners, high, across, preferred_element_type=jnp.float32)
    corner_spectra += lax.dot_general(corners, low, across, preferred_element_type=jnp.float32)
    sums_high = sums.astype(jnp.bfloat16)
    sums_low = (sums - sums_high.astype(jnp.float32)).astype(jnp.bfloat16)
    spectra = dot(
        jnp.concatenate([high, high, low], axis=1), jnp.concatenate([sums_high, sums_low, sums_high], axis=0)
    )
    spectra = spectra.astype(jnp.bfloat16)
    lane_start = (place % 2) * (LANES // 2) + (place // 2) * rows
    lane = lax.broadcasted_iota(jnp.int32, (CORNER_ROWS, LANES), 1)
    mine = (lane >= lane_start) & (lane < lane_start + rows)
    for step in range(devices):
        block = spectra[step * rows : (step + 1) * rows]
        outs[step][0:rows, :] = block[:, :LANES]
        outs[step][rows : 2 * rows, :] = block[:, LANES:]
        turned = pltpu.roll(corner_spectra, lax.rem(lane_start - step * rows + LANES, LANES), 1)
        outs[step][2 * rows : 2 * rows + CORNER_ROWS, :] = jnp.where(mine, turned, 0.0).astype(jnp.bfloat16)
    fill_slots(ids_ref, near_ids_ref, codes_ref, slot_ref, near_ref, kept_codes_ref)
    for partner in range(paired_ref.shape[1]):
        partner_ref[0, partner] = slot_ref[paired_ref[0, partner]]


def collect_kernel(band_routes, tile_routes, place_ref, tile_ref, rim_map_ref, *rest):
    devices, arrivals = len(band_routes) + 1, len(tile_routes) + 1
    blocks, rest = rest[:devices], rest[devices:]
    bands, (height_ref, held_ref) = rest[:arrivals], rest[arrivals:]
    place = place_ref[0]
    rows = (blocks[0].shape[0] - CORNER_ROWS) // 2
    total = height_ref.shape[0]
    corners = jnp.zeros((CORNER_ROWS, LANES), jnp.float32)
    for step in range(devices):
        source = look_up(senders(band_routes[step - 1]), place) if step else place
        field, half = source % 2, source // 2
        start = pl.multiple_of(field * total + half * rows, rows)
        held_ref[pl.ds(start, rows), :] = blocks[step][0:rows, :]
        held_ref[pl.ds(2 * total + start, rows), :] = blocks[step][rows : 2 * rows, :]
        corners += blocks[step][2 * rows :, :].astype(jnp.float32)
    height_ref[...] = held_ref[0:total, :]
    row = lax.broadcasted_iota(jnp.int32, (CORNER_ROWS, 2 * LANES), 0)
    lane = lax.broadcasted_iota(jnp.int32, (CORNER_ROWS, 2 * LANES), 1)
    first = jnp.where(lane < LANES, HEIGHT_CORNER_LANE, CORNER_LANE)
    spread = jnp.where((lane % HALF == row + first) & (row < 4), 1.0, 0.0).astype(jnp.bfloat16)
    corners = lax.dot_general(
        corners.astype(jnp.bfloat16), spread, (((0,), (0,)), ((), ())), preferred_element_type=jnp.float32
    )
    corners = corners[:total, :LANES] + corners[total:, LANES:]
    lane = lax.broadcasted_iota(jnp.int32, (total // 2, LANES), 1)
    rims = held_ref[2 * total : 3 * total, :]
    for step in range(arrivals):
        bands[step][0:total, :] = held_ref[total : 2 * total, :]
        bands[step][total : 2 * total, :] = held_ref[3 * total : 4 * total, :]
        receiver = look_up(tile_routes[step - 1], tile_ref[0]) if step else tile_ref[0]
        columns = pl.ds(pl.multiple_of(receiver * LANES, LANES), LANES)
        part = dot(rims, rim_map_ref[:, columns]) + corners
        packed = jnp.where(lane < HALF, part[: total // 2], part[total // 2 :])
        bands[step][2 * total :, :] = packed.astype(jnp.bfloat16)


def rim_lane(edge, position):
    return RIM_LANES[edge] + (position // 2 if edge in (NORTH, SOUTH) else position)


def rim_cell(edge, position):
    across = SIDE // 4
    if edge == NORTH:
        return position
    if edge == EAST:
        return position * across + across - 1
    if edge == SOUTH:
        return LANES - across + position
    return position * across


def turn(position, reverse):
    return position + reverse * (BLOCKS - 1 - 2 * position)


def fill_slots(ids_ref, near_ids_ref, codes_ref, slot_ref, near_ref, kept_codes_ref):
    slots = ids_ref.shape[0]

    def invert(slot, carry):
        slot_ref[ids_ref[slot]] = slot
        return carry

    def find(slot, carry):
        for edge in range(4):
            near_ref[slot, edge] = slot_ref[near_ids_ref[slot, edge]]
            kept_codes_ref[slot, edge] = codes_ref[slot, edge]
        return carry

    lax.fori_loop(0, slots, invert, 0, unroll=slots <= 8)
    lax.fori_loop(0, slots, find, 0, unroll=slots <= 8)


def edge_terms(slot, edge, near_ref, codes_ref):
    near = near_ref[slot, edge]
    code = codes_ref[slot, edge]
    touching, reverse = code % 4, code // 4
    beyond_code = codes_ref[near, touching]
    carried = (near, touching, reverse)
    summed = (near_ref[near, touching], beyond_code % 4, jnp.bitwise_xor(reverse, beyond_code // 4))
    ends = []
    for end in range(2):
        rim_edge = look_up([END_RIMS[option][end][0] for option in range(4)], touching)
        rim_end = look_up([END_RIMS[option][end][1] for option in range(4)], touching)
        other_code = codes_ref[near, rim_edge]
        other_end = jnp.bitwise_xor(rim_end, other_code // 4)
        corner = look_up([EDGE_CORNERS[i // 2][i % 2] for i in range(8)], other_code % 4 * 2 + other_end)
        ends.append((near_ref[near, rim_edge], corner, turn((BLOCKS - 1) * end, reverse)))
    return carried, summed, ends


def rim_map_kernel(tile_ref, near_ref, codes_ref, rim_map_ref, wide_ref):
    tile = tile_ref[0]
    wide_ref[...] = jnp.zeros_like(wide_ref)
    block = lax.broadcasted_iota(jnp.int32, (BLOCKS, LANES), 0)
    lane = lax.broadcasted_iota(jnp.int32, (BLOCKS, LANES), 1) % HALF

    def fill(slot, carry):
        columns = pl.ds(pl.multiple_of(slot * LANES, LANES), LANES)
        for edge in range(4):
            carried, summed, _ = edge_terms(slot, edge, near_ref, codes_ref)
            for base, (source, source_edge, reverse) in ((0, carried), (4 * BLOCKS, summed)):
                hit = (lane == rim_lane(edge, turn(block, reverse))) & (source == tile)
                start = pl.multiple_of(base + source_edge * BLOCKS, BLOCKS)
                wide_ref[pl.ds(start, BLOCKS), columns] += hit.astype(jnp.float32)
        return carry

    slots = near_ref.shape[0]
    lax.fori_loop(0, slots, fill, 0, unroll=slots <= 8)
    rim_map_ref[...] = wide_ref[...].astype(jnp.bfloat16)


def partner_map_kernel(
    routes,
    tile_ref,
    near_ref,
    codes_ref,
    partner_ref,
    velocity_map_ref,
    rim_map_ref,
    chosen_ref,
    arrival_ref,
    wide_ref,
    rim_ref,
):
    tile = tile_ref[0]
    row = lax.broadcasted_iota(jnp.int32, (LANES, LANES), 0) % HALF
    cell = lax.broadcasted_iota(jnp.int32, (LANES, LANES), 1)
    placed = jnp.zeros((LANES, LANES), jnp.bool_)
    for edge in range(4):
        count = SIDE // 4 if edge in (NORTH, SOUTH) else BLOCKS
        position = row - RIM_LANES[edge]
        placed |= (position >= 0) & (position < count) & (cell == rim_cell(edge, position))
    placed = placed.astype(jnp.float32)
    wide_ref[...] = jnp.zeros_like(wide_ref)
    rim_ref[...] = jnp.zeros_like(rim_ref)
    rim_ref[0:LANES, 0:LANES] = placed
    for step, route in enumerate(routes):
        sent = look_up([float(receiver != sender) for sender, receiver in enumerate(route)], tile, jnp.float32)
        rim_ref[(step + 1) * LANES : (step + 2) * LANES, 0:LANES] = placed * sent
    for sender in range(len(routes[0])):
        steps = [0] * len(routes[0])
        for step, route in enumerate(routes):
            if route[sender] != sender:
                steps[route[sender]] = step + 1
        arrival_ref[sender] = look_up(steps, tile)
    block = lax.broadcasted_iota(jnp.int32, (BLOCKS, LANES), 0)
    cell = lax.broadcasted_iota(jnp.int32, (BLOCKS, LANES), 1)
    corner_row = lax.broadcasted_iota(jnp.int32, (8, LANES), 0)
    corner_cell = lax.broadcasted_iota(jnp.int32, (8, LANES), 1)
    step = lax.broadcasted_iota(jnp.int32, (chosen_ref.shape[0], LANES), 0)

    def target(edge, position):
        return rim_cell(edge, position // 2 if edge in (NORTH, SOUTH) else position)

    def add_corners(ends, edge, first_lane, columns):
        for source, corner, position in ends:
            hit = (corner_row == corner) & (corner_cell == target(edge, position))
            for base in (first_lane, HALF + first_lane):
                start = pl.multiple_of(arrival_ref[source] * LANES + base, 8)
                rim_ref[pl.ds(start, 8), columns] += hit.astype(jnp.float32)

    for edge in range(4):
        _, _, ends = edge_terms(tile, edge, near_ref, codes_ref)
        add_corners(ends, edge, HEIGHT_CORNER_LANE, slice(0, LANES))
    for partner in range(partner_ref.shape[1]):
        slot = partner_ref[0, partner]
        columns = slice(partner * LANES, (partner + 1) * LANES)
        rim_columns = slice((partner + 1) * LANES, (partner + 2) * LANES)
        chosen_ref[:, columns] = (step == arrival_ref[slot]).astype(jnp.float32)
        for edge in range(4):
            carried, summed, ends = edge_terms(slot, edge, near_ref, codes_ref)
            for base, (source, source_edge, reverse) in ((0, carried), (4 * BLOCKS, summed)):
                hit = cell == target(edge, turn(block, reverse))
                start = pl.multiple_of(arrival_ref[source] * LANES + base + source_edge * BLOCKS, BLOCKS)
                wide_ref[pl.ds(start, BLOCKS), columns] += hit.astype(jnp.float32)
            add_corners(ends, edge, CORNER_LANE, rim_columns)
    velocity_map_ref[...] = wide_ref[...].astype(jnp.bfloat16)
    rim_map_ref[...] = rim_ref[...].astype(jnp.bfloat16)


def density_kernel(
    arrivals, partners, scale, per_band, height_ref, velocity_map_ref, rim_map_ref, chosen_ref, *rest
):
    bands, (out_ref, cross_ref, sent) = rest[:arrivals], rest[arrivals:]
    total = height_ref.shape[0]
    rims = jnp.concatenate([band[2 * total :, :] for band in bands], axis=1)
    first_half = lax.broadcasted_iota(jnp.int32, rims.shape, 1) % LANES < HALF
    rims = rims.astype(jnp.float32)
    rims = jnp.concatenate([jnp.where(first_half, rims, 0.0), jnp.where(first_half, 0.0, rims)], axis=0)
    rims = dot(rims.astype(jnp.bfloat16), rim_map_ref[...])
    height = height_ref[...].astype(jnp.float32) + rims[:, :LANES]
    velocity = dot(jnp.concatenate([band[total : 2 * total, :] for band in bands], axis=1), velocity_map_ref[...])
    velocity += rims[:, LANES:]
    for step in range(arrivals):
        own = bands[step][0:total, :].astype(jnp.float32)
        velocity += jnp.concatenate([own] * partners, axis=1) * chosen_ref[step : step + 1, :]
    velocity = velocity.astype(jnp.bfloat16)
    height = height.astype(jnp.bfloat16).astype(jnp.float32)
    row = lax.broadcasted_iota(jnp.int32, height.shape, 0)
    rotated = jnp.where(
        (row // per_band) % 2 == 0,
        pltpu.roll(height, total - per_band, 0),
        -pltpu.roll(height, per_band, 0),
    )
    turned = jnp.concatenate([height.T, rotated.T], axis=0)
    lane = lax.broadcasted_iota(jnp.int32, turned.shape, 1)
    copies = []
    for frequency in range(per_band):
        left = jnp.where(lane % per_band == frequency, turned, 0.0).astype(jnp.bfloat16)
        cross = dot(left, velocity) * scale
        for partner in range(partners):
            for part in range(2):
                index = (partner * 2 + part) * per_band + frequency
                rows = pl.ds(index * LANES, LANES)
                cross_ref[rows, :] = cross[
                    part * LANES : (part + 1) * LANES, partner * LANES : (partner + 1) * LANES
                ]
                copies.append(pltpu.make_async_copy(cross_ref.at[rows], out_ref.at[rows], sent.at[index]))
                copies[-1].start()
    for copy in copies:
        copy.wait()


SMEM = pl.BlockSpec(memory_space=pltpu.SMEM)
VMEM = pl.BlockSpec(memory_space=pltpu.VMEM)


def kept(shape, dtype):
    return pltpu.VMEM(shape, dtype)


def scalars(shape, dtype):
    return pltpu.SMEM(shape, dtype)


def near_scalars(value):
    return pltpu.with_memory_space_constraint(value, pltpu.SMEM)


def near(value):
    return pltpu.with_memory_space_constraint(value, pltpu.VMEM)


def shards(tiles, freqs, field_count, fields, slot_tile_ids, neighbour_tile_ids, neighbour_rotation_code, paired_tile_ids):
    field = fields.reshape(fields.shape[2], fields.shape[3])
    samples = field.shape[0]
    devices = freqs * field_count
    per_band = FREQS // devices
    rows = samples // SEGLEN * 2 * per_band
    total = freqs * rows
    partners = paired_tile_ids.shape[1]
    tile = lax.axis_index("tiles").astype(jnp.int32).reshape(1)
    place = (lax.axis_index("freq") * field_count + lax.axis_index("field")).astype(jnp.int32).reshape(1)

    band_routes = routes_for(devices, BAND_ROUTES)
    tile_routes = routes_for(tiles, TILE_ROUTES)
    arrivals = len(tile_routes) + 1

    piece = kept((2 * rows + CORNER_ROWS, LANES), jnp.bfloat16)
    slots = slot_tile_ids.shape[0]
    near_slots, codes, partner_slots, *pieces = pl.pallas_call(
        functools.partial(transform_kernel, band_routes),
        out_shape=[
            scalars((slots, 4), jnp.int32),
            scalars((slots, 4), jnp.int32),
            scalars((1, partners), jnp.int32),
        ]
        + [piece] * devices,
        in_specs=[SMEM] * 5 + [VMEM] * 6,
        out_specs=[SMEM] * 3 + [VMEM] * devices,
        scratch_shapes=[pltpu.SMEM((slots,), jnp.int32)],
        name="transform",
    )(
        place,
        slot_tile_ids,
        neighbour_tile_ids,
        neighbour_rotation_code,
        paired_tile_ids,
        field,
        *cell_tables(),
        *time_tables(devices, samples),
    )
    near_slots, codes, partner_slots = map(near_scalars, (near_slots, codes, partner_slots))
    pieces = [pieces[0]] + [
        lax.ppermute(piece, ("freq", "field"), list(enumerate(route)))
        for piece, route in zip(pieces[1:], band_routes)
    ]

    rim_map = pl.pallas_call(
        rim_map_kernel,
        out_shape=kept((LANES, slots * LANES), jnp.bfloat16),
        in_specs=[SMEM] * 3,
        out_specs=VMEM,
        scratch_shapes=[pltpu.VMEM((LANES, slots * LANES), jnp.float32)],
        name="rim_map",
    )(tile, near_slots, codes)

    *sent, height = pl.pallas_call(
        functools.partial(collect_kernel, band_routes, tile_routes),
        out_shape=[kept((5 * total // 2, LANES), jnp.bfloat16)] * arrivals + [kept((total, LANES), jnp.bfloat16)],
        in_specs=[SMEM] * 2 + [VMEM] * (1 + devices),
        out_specs=[VMEM] * (arrivals + 1),
        scratch_shapes=[pltpu.VMEM((4 * total, LANES), jnp.bfloat16)],
        name="collect",
    )(place, tile, *map(near, (rim_map, *pieces)))

    velocity_map, rim_map, chosen = pl.pallas_call(
        functools.partial(partner_map_kernel, tile_routes),
        out_shape=[
            kept((arrivals * LANES, partners * LANES), jnp.bfloat16),
            kept((arrivals * LANES, (1 + partners) * LANES), jnp.bfloat16),
            kept((arrivals + -arrivals % 8, partners * LANES), jnp.float32),
        ],
        in_specs=[SMEM] * 4,
        out_specs=[VMEM] * 3,
        scratch_shapes=[
            pltpu.SMEM((slots,), jnp.int32),
            pltpu.VMEM((arrivals * LANES, partners * LANES), jnp.float32),
            pltpu.VMEM((arrivals * LANES, (1 + partners) * LANES), jnp.float32),
        ],
        name="partner_map",
    )(tile, near_slots, codes, partner_slots)

    bands = [sent[0]]
    for band, route in zip(sent[1:], tile_routes):
        pairs = []
        for sender, receiver in enumerate(route):
            for core in range(field_count):
                there = receiver * field_count + (core if receiver != sender else field_count - 1 - core)
                pairs.append((sender * field_count + core, there))
        bands.append(lax.ppermute(band, ("tiles", "field"), pairs))

    segments = freqs * samples // SEGLEN
    scale = 1.0 / (segments * SEGLEN * 0.375)
    blocks = partners * 2 * per_band
    density = pl.pallas_call(
        functools.partial(density_kernel, arrivals, partners, scale, per_band),
        out_shape=jax.ShapeDtypeStruct((blocks * LANES, LANES), jnp.float32),
        in_specs=[VMEM] * (4 + arrivals),
        out_specs=pl.BlockSpec(memory_space=pl.ANY),
        scratch_shapes=[
            pltpu.VMEM((blocks * LANES, LANES), jnp.float32),
            pltpu.SemaphoreType.DMA((blocks,)),
        ],
        name="density",
    )(*map(near, (height, velocity_map, rim_map, chosen, *bands)))
    return density.reshape(1, partners, 2, per_band, LANES, LANES)


def solution(mesh):
    placed = (P("field", "tiles", ("groups", "freq"), None), P(), P(), P(), P("tiles", None))
    return jax.shard_map(
        functools.partial(shards, mesh.shape["tiles"], mesh.shape["freq"], mesh.shape["field"]),
        mesh=mesh,
        in_specs=placed,
        out_specs=P(("groups", "tiles"), None, None, ("freq", "field"), None, None),
        check_vma=False,
    )
```

```python
import functools
import math

import jax
import jax.numpy as jnp
import ml_dtypes
import numpy as np
from jax import lax
from jax.experimental import pallas as pl
from jax.experimental.pallas import tpu as pltpu
from jax.sharding import PartitionSpec as P

SIDE = 32
SEGLEN = 64
LANES = 128
BLOCKS = SIDE // 2
CORNER_ROWS = 16
FREQS = SEGLEN // 2

NORTH, EAST, SOUTH, WEST = range(4)
HALF = LANES // 2
RIM_LANES = (0, SIDE // 4, SIDE // 4 + BLOCKS, SIDE // 2 + BLOCKS)
CORNER_LANE = SIDE // 2 + 2 * BLOCKS
HEIGHT_CORNER_LANE = CORNER_LANE + 8
EDGE_CORNERS = ((0, 1), (1, 3), (2, 3), (0, 2))
END_RIMS = (
    ((WEST, 0), (EAST, 0)),
    ((NORTH, 1), (SOUTH, 1)),
    ((WEST, 1), (EAST, 1)),
    ((NORTH, 0), (SOUTH, 0)),
)

BAND_ROUTES = ((1, 3, 0, 2), (3, 2, 1, 0), (2, 0, 3, 1))
TILE_ROUTES = ((1, 3, 2, 0), (2, 1, 0, 3), (3, 0, 1, 2), (0, 2, 3, 1))


def routes_for(count, preferred):
    if len(preferred[0]) == count:
        return preferred
    return tuple(tuple(i ^ step for i in range(count)) for step in range(1, count))


def senders(route):
    return tuple(route.index(i) for i in range(len(route)))


def look_up(table, index, dtype=jnp.int32):
    value = dtype(table[0])
    for i in range(1, len(table)):
        value = jnp.where(index == i, dtype(table[i]), value)
    return value


def split_bf16(values):
    high = values.astype(ml_dtypes.bfloat16)
    low = (values - high.astype(np.float64)).astype(ml_dtypes.bfloat16)
    return high, low


@functools.lru_cache(maxsize=None)
def cell_table():
    cells = SIDE * SIDE

    def at(row, column):
        return row * SIDE + column

    near = np.zeros((cells, cells))
    pool = np.zeros((cells, LANES))
    for row in range(SIDE):
        for column in range(SIDE):
            pool[at(row, column), (row // 2) * (SIDE // 4) + column // 4] = 1
            for down, right in ((1, 0), (-1, 0), (0, 1), (0, -1)):
                if 0 <= row + down < SIDE and 0 <= column + right < SIDE:
                    near[at(row + down, column + right), at(row, column)] = 1
    last = SIDE - 1
    outer = [[at(0, i), at(i, last), at(last, i), at(i, 0)] for i in range(SIDE)]
    inner = [[at(1, i), at(i, last - 1), at(last - 1, i), at(i, 1)] for i in range(SIDE)]
    carried = np.zeros((cells, 4 * BLOCKS))
    sums = np.zeros((cells, 4 * BLOCKS))
    for edge in range(4):
        for i in range(SIDE):
            block = edge * BLOCKS + i // 2
            sums[outer[i][edge], block] += 1
            carried[outer[i][edge], block] += 1
            carried[inner[i][edge], block] += 1
            if i > 0:
                carried[outer[i - 1][edge], block] += 2
            if i < last:
                carried[outer[i + 1][edge], block] += 2
    cell_map = np.concatenate([near @ near @ pool, carried, sums], axis=1)
    return cell_map.astype(ml_dtypes.float8_e4m3fn)


@functools.lru_cache(maxsize=None)
def time_table(bands, samples):
    per_band = FREQS // bands
    segments = samples // SEGLEN
    time = np.arange(SEGLEN)
    frequency = np.arange(FREQS)
    angles = 2.0 * math.pi / SEGLEN * (frequency[:, None] * time[None, :] % SEGLEN)
    window = 0.5 - 0.5 * np.cos(2.0 * math.pi / SEGLEN * time)
    waves = np.stack([window * np.cos(angles), -window * np.sin(angles)]) / 16.0
    table = np.zeros((bands, segments, 2, per_band, segments, SEGLEN))
    for segment in range(segments):
        table[:, segment, :, :, segment, :] = waves.reshape(2, bands, per_band, SEGLEN).transpose(1, 0, 2, 3)
    table = table.reshape(bands * segments * 2 * per_band, samples)
    return np.concatenate(split_bf16(table), axis=0)


def dot(left, right):
    return jnp.dot(left, right, preferred_element_type=jnp.float32)


def transform_kernel(
    routes,
    place_ref,
    ids_ref,
    near_ids_ref,
    codes_ref,
    paired_ref,
    x_ref,
    cells_ref,
    waves_ref,
    near_ref,
    kept_codes_ref,
    partner_ref,
    *rest,
):
    outs, slot_ref = rest[:-1], rest[-1]
    place = place_ref[0]
    devices = len(outs)
    count = waves_ref.shape[0] // 2
    rows = count // devices
    x = x_ref[...]
    sums = dot(x, cells_ref[...].astype(jnp.bfloat16))
    bands = [place] + [look_up(route, place) for route in routes]
    starts = [pl.multiple_of(band * rows, rows) for band in bands]
    high = jnp.concatenate([waves_ref[pl.ds(start, rows), :] for start in starts], axis=0)
    low = jnp.concatenate([waves_ref[pl.ds(count + start, rows), :] for start in starts], axis=0)
    across = (((1,), (1,)), ((), ()))
    row = lax.broadcasted_iota(jnp.int32, (CORNER_ROWS, LANES), 0)
    lane = lax.broadcasted_iota(jnp.int32, (CORNER_ROWS, LANES), 1)
    first = ((row == 0) & (lane == 0)) | ((row == 1) & (lane == SIDE - 1))
    last = ((row == 2) & (lane == LANES - SIDE)) | ((row == 3) & (lane == LANES - 1))
    first, last = (jnp.where(hit, 1.0, 0.0).astype(jnp.bfloat16) for hit in (first, last))
    corners = lax.dot_general(first, x[:, :LANES], across, preferred_element_type=jnp.float32)
    corners += lax.dot_general(
        last, x[:, SIDE * SIDE - LANES :], across, preferred_element_type=jnp.float32
    )
    corners = corners.astype(jnp.bfloat16)
    corner_spectra = lax.dot_general(corners, high, across, preferred_element_type=jnp.float32)
    corner_spectra += lax.dot_general(corners, low, across, preferred_element_type=jnp.float32)
    sums_high = sums.astype(jnp.bfloat16)
    sums_low = (sums - sums_high.astype(jnp.float32)).astype(jnp.bfloat16)
    spectra = dot(
        jnp.concatenate([high, high, low], axis=1), jnp.concatenate([sums_high, sums_low, sums_high], axis=0)
    )
    spectra = spectra.astype(jnp.bfloat16)
    lane_start = (place % 2) * (LANES // 2) + (place // 2) * rows
    lane = lax.broadcasted_iota(jnp.int32, (CORNER_ROWS, LANES), 1)
    mine = (lane >= lane_start) & (lane < lane_start + rows)
    for step in range(devices):
        block = spectra[step * rows : (step + 1) * rows]
        outs[step][0:rows, :] = block[:, :LANES]
        outs[step][rows : 2 * rows, :] = block[:, LANES:]
        turned = pltpu.roll(corner_spectra, lax.rem(lane_start - step * rows + LANES, LANES), 1)
        outs[step][2 * rows : 2 * rows + CORNER_ROWS, :] = jnp.where(mine, turned, 0.0).astype(jnp.bfloat16)
    fill_slots(ids_ref, near_ids_ref, codes_ref, slot_ref, near_ref, kept_codes_ref)
    for partner in range(paired_ref.shape[1]):
        partner_ref[0, partner] = slot_ref[paired_ref[0, partner]]


def collect_kernel(band_routes, tile_routes, place_ref, tile_ref, rim_map_ref, *rest):
    devices, arrivals = len(band_routes) + 1, len(tile_routes) + 1
    blocks, rest = rest[:devices], rest[devices:]
    bands, (height_ref, held_ref) = rest[:arrivals], rest[arrivals:]
    place = place_ref[0]
    rows = (blocks[0].shape[0] - CORNER_ROWS) // 2
    total = height_ref.shape[0]
    corners = jnp.zeros((CORNER_ROWS, LANES), jnp.float32)
    for step in range(devices):
        source = look_up(senders(band_routes[step - 1]), place) if step else place
        field, half = source % 2, source // 2
        start = pl.multiple_of(field * total + half * rows, rows)
        held_ref[pl.ds(start, rows), :] = blocks[step][0:rows, :]
        held_ref[pl.ds(2 * total + start, rows), :] = blocks[step][rows : 2 * rows, :]
        corners += blocks[step][2 * rows :, :].astype(jnp.float32)
    height_ref[...] = held_ref[0:total, :]
    row = lax.broadcasted_iota(jnp.int32, (CORNER_ROWS, 2 * LANES), 0)
    lane = lax.broadcasted_iota(jnp.int32, (CORNER_ROWS, 2 * LANES), 1)
    first = jnp.where(lane < LANES, HEIGHT_CORNER_LANE, CORNER_LANE)
    spread = jnp.where((lane % HALF == row + first) & (row < 4), 1.0, 0.0).astype(jnp.bfloat16)
    corners = lax.dot_general(
        corners.astype(jnp.bfloat16), spread, (((0,), (0,)), ((), ())), preferred_element_type=jnp.float32
    )
    corners = corners[:total, :LANES] + corners[total:, LANES:]
    lane = lax.broadcasted_iota(jnp.int32, (total // 2, LANES), 1)
    rims = held_ref[2 * total : 3 * total, :]
    for step in range(arrivals):
        bands[step][0:total, :] = held_ref[total : 2 * total, :]
        bands[step][total : 2 * total, :] = held_ref[3 * total : 4 * total, :]
        receiver = look_up(tile_routes[step - 1], tile_ref[0]) if step else tile_ref[0]
        columns = pl.ds(pl.multiple_of(receiver * LANES, LANES), LANES)
        part = dot(rims, rim_map_ref[:, columns]) + corners
        packed = jnp.where(lane < HALF, part[: total // 2], part[total // 2 :])
        bands[step][2 * total :, :] = packed.astype(jnp.bfloat16)


def rim_lane(edge, position):
    return RIM_LANES[edge] + (position // 2 if edge in (NORTH, SOUTH) else position)


def rim_cell(edge, position):
    across = SIDE // 4
    if edge == NORTH:
        return position
    if edge == EAST:
        return position * across + across - 1
    if edge == SOUTH:
        return LANES - across + position
    return position * across


def turn(position, reverse):
    return position + reverse * (BLOCKS - 1 - 2 * position)


def fill_slots(ids_ref, near_ids_ref, codes_ref, slot_ref, near_ref, kept_codes_ref):
    slots = ids_ref.shape[0]

    def invert(slot, carry):
        slot_ref[ids_ref[slot]] = slot
        return carry

    def find(slot, carry):
        for edge in range(4):
            near_ref[slot, edge] = slot_ref[near_ids_ref[slot, edge]]
            kept_codes_ref[slot, edge] = codes_ref[slot, edge]
        return carry

    lax.fori_loop(0, slots, invert, 0, unroll=slots <= 8)
    lax.fori_loop(0, slots, find, 0, unroll=slots <= 8)


def edge_terms(slot, edge, near_ref, codes_ref):
    near = near_ref[slot, edge]
    code = codes_ref[slot, edge]
    touching, reverse = code % 4, code // 4
    beyond_code = codes_ref[near, touching]
    carried = (near, touching, reverse)
    summed = (near_ref[near, touching], beyond_code % 4, jnp.bitwise_xor(reverse, beyond_code // 4))
    ends = []
    for end in range(2):
        rim_edge = look_up([END_RIMS[option][end][0] for option in range(4)], touching)
        rim_end = look_up([END_RIMS[option][end][1] for option in range(4)], touching)
        other_code = codes_ref[near, rim_edge]
        other_end = jnp.bitwise_xor(rim_end, other_code // 4)
        corner = look_up([EDGE_CORNERS[i // 2][i % 2] for i in range(8)], other_code % 4 * 2 + other_end)
        ends.append((near_ref[near, rim_edge], corner, turn((BLOCKS - 1) * end, reverse)))
    return carried, summed, ends


def rim_map_kernel(tile_ref, near_ref, codes_ref, rim_map_ref, wide_ref):
    tile = tile_ref[0]
    wide_ref[...] = jnp.zeros_like(wide_ref)
    block = lax.broadcasted_iota(jnp.int32, (BLOCKS, LANES), 0)
    lane = lax.broadcasted_iota(jnp.int32, (BLOCKS, LANES), 1) % HALF

    def fill(slot, carry):
        columns = pl.ds(pl.multiple_of(slot * LANES, LANES), LANES)
        for edge in range(4):
            carried, summed, _ = edge_terms(slot, edge, near_ref, codes_ref)
            for base, (source, source_edge, reverse) in ((0, carried), (4 * BLOCKS, summed)):
                hit = (lane == rim_lane(edge, turn(block, reverse))) & (source == tile)
                start = pl.multiple_of(base + source_edge * BLOCKS, BLOCKS)
                wide_ref[pl.ds(start, BLOCKS), columns] += hit.astype(jnp.float32)
        return carry

    slots = near_ref.shape[0]
    lax.fori_loop(0, slots, fill, 0, unroll=slots <= 8)
    rim_map_ref[...] = wide_ref[...].astype(jnp.bfloat16)


def partner_map_kernel(
    routes,
    tile_ref,
    near_ref,
    codes_ref,
    partner_ref,
    velocity_map_ref,
    rim_map_ref,
    chosen_ref,
    arrival_ref,
    wide_ref,
    rim_ref,
):
    tile = tile_ref[0]
    row = lax.broadcasted_iota(jnp.int32, (LANES, LANES), 0) % HALF
    cell = lax.broadcasted_iota(jnp.int32, (LANES, LANES), 1)
    placed = jnp.zeros((LANES, LANES), jnp.bool_)
    for edge in range(4):
        count = SIDE // 4 if edge in (NORTH, SOUTH) else BLOCKS
        position = row - RIM_LANES[edge]
        placed |= (position >= 0) & (position < count) & (cell == rim_cell(edge, position))
    placed = placed.astype(jnp.float32)
    wide_ref[...] = jnp.zeros_like(wide_ref)
    rim_ref[...] = jnp.zeros_like(rim_ref)
    rim_ref[0:LANES, 0:LANES] = placed
    for step, route in enumerate(routes):
        sent = look_up([float(receiver != sender) for sender, receiver in enumerate(route)], tile, jnp.float32)
        rim_ref[(step + 1) * LANES : (step + 2) * LANES, 0:LANES] = placed * sent
    for sender in range(len(routes[0])):
        steps = [0] * len(routes[0])
        for step, route in enumerate(routes):
            if route[sender] != sender:
                steps[route[sender]] = step + 1
        arrival_ref[sender] = look_up(steps, tile)
    block = lax.broadcasted_iota(jnp.int32, (BLOCKS, LANES), 0)
    cell = lax.broadcasted_iota(jnp.int32, (BLOCKS, LANES), 1)
    corner_row = lax.broadcasted_iota(jnp.int32, (8, LANES), 0)
    corner_cell = lax.broadcasted_iota(jnp.int32, (8, LANES), 1)
    step = lax.broadcasted_iota(jnp.int32, (chosen_ref.shape[0], LANES), 0)

    def target(edge, position):
        return rim_cell(edge, position // 2 if edge in (NORTH, SOUTH) else position)

    def add_corners(ends, edge, first_lane, columns):
        for source, corner, position in ends:
            hit = (corner_row == corner) & (corner_cell == target(edge, position))
            for base in (first_lane, HALF + first_lane):
                start = pl.multiple_of(arrival_ref[source] * LANES + base, 8)
                rim_ref[pl.ds(start, 8), columns] += hit.astype(jnp.float32)

    for edge in range(4):
        _, _, ends = edge_terms(tile, edge, near_ref, codes_ref)
        add_corners(ends, edge, HEIGHT_CORNER_LANE, slice(0, LANES))
    for partner in range(partner_ref.shape[1]):
        slot = partner_ref[0, partner]
        columns = slice(partner * LANES, (partner + 1) * LANES)
        rim_columns = slice((partner + 1) * LANES, (partner + 2) * LANES)
        chosen_ref[:, columns] = (step == arrival_ref[slot]).astype(jnp.float32)
        for edge in range(4):
            carried, summed, ends = edge_terms(slot, edge, near_ref, codes_ref)
            for base, (source, source_edge, reverse) in ((0, carried), (4 * BLOCKS, summed)):
                hit = cell == target(edge, turn(block, reverse))
                start = pl.multiple_of(arrival_ref[source] * LANES + base + source_edge * BLOCKS, BLOCKS)
                wide_ref[pl.ds(start, BLOCKS), columns] += hit.astype(jnp.float32)
            add_corners(ends, edge, CORNER_LANE, rim_columns)
    velocity_map_ref[...] = wide_ref[...].astype(jnp.bfloat16)
    rim_map_ref[...] = rim_ref[...].astype(jnp.bfloat16)


def density_kernel(
    arrivals, partners, scale, per_band, height_ref, velocity_map_ref, rim_map_ref, chosen_ref, *rest
):
    bands, (out_ref, cross_ref, sent) = rest[:arrivals], rest[arrivals:]
    total = height_ref.shape[0]
    rims = jnp.concatenate([band[2 * total :, :] for band in bands], axis=1)
    first_half = lax.broadcasted_iota(jnp.int32, rims.shape, 1) % LANES < HALF
    rims = rims.astype(jnp.float32)
    rims = jnp.concatenate([jnp.where(first_half, rims, 0.0), jnp.where(first_half, 0.0, rims)], axis=0)
    rims = dot(rims.astype(jnp.bfloat16), rim_map_ref[...])
    height = height_ref[...].astype(jnp.float32) + rims[:, :LANES]
    velocity = dot(jnp.concatenate([band[total : 2 * total, :] for band in bands], axis=1), velocity_map_ref[...])
    velocity += rims[:, LANES:]
    for step in range(arrivals):
        own = bands[step][0:total, :].astype(jnp.float32)
        velocity += jnp.concatenate([own] * partners, axis=1) * chosen_ref[step : step + 1, :]
    velocity = velocity.astype(jnp.bfloat16)
    height = height.astype(jnp.bfloat16).astype(jnp.float32)
    row = lax.broadcasted_iota(jnp.int32, height.shape, 0)
    rotated = jnp.where(
        (row // per_band) % 2 == 0,
        pltpu.roll(height, total - per_band, 0),
        -pltpu.roll(height, per_band, 0),
    )
    turned = jnp.concatenate([height.T, rotated.T], axis=0)
    lane = lax.broadcasted_iota(jnp.int32, turned.shape, 1)
    copies = []
    for frequency in range(per_band):
        left = jnp.where(lane % per_band == frequency, turned, 0.0).astype(jnp.bfloat16)
        cross = dot(left, velocity) * scale
        for partner in range(partners):
            for part in range(2):
                index = (partner * 2 + part) * per_band + frequency
                rows = pl.ds(index * LANES, LANES)
                cross_ref[rows, :] = cross[
                    part * LANES : (part + 1) * LANES, partner * LANES : (partner + 1) * LANES
                ]
                copies.append(pltpu.make_async_copy(cross_ref.at[rows], out_ref.at[rows], sent.at[index]))
                copies[-1].start()
    for copy in copies:
        copy.wait()


SMEM = pl.BlockSpec(memory_space=pltpu.SMEM)
VMEM = pl.BlockSpec(memory_space=pltpu.VMEM)


def kept(shape, dtype):
    return pltpu.VMEM(shape, dtype)


def scalars(shape, dtype):
    return pltpu.SMEM(shape, dtype)


def near_scalars(value):
    return pltpu.with_memory_space_constraint(value, pltpu.SMEM)


def near(value):
    return pltpu.with_memory_space_constraint(value, pltpu.VMEM)


def shards(tiles, freqs, field_count, fields, slot_tile_ids, neighbour_tile_ids, neighbour_rotation_code, paired_tile_ids):
    field = fields.reshape(fields.shape[2], fields.shape[3])
    samples = field.shape[0]
    devices = freqs * field_count
    per_band = FREQS // devices
    rows = samples // SEGLEN * 2 * per_band
    total = freqs * rows
    partners = paired_tile_ids.shape[1]
    tile = lax.axis_index("tiles").astype(jnp.int32).reshape(1)
    place = (lax.axis_index("freq") * field_count + lax.axis_index("field")).astype(jnp.int32).reshape(1)

    band_routes = routes_for(devices, BAND_ROUTES)
    tile_routes = routes_for(tiles, TILE_ROUTES)
    arrivals = len(tile_routes) + 1

    piece = kept((2 * rows + CORNER_ROWS, LANES), jnp.bfloat16)
    slots = slot_tile_ids.shape[0]
    near_slots, codes, partner_slots, *pieces = pl.pallas_call(
        functools.partial(transform_kernel, band_routes),
        out_shape=[
            scalars((slots, 4), jnp.int32),
            scalars((slots, 4), jnp.int32),
            scalars((1, partners), jnp.int32),
        ]
        + [piece] * devices,
        in_specs=[SMEM] * 5 + [VMEM] * 3,
        out_specs=[SMEM] * 3 + [VMEM] * devices,
        scratch_shapes=[pltpu.SMEM((slots,), jnp.int32)],
        name="transform",
    )(
        place,
        slot_tile_ids,
        neighbour_tile_ids,
        neighbour_rotation_code,
        paired_tile_ids,
        field,
        cell_table(),
        time_table(devices, samples),
    )
    near_slots, codes, partner_slots = map(near_scalars, (near_slots, codes, partner_slots))
    pieces = [pieces[0]] + [
        lax.ppermute(piece, ("freq", "field"), list(enumerate(route)))
        for piece, route in zip(pieces[1:], band_routes)
    ]

    rim_map = pl.pallas_call(
        rim_map_kernel,
        out_shape=kept((LANES, slots * LANES), jnp.bfloat16),
        in_specs=[SMEM] * 3,
        out_specs=VMEM,
        scratch_shapes=[pltpu.VMEM((LANES, slots * LANES), jnp.float32)],
        name="rim_map",
    )(tile, near_slots, codes)

    *sent, height = pl.pallas_call(
        functools.partial(collect_kernel, band_routes, tile_routes),
        out_shape=[kept((5 * total // 2, LANES), jnp.bfloat16)] * arrivals + [kept((total, LANES), jnp.bfloat16)],
        in_specs=[SMEM] * 2 + [VMEM] * (1 + devices),
        out_specs=[VMEM] * (arrivals + 1),
        scratch_shapes=[pltpu.VMEM((4 * total, LANES), jnp.bfloat16)],
        name="collect",
    )(place, tile, *map(near, (rim_map, *pieces)))

    velocity_map, rim_map, chosen = pl.pallas_call(
        functools.partial(partner_map_kernel, tile_routes),
        out_shape=[
            kept((arrivals * LANES, partners * LANES), jnp.bfloat16),
            kept((arrivals * LANES, (1 + partners) * LANES), jnp.bfloat16),
            kept((arrivals + -arrivals % 8, partners * LANES), jnp.float32),
        ],
        in_specs=[SMEM] * 4,
        out_specs=[VMEM] * 3,
        scratch_shapes=[
            pltpu.SMEM((slots,), jnp.int32),
            pltpu.VMEM((arrivals * LANES, partners * LANES), jnp.float32),
            pltpu.VMEM((arrivals * LANES, (1 + partners) * LANES), jnp.float32),
        ],
        name="partner_map",
    )(tile, near_slots, codes, partner_slots)

    bands = [sent[0]]
    for band, route in zip(sent[1:], tile_routes):
        pairs = []
        for sender, receiver in enumerate(route):
            for core in range(field_count):
                there = receiver * field_count + (core if receiver != sender else field_count - 1 - core)
                pairs.append((sender * field_count + core, there))
        bands.append(lax.ppermute(band, ("tiles", "field"), pairs))

    segments = freqs * samples // SEGLEN
    scale = 1.0 / (segments * SEGLEN * 0.375)
    blocks = partners * 2 * per_band
    density = pl.pallas_call(
        functools.partial(density_kernel, arrivals, partners, scale, per_band),
        out_shape=jax.ShapeDtypeStruct((blocks * LANES, LANES), jnp.float32),
        in_specs=[VMEM] * (4 + arrivals),
        out_specs=pl.BlockSpec(memory_space=pl.ANY),
        scratch_shapes=[
            pltpu.VMEM((blocks * LANES, LANES), jnp.float32),
            pltpu.SemaphoreType.DMA((blocks,)),
        ],
        name="density",
    )(*map(near, (height, velocity_map, rim_map, chosen, *bands)))
    return density.reshape(1, partners, 2, per_band, LANES, LANES)


def solution(mesh):
    placed = (P("field", "tiles", ("groups", "freq"), None), P(), P(), P(), P("tiles", None))
    return jax.shard_map(
        functools.partial(shards, mesh.shape["tiles"], mesh.shape["freq"], mesh.shape["field"]),
        mesh=mesh,
        in_specs=placed,
        out_specs=P(("groups", "tiles"), None, None, ("freq", "field"), None, None),
        check_vma=False,
    )
```

```python
import functools
import math

import jax
import jax.numpy as jnp
import ml_dtypes
import numpy as np
from jax import lax
from jax.experimental import pallas as pl
from jax.experimental.pallas import tpu as pltpu
from jax.sharding import PartitionSpec as P

SIDE = 32
SEGLEN = 64
LANES = 128
BLOCKS = SIDE // 2
CORNER_ROWS = 16
FREQS = SEGLEN // 2

NORTH, EAST, SOUTH, WEST = range(4)
HALF = LANES // 2
RIM_LANES = (0, SIDE // 4, SIDE // 4 + BLOCKS, SIDE // 2 + BLOCKS)
CORNER_LANE = SIDE // 2 + 2 * BLOCKS
HEIGHT_CORNER_LANE = CORNER_LANE + 8
EDGE_CORNERS = ((0, 1), (1, 3), (2, 3), (0, 2))
END_RIMS = (
    ((WEST, 0), (EAST, 0)),
    ((NORTH, 1), (SOUTH, 1)),
    ((WEST, 1), (EAST, 1)),
    ((NORTH, 0), (SOUTH, 0)),
)

BAND_ROUTES = ((1, 3, 0, 2), (3, 2, 1, 0), (2, 0, 3, 1))
TILE_ROUTES = ((1, 3, 2, 0), (2, 1, 0, 3), (3, 0, 1, 2), (0, 2, 3, 1))


def routes_for(count, preferred):
    if len(preferred[0]) == count:
        return preferred
    return tuple(tuple(i ^ step for i in range(count)) for step in range(1, count))


def senders(route):
    return tuple(route.index(i) for i in range(len(route)))


def look_up(table, index, dtype=jnp.int32):
    value = dtype(table[0])
    for i in range(1, len(table)):
        value = jnp.where(index == i, dtype(table[i]), value)
    return value


def split_bf16(values):
    high = values.astype(ml_dtypes.bfloat16)
    low = (values - high.astype(np.float64)).astype(ml_dtypes.bfloat16)
    return high, low


@functools.lru_cache(maxsize=None)
def cell_table():
    cells = SIDE * SIDE

    def at(row, column):
        return row * SIDE + column

    near = np.zeros((cells, cells))
    pool = np.zeros((cells, LANES))
    for row in range(SIDE):
        for column in range(SIDE):
            pool[at(row, column), (row // 2) * (SIDE // 4) + column // 4] = 1
            for down, right in ((1, 0), (-1, 0), (0, 1), (0, -1)):
                if 0 <= row + down < SIDE and 0 <= column + right < SIDE:
                    near[at(row + down, column + right), at(row, column)] = 1
    last = SIDE - 1
    outer = [[at(0, i), at(i, last), at(last, i), at(i, 0)] for i in range(SIDE)]
    inner = [[at(1, i), at(i, last - 1), at(last - 1, i), at(i, 1)] for i in range(SIDE)]
    carried = np.zeros((cells, 4 * BLOCKS))
    sums = np.zeros((cells, 4 * BLOCKS))
    for edge in range(4):
        for i in range(SIDE):
            block = edge * BLOCKS + i // 2
            sums[outer[i][edge], block] += 1
            carried[outer[i][edge], block] += 1
            carried[inner[i][edge], block] += 1
            if i > 0:
                carried[outer[i - 1][edge], block] += 2
            if i < last:
                carried[outer[i + 1][edge], block] += 2
    cell_map = np.concatenate([near @ near @ pool, carried, sums], axis=1)
    return cell_map.astype(ml_dtypes.float8_e4m3fn)


@functools.lru_cache(maxsize=None)
def time_table(bands, samples):
    per_band = FREQS // bands
    segments = samples // SEGLEN
    time = np.arange(SEGLEN)
    frequency = np.arange(FREQS)
    angles = 2.0 * math.pi / SEGLEN * (frequency[:, None] * time[None, :] % SEGLEN)
    window = 0.5 - 0.5 * np.cos(2.0 * math.pi / SEGLEN * time)
    waves = np.stack([window * np.cos(angles), -window * np.sin(angles)]) / 16.0
    table = np.zeros((bands, segments, 2, per_band, segments, SEGLEN))
    for segment in range(segments):
        table[:, segment, :, :, segment, :] = waves.reshape(2, bands, per_band, SEGLEN).transpose(1, 0, 2, 3)
    table = table.reshape(bands * segments * 2 * per_band, samples)
    return np.concatenate(split_bf16(table), axis=0)


def dot(left, right):
    return jnp.dot(left, right, preferred_element_type=jnp.float32)


def transform_kernel(
    routes,
    place_ref,
    ids_ref,
    near_ids_ref,
    codes_ref,
    paired_ref,
    x_ref,
    cells_ref,
    waves_ref,
    near_ref,
    kept_codes_ref,
    partner_ref,
    *rest,
):
    outs, slot_ref = rest[:-1], rest[-1]
    place = place_ref[0]
    devices = len(outs)
    count = waves_ref.shape[0] // 2
    rows = count // devices
    x = x_ref[...]
    sums = dot(x, cells_ref[...].astype(jnp.bfloat16))
    bands = [place] + [look_up(route, place) for route in routes]
    starts = [pl.multiple_of(band * rows, rows) for band in bands]
    high = jnp.concatenate([waves_ref[pl.ds(start, rows), :] for start in starts], axis=0)
    low = jnp.concatenate([waves_ref[pl.ds(count + start, rows), :] for start in starts], axis=0)
    across = (((1,), (1,)), ((), ()))
    row = lax.broadcasted_iota(jnp.int32, (CORNER_ROWS, LANES), 0)
    lane = lax.broadcasted_iota(jnp.int32, (CORNER_ROWS, LANES), 1)
    first = ((row == 0) & (lane == 0)) | ((row == 1) & (lane == SIDE - 1))
    last = ((row == 2) & (lane == LANES - SIDE)) | ((row == 3) & (lane == LANES - 1))
    first, last = (jnp.where(hit, 1.0, 0.0).astype(jnp.bfloat16) for hit in (first, last))
    corners = lax.dot_general(first, x[:, :LANES], across, preferred_element_type=jnp.float32)
    corners += lax.dot_general(
        last, x[:, SIDE * SIDE - LANES :], across, preferred_element_type=jnp.float32
    )
    corners = corners.astype(jnp.bfloat16)
    corner_spectra = lax.dot_general(corners, high, across, preferred_element_type=jnp.float32)
    corner_spectra += lax.dot_general(corners, low, across, preferred_element_type=jnp.float32)
    sums_high = sums.astype(jnp.bfloat16)
    sums_low = (sums - sums_high.astype(jnp.float32)).astype(jnp.bfloat16)
    spectra = dot(
        jnp.concatenate([high, high, low], axis=1), jnp.concatenate([sums_high, sums_low, sums_high], axis=0)
    )
    spectra = spectra.astype(jnp.bfloat16)
    lane_start = (place % 2) * (LANES // 2) + (place // 2) * rows
    lane = lax.broadcasted_iota(jnp.int32, (CORNER_ROWS, LANES), 1)
    mine = (lane >= lane_start) & (lane < lane_start + rows)
    for step in range(devices):
        block = spectra[step * rows : (step + 1) * rows]
        outs[step][0:rows, :] = block[:, :LANES]
        outs[step][rows : 2 * rows, :] = block[:, LANES:]
        turned = pltpu.roll(corner_spectra, lax.rem(lane_start - step * rows + LANES, LANES), 1)
        outs[step][2 * rows : 2 * rows + CORNER_ROWS, :] = jnp.where(mine, turned, 0.0).astype(jnp.bfloat16)
    fill_slots(ids_ref, near_ids_ref, codes_ref, slot_ref, near_ref, kept_codes_ref)
    for partner in range(paired_ref.shape[1]):
        partner_ref[0, partner] = slot_ref[paired_ref[0, partner]]


def collect_kernel(band_routes, tile_routes, place_ref, tile_ref, rim_map_ref, *rest):
    devices, arrivals = len(band_routes) + 1, len(tile_routes) + 1
    blocks, rest = rest[:devices], rest[devices:]
    bands, (height_ref, held_ref) = rest[:arrivals], rest[arrivals:]
    place = place_ref[0]
    rows = (blocks[0].shape[0] - CORNER_ROWS) // 2
    total = height_ref.shape[0]
    corners = jnp.zeros((CORNER_ROWS, LANES), jnp.float32)
    for step in range(devices):
        source = look_up(senders(band_routes[step - 1]), place) if step else place
        field, half = source % 2, source // 2
        start = pl.multiple_of(field * total + half * rows, rows)
        held_ref[pl.ds(start, rows), :] = blocks[step][0:rows, :]
        held_ref[pl.ds(2 * total + start, rows), :] = blocks[step][rows : 2 * rows, :]
        corners += blocks[step][2 * rows :, :].astype(jnp.float32)
    height_ref[...] = held_ref[0:total, :]
    row = lax.broadcasted_iota(jnp.int32, (CORNER_ROWS, 2 * LANES), 0)
    lane = lax.broadcasted_iota(jnp.int32, (CORNER_ROWS, 2 * LANES), 1)
    first = jnp.where(lane < LANES, HEIGHT_CORNER_LANE, CORNER_LANE)
    spread = jnp.where((lane % HALF == row + first) & (row < 4), 1.0, 0.0).astype(jnp.bfloat16)
    corners = lax.dot_general(
        corners.astype(jnp.bfloat16), spread, (((0,), (0,)), ((), ())), preferred_element_type=jnp.float32
    )
    corners = corners[:total, :LANES] + corners[total:, LANES:]
    lane = lax.broadcasted_iota(jnp.int32, (total // 2, LANES), 1)
    rims = held_ref[2 * total : 3 * total, :]
    for step in range(arrivals):
        bands[step][0:total, :] = held_ref[total : 2 * total, :]
        bands[step][total : 2 * total, :] = held_ref[3 * total : 4 * total, :]
        receiver = look_up(tile_routes[step - 1], tile_ref[0]) if step else tile_ref[0]
        columns = pl.ds(pl.multiple_of(receiver * LANES, LANES), LANES)
        part = dot(rims, rim_map_ref[:, columns]) + corners
        packed = jnp.where(lane < HALF, part[: total // 2], part[total // 2 :])
        bands[step][2 * total :, :] = packed.astype(jnp.bfloat16)


def rim_lane(edge, position):
    return RIM_LANES[edge] + (position // 2 if edge in (NORTH, SOUTH) else position)


def rim_cell(edge, position):
    across = SIDE // 4
    if edge == NORTH:
        return position
    if edge == EAST:
        return position * across + across - 1
    if edge == SOUTH:
        return LANES - across + position
    return position * across


def turn(position, reverse):
    return position + reverse * (BLOCKS - 1 - 2 * position)


def fill_slots(ids_ref, near_ids_ref, codes_ref, slot_ref, near_ref, kept_codes_ref):
    slots = ids_ref.shape[0]

    def invert(slot, carry):
        slot_ref[ids_ref[slot]] = slot
        return carry

    def find(slot, carry):
        for edge in range(4):
            near_ref[slot, edge] = slot_ref[near_ids_ref[slot, edge]]
            kept_codes_ref[slot, edge] = codes_ref[slot, edge]
        return carry

    lax.fori_loop(0, slots, invert, 0, unroll=slots <= 8)
    lax.fori_loop(0, slots, find, 0, unroll=slots <= 8)


def edge_terms(slot, edge, near_ref, codes_ref):
    near = near_ref[slot, edge]
    code = codes_ref[slot, edge]
    touching, reverse = code % 4, code // 4
    beyond_code = codes_ref[near, touching]
    carried = (near, touching, reverse)
    summed = (near_ref[near, touching], beyond_code % 4, jnp.bitwise_xor(reverse, beyond_code // 4))
    ends = []
    for end in range(2):
        rim_edge = look_up([END_RIMS[option][end][0] for option in range(4)], touching)
        rim_end = look_up([END_RIMS[option][end][1] for option in range(4)], touching)
        other_code = codes_ref[near, rim_edge]
        other_end = jnp.bitwise_xor(rim_end, other_code // 4)
        corner = look_up([EDGE_CORNERS[i // 2][i % 2] for i in range(8)], other_code % 4 * 2 + other_end)
        ends.append((near_ref[near, rim_edge], corner, turn((BLOCKS - 1) * end, reverse)))
    return carried, summed, ends


def rim_map_kernel(tile_ref, near_ref, codes_ref, rim_map_ref, wide_ref):
    tile = tile_ref[0]
    wide_ref[...] = jnp.zeros_like(wide_ref)
    block = lax.broadcasted_iota(jnp.int32, (BLOCKS, LANES), 0)
    lane = lax.broadcasted_iota(jnp.int32, (BLOCKS, LANES), 1) % HALF

    def fill(slot, carry):
        columns = pl.ds(pl.multiple_of(slot * LANES, LANES), LANES)
        for edge in range(4):
            carried, summed, _ = edge_terms(slot, edge, near_ref, codes_ref)
            for base, (source, source_edge, reverse) in ((0, carried), (4 * BLOCKS, summed)):
                hit = (lane == rim_lane(edge, turn(block, reverse))) & (source == tile)
                start = pl.multiple_of(base + source_edge * BLOCKS, BLOCKS)
                wide_ref[pl.ds(start, BLOCKS), columns] += hit.astype(jnp.float32)
        return carry

    slots = near_ref.shape[0]
    lax.fori_loop(0, slots, fill, 0, unroll=slots <= 8)
    rim_map_ref[...] = wide_ref[...].astype(jnp.bfloat16)


def partner_map_kernel(
    routes,
    tile_ref,
    near_ref,
    codes_ref,
    partner_ref,
    velocity_map_ref,
    rim_map_ref,
    chosen_ref,
    arrival_ref,
    wide_ref,
    rim_ref,
):
    tile = tile_ref[0]
    row = lax.broadcasted_iota(jnp.int32, (LANES, LANES), 0) % HALF
    cell = lax.broadcasted_iota(jnp.int32, (LANES, LANES), 1)
    placed = jnp.zeros((LANES, LANES), jnp.bool_)
    for edge in range(4):
        count = SIDE // 4 if edge in (NORTH, SOUTH) else BLOCKS
        position = row - RIM_LANES[edge]
        placed |= (position >= 0) & (position < count) & (cell == rim_cell(edge, position))
    placed = placed.astype(jnp.float32)
    wide_ref[...] = jnp.zeros_like(wide_ref)
    rim_ref[...] = jnp.zeros_like(rim_ref)
    rim_ref[0:LANES, 0:LANES] = placed
    for step, route in enumerate(routes):
        sent = look_up([float(receiver != sender) for sender, receiver in enumerate(route)], tile, jnp.float32)
        rim_ref[(step + 1) * LANES : (step + 2) * LANES, 0:LANES] = placed * sent
    for sender in range(len(routes[0])):
        steps = [0] * len(routes[0])
        for step, route in enumerate(routes):
            if route[sender] != sender:
                steps[route[sender]] = step + 1
        arrival_ref[sender] = look_up(steps, tile)
    block = lax.broadcasted_iota(jnp.int32, (BLOCKS, LANES), 0)
    cell = lax.broadcasted_iota(jnp.int32, (BLOCKS, LANES), 1)
    corner_row = lax.broadcasted_iota(jnp.int32, (8, LANES), 0)
    corner_cell = lax.broadcasted_iota(jnp.int32, (8, LANES), 1)
    step = lax.broadcasted_iota(jnp.int32, (chosen_ref.shape[0], LANES), 0)

    def target(edge, position):
        return rim_cell(edge, position // 2 if edge in (NORTH, SOUTH) else position)

    def add_corners(ends, edge, first_lane, columns):
        for source, corner, position in ends:
            hit = (corner_row == corner) & (corner_cell == target(edge, position))
            for base in (first_lane, HALF + first_lane):
                start = pl.multiple_of(arrival_ref[source] * LANES + base, 8)
                rim_ref[pl.ds(start, 8), columns] += hit.astype(jnp.float32)

    for edge in range(4):
        _, _, ends = edge_terms(tile, edge, near_ref, codes_ref)
        add_corners(ends, edge, HEIGHT_CORNER_LANE, slice(0, LANES))
    for partner in range(partner_ref.shape[1]):
        slot = partner_ref[0, partner]
        columns = slice(partner * LANES, (partner + 1) * LANES)
        rim_columns = slice((partner + 1) * LANES, (partner + 2) * LANES)
        chosen_ref[:, columns] = (step == arrival_ref[slot]).astype(jnp.float32)
        for edge in range(4):
            carried, summed, ends = edge_terms(slot, edge, near_ref, codes_ref)
            for base, (source, source_edge, reverse) in ((0, carried), (4 * BLOCKS, summed)):
                hit = cell == target(edge, turn(block, reverse))
                start = pl.multiple_of(arrival_ref[source] * LANES + base + source_edge * BLOCKS, BLOCKS)
                wide_ref[pl.ds(start, BLOCKS), columns] += hit.astype(jnp.float32)
            add_corners(ends, edge, CORNER_LANE, rim_columns)
    velocity_map_ref[...] = wide_ref[...].astype(jnp.bfloat16)
    rim_map_ref[...] = rim_ref[...].astype(jnp.bfloat16)


def add_arrivals(height, velocity, first, bands, velocity_map_ref, rim_map_ref, chosen_ref):
    total = height.shape[0]
    partners = velocity.shape[1] // LANES
    rows = slice(first * LANES, (first + len(bands)) * LANES)
    rims = jnp.concatenate([band[2 * total :, :] for band in bands], axis=1)
    first_half = lax.broadcasted_iota(jnp.int32, rims.shape, 1) % LANES < HALF
    rims = rims.astype(jnp.float32)
    rims = jnp.concatenate([jnp.where(first_half, rims, 0.0), jnp.where(first_half, 0.0, rims)], axis=0)
    rims = dot(rims.astype(jnp.bfloat16), rim_map_ref[rows, :])
    pairs = jnp.concatenate([band[total : 2 * total, :] for band in bands], axis=1)
    velocity = velocity + dot(pairs, velocity_map_ref[rows, :]) + rims[:, LANES:]
    for step, band in enumerate(bands):
        own = band[0:total, :].astype(jnp.float32)
        chosen = chosen_ref[first + step : first + step + 1, :]
        velocity += jnp.concatenate([own] * partners, axis=1) * chosen
    return height + rims[:, :LANES], velocity


def early_kernel(height_ref, velocity_map_ref, rim_map_ref, chosen_ref, *rest):
    bands, (height_sum_ref, velocity_sum_ref) = rest[:-2], rest[-2:]
    height = height_ref[...].astype(jnp.float32)
    velocity = jnp.zeros(velocity_sum_ref.shape, jnp.float32)
    height, velocity = add_arrivals(height, velocity, 0, bands, velocity_map_ref, rim_map_ref, chosen_ref)
    height_sum_ref[...] = height
    velocity_sum_ref[...] = velocity


def density_kernel(
    early, partners, scale, per_band, height_ref, velocity_ref, velocity_map_ref, rim_map_ref, chosen_ref, *rest
):
    bands, (out_ref, cross_ref, sent) = rest[:-3], rest[-3:]
    total = height_ref.shape[0]
    height, velocity = add_arrivals(
        height_ref[...], velocity_ref[...], early, bands, velocity_map_ref, rim_map_ref, chosen_ref
    )
    velocity = velocity.astype(jnp.bfloat16)
    height = height.astype(jnp.bfloat16).astype(jnp.float32)
    row = lax.broadcasted_iota(jnp.int32, height.shape, 0)
    rotated = jnp.where(
        (row // per_band) % 2 == 0,
        pltpu.roll(height, total - per_band, 0),
        -pltpu.roll(height, per_band, 0),
    )
    turned = jnp.concatenate([height.T, rotated.T], axis=0)
    lane = lax.broadcasted_iota(jnp.int32, turned.shape, 1)
    copies = []
    for frequency in range(per_band):
        left = jnp.where(lane % per_band == frequency, turned, 0.0).astype(jnp.bfloat16)
        cross = dot(left, velocity) * scale
        for partner in range(partners):
            for part in range(2):
                index = (partner * 2 + part) * per_band + frequency
                rows = pl.ds(index * LANES, LANES)
                cross_ref[rows, :] = cross[
                    part * LANES : (part + 1) * LANES, partner * LANES : (partner + 1) * LANES
                ]
                copies.append(pltpu.make_async_copy(cross_ref.at[rows], out_ref.at[rows], sent.at[index]))
                copies[-1].start()
    for copy in copies:
        copy.wait()


SMEM = pl.BlockSpec(memory_space=pltpu.SMEM)
VMEM = pl.BlockSpec(memory_space=pltpu.VMEM)


def kept(shape, dtype):
    return pltpu.VMEM(shape, dtype)


def scalars(shape, dtype):
    return pltpu.SMEM(shape, dtype)


def near_scalars(value):
    return pltpu.with_memory_space_constraint(value, pltpu.SMEM)


def near(value):
    return pltpu.with_memory_space_constraint(value, pltpu.VMEM)


def shards(tiles, freqs, field_count, fields, slot_tile_ids, neighbour_tile_ids, neighbour_rotation_code, paired_tile_ids):
    field = fields.reshape(fields.shape[2], fields.shape[3])
    samples = field.shape[0]
    devices = freqs * field_count
    per_band = FREQS // devices
    rows = samples // SEGLEN * 2 * per_band
    total = freqs * rows
    partners = paired_tile_ids.shape[1]
    tile = lax.axis_index("tiles").astype(jnp.int32).reshape(1)
    place = (lax.axis_index("freq") * field_count + lax.axis_index("field")).astype(jnp.int32).reshape(1)

    band_routes = routes_for(devices, BAND_ROUTES)
    tile_routes = routes_for(tiles, TILE_ROUTES)
    arrivals = len(tile_routes) + 1

    piece = kept((2 * rows + CORNER_ROWS, LANES), jnp.bfloat16)
    slots = slot_tile_ids.shape[0]
    near_slots, codes, partner_slots, *pieces = pl.pallas_call(
        functools.partial(transform_kernel, band_routes),
        out_shape=[
            scalars((slots, 4), jnp.int32),
            scalars((slots, 4), jnp.int32),
            scalars((1, partners), jnp.int32),
        ]
        + [piece] * devices,
        in_specs=[SMEM] * 5 + [VMEM] * 3,
        out_specs=[SMEM] * 3 + [VMEM] * devices,
        scratch_shapes=[pltpu.SMEM((slots,), jnp.int32)],
        name="transform",
    )(
        place,
        slot_tile_ids,
        neighbour_tile_ids,
        neighbour_rotation_code,
        paired_tile_ids,
        field,
        cell_table(),
        time_table(devices, samples),
    )
    near_slots, codes, partner_slots = map(near_scalars, (near_slots, codes, partner_slots))
    pieces = [pieces[0]] + [
        lax.ppermute(piece, ("freq", "field"), list(enumerate(route)))
        for piece, route in zip(pieces[1:], band_routes)
    ]

    rim_map = pl.pallas_call(
        rim_map_kernel,
        out_shape=kept((LANES, slots * LANES), jnp.bfloat16),
        in_specs=[SMEM] * 3,
        out_specs=VMEM,
        scratch_shapes=[pltpu.VMEM((LANES, slots * LANES), jnp.float32)],
        name="rim_map",
    )(tile, near_slots, codes)

    *sent, height = pl.pallas_call(
        functools.partial(collect_kernel, band_routes, tile_routes),
        out_shape=[kept((5 * total // 2, LANES), jnp.bfloat16)] * arrivals + [kept((total, LANES), jnp.bfloat16)],
        in_specs=[SMEM] * 2 + [VMEM] * (1 + devices),
        out_specs=[VMEM] * (arrivals + 1),
        scratch_shapes=[pltpu.VMEM((4 * total, LANES), jnp.bfloat16)],
        name="collect",
    )(place, tile, *map(near, (rim_map, *pieces)))

    velocity_map, rim_map, chosen = pl.pallas_call(
        functools.partial(partner_map_kernel, tile_routes),
        out_shape=[
            kept((arrivals * LANES, partners * LANES), jnp.bfloat16),
            kept((arrivals * LANES, (1 + partners) * LANES), jnp.bfloat16),
            kept((arrivals + -arrivals % 8, partners * LANES), jnp.float32),
        ],
        in_specs=[SMEM] * 4,
        out_specs=[VMEM] * 3,
        scratch_shapes=[
            pltpu.SMEM((slots,), jnp.int32),
            pltpu.VMEM((arrivals * LANES, partners * LANES), jnp.float32),
            pltpu.VMEM((arrivals * LANES, (1 + partners) * LANES), jnp.float32),
        ],
        name="partner_map",
    )(tile, near_slots, codes, partner_slots)

    bands = [sent[0]]
    for band, route in zip(sent[1:], tile_routes):
        pairs = []
        for sender, receiver in enumerate(route):
            for core in range(field_count):
                there = receiver * field_count + (core if receiver != sender else field_count - 1 - core)
                pairs.append((sender * field_count + core, there))
        bands.append(lax.ppermute(band, ("tiles", "field"), pairs))

    early = arrivals - 2
    height, velocity = pl.pallas_call(
        early_kernel,
        out_shape=[kept((total, LANES), jnp.float32), kept((total, partners * LANES), jnp.float32)],
        in_specs=[VMEM] * (4 + early),
        out_specs=[VMEM] * 2,
        name="early",
    )(*map(near, (height, velocity_map, rim_map, chosen, *bands[:early])))

    segments = freqs * samples // SEGLEN
    scale = 1.0 / (segments * SEGLEN * 0.375)
    blocks = partners * 2 * per_band
    density = pl.pallas_call(
        functools.partial(density_kernel, early, partners, scale, per_band),
        out_shape=jax.ShapeDtypeStruct((blocks * LANES, LANES), jnp.float32),
        in_specs=[VMEM] * (5 + arrivals - early),
        out_specs=pl.BlockSpec(memory_space=pl.ANY),
        scratch_shapes=[
            pltpu.VMEM((blocks * LANES, LANES), jnp.float32),
            pltpu.SemaphoreType.DMA((blocks,)),
        ],
        name="density",
    )(*map(near, (height, velocity, velocity_map, rim_map, chosen, *bands[early:])))
    return density.reshape(1, partners, 2, per_band, LANES, LANES)


def solution(mesh):
    placed = (P("field", "tiles", ("groups", "freq"), None), P(), P(), P(), P("tiles", None))
    return jax.shard_map(
        functools.partial(shards, mesh.shape["tiles"], mesh.shape["freq"], mesh.shape["field"]),
        mesh=mesh,
        in_specs=placed,
        out_specs=P(("groups", "tiles"), None, None, ("freq", "field"), None, None),
        check_vma=False,
    )
```

```python
import functools
import math

import jax
import jax.numpy as jnp
import ml_dtypes
import numpy as np
from jax import lax
from jax.experimental import pallas as pl
from jax.experimental.pallas import tpu as pltpu
from jax.sharding import PartitionSpec as P

SIDE = 32
SEGLEN = 64
LANES = 128
BLOCKS = SIDE // 2
CORNER_ROWS = 16
FREQS = SEGLEN // 2

NORTH, EAST, SOUTH, WEST = range(4)
HALF = LANES // 2
RIM_LANES = (0, SIDE // 4, SIDE // 4 + BLOCKS, SIDE // 2 + BLOCKS)
CORNER_LANE = SIDE // 2 + 2 * BLOCKS
HEIGHT_CORNER_LANE = CORNER_LANE + 8
EDGE_CORNERS = ((0, 1), (1, 3), (2, 3), (0, 2))
END_RIMS = (
    ((WEST, 0), (EAST, 0)),
    ((NORTH, 1), (SOUTH, 1)),
    ((WEST, 1), (EAST, 1)),
    ((NORTH, 0), (SOUTH, 0)),
)

BAND_ROUTES = ((2, 3, 0, 1), (3, 2, 1, 0), (1, 0, 3, 2))
TILE_ROUTES = ((1, 3, 2, 0), (2, 1, 0, 3), (3, 0, 1, 2), (0, 2, 3, 1))


def routes_for(count, preferred):
    if len(preferred[0]) == count:
        return preferred
    return tuple(tuple(i ^ step for i in range(count)) for step in range(1, count))


def senders(route):
    return tuple(route.index(i) for i in range(len(route)))


def look_up(table, index, dtype=jnp.int32):
    value = dtype(table[0])
    for i in range(1, len(table)):
        value = jnp.where(index == i, dtype(table[i]), value)
    return value


def split_bf16(values):
    high = values.astype(ml_dtypes.bfloat16)
    low = (values - high.astype(np.float64)).astype(ml_dtypes.bfloat16)
    return high, low


@functools.lru_cache(maxsize=None)
def cell_table():
    cells = SIDE * SIDE

    def at(row, column):
        return row * SIDE + column

    near = np.zeros((cells, cells))
    pool = np.zeros((cells, LANES))
    for row in range(SIDE):
        for column in range(SIDE):
            pool[at(row, column), (row // 2) * (SIDE // 4) + column // 4] = 1
            for down, right in ((1, 0), (-1, 0), (0, 1), (0, -1)):
                if 0 <= row + down < SIDE and 0 <= column + right < SIDE:
                    near[at(row + down, column + right), at(row, column)] = 1
    last = SIDE - 1
    outer = [[at(0, i), at(i, last), at(last, i), at(i, 0)] for i in range(SIDE)]
    inner = [[at(1, i), at(i, last - 1), at(last - 1, i), at(i, 1)] for i in range(SIDE)]
    carried = np.zeros((cells, 4 * BLOCKS))
    sums = np.zeros((cells, 4 * BLOCKS))
    for edge in range(4):
        for i in range(SIDE):
            block = edge * BLOCKS + i // 2
            sums[outer[i][edge], block] += 1
            carried[outer[i][edge], block] += 1
            carried[inner[i][edge], block] += 1
            if i > 0:
                carried[outer[i - 1][edge], block] += 2
            if i < last:
                carried[outer[i + 1][edge], block] += 2
    cell_map = np.concatenate([near @ near @ pool, carried, sums], axis=1)
    return cell_map.astype(ml_dtypes.float8_e4m3fn)


@functools.lru_cache(maxsize=None)
def time_table(bands, samples):
    per_band = FREQS // bands
    segments = samples // SEGLEN
    time = np.arange(SEGLEN)
    frequency = np.arange(FREQS)
    angles = 2.0 * math.pi / SEGLEN * (frequency[:, None] * time[None, :] % SEGLEN)
    window = 0.5 - 0.5 * np.cos(2.0 * math.pi / SEGLEN * time)
    waves = np.stack([window * np.cos(angles), -window * np.sin(angles)]) / 16.0
    table = np.zeros((bands, segments, 2, per_band, segments, SEGLEN))
    for segment in range(segments):
        table[:, segment, :, :, segment, :] = waves.reshape(2, bands, per_band, SEGLEN).transpose(1, 0, 2, 3)
    table = table.reshape(bands * segments * 2 * per_band, samples)
    return np.concatenate(split_bf16(table), axis=0)


def dot(left, right):
    return jnp.dot(left, right, preferred_element_type=jnp.float32)


def transform_kernel(
    routes,
    place_ref,
    ids_ref,
    near_ids_ref,
    codes_ref,
    paired_ref,
    x_ref,
    cells_ref,
    waves_ref,
    near_ref,
    kept_codes_ref,
    partner_ref,
    *rest,
):
    outs, slot_ref = rest[:-1], rest[-1]
    place = place_ref[0]
    devices = len(outs)
    count = waves_ref.shape[0] // 2
    rows = count // devices
    x = x_ref[...]
    sums = dot(x, cells_ref[...].astype(jnp.bfloat16))
    bands = [place] + [look_up(route, place) for route in routes]
    starts = [pl.multiple_of(band * rows, rows) for band in bands]
    high = jnp.concatenate([waves_ref[pl.ds(start, rows), :] for start in starts], axis=0)
    low = jnp.concatenate([waves_ref[pl.ds(count + start, rows), :] for start in starts], axis=0)
    across = (((1,), (1,)), ((), ()))
    row = lax.broadcasted_iota(jnp.int32, (CORNER_ROWS, LANES), 0)
    lane = lax.broadcasted_iota(jnp.int32, (CORNER_ROWS, LANES), 1)
    first = ((row == 0) & (lane == 0)) | ((row == 1) & (lane == SIDE - 1))
    last = ((row == 2) & (lane == LANES - SIDE)) | ((row == 3) & (lane == LANES - 1))
    first, last = (jnp.where(hit, 1.0, 0.0).astype(jnp.bfloat16) for hit in (first, last))
    corners = lax.dot_general(first, x[:, :LANES], across, preferred_element_type=jnp.float32)
    corners += lax.dot_general(
        last, x[:, SIDE * SIDE - LANES :], across, preferred_element_type=jnp.float32
    )
    corners = corners.astype(jnp.bfloat16)
    corner_spectra = lax.dot_general(corners, high, across, preferred_element_type=jnp.float32)
    corner_spectra += lax.dot_general(corners, low, across, preferred_element_type=jnp.float32)
    sums_high = sums.astype(jnp.bfloat16)
    sums_low = (sums - sums_high.astype(jnp.float32)).astype(jnp.bfloat16)
    spectra = dot(
        jnp.concatenate([high, high, low], axis=1), jnp.concatenate([sums_high, sums_low, sums_high], axis=0)
    )
    spectra = spectra.astype(jnp.bfloat16)
    lane_start = (place % 2) * (LANES // 2) + (place // 2) * rows
    lane = lax.broadcasted_iota(jnp.int32, (CORNER_ROWS, LANES), 1)
    mine = (lane >= lane_start) & (lane < lane_start + rows)
    for step in range(devices):
        block = spectra[step * rows : (step + 1) * rows]
        outs[step][0:rows, :] = block[:, :LANES]
        outs[step][rows : 2 * rows, :] = block[:, LANES:]
        turned = pltpu.roll(corner_spectra, lax.rem(lane_start - step * rows + LANES, LANES), 1)
        outs[step][2 * rows : 2 * rows + CORNER_ROWS, :] = jnp.where(mine, turned, 0.0).astype(jnp.bfloat16)
    fill_slots(ids_ref, near_ids_ref, codes_ref, slot_ref, near_ref, kept_codes_ref)
    for partner in range(paired_ref.shape[1]):
        partner_ref[0, partner] = slot_ref[paired_ref[0, partner]]


def collect_kernel(band_routes, tile_routes, place_ref, tile_ref, rim_map_ref, *rest):
    devices, arrivals = len(band_routes) + 1, len(tile_routes) + 1
    blocks, rest = rest[:devices], rest[devices:]
    bands, (height_ref, held_ref) = rest[:arrivals], rest[arrivals:]
    place = place_ref[0]
    rows = (blocks[0].shape[0] - CORNER_ROWS) // 2
    total = height_ref.shape[0]
    corners = jnp.zeros((CORNER_ROWS, LANES), jnp.float32)
    for step in range(devices):
        source = look_up(senders(band_routes[step - 1]), place) if step else place
        field, half = source % 2, source // 2
        start = pl.multiple_of(field * total + half * rows, rows)
        held_ref[pl.ds(start, rows), :] = blocks[step][0:rows, :]
        held_ref[pl.ds(2 * total + start, rows), :] = blocks[step][rows : 2 * rows, :]
        corners += blocks[step][2 * rows :, :].astype(jnp.float32)
    height_ref[...] = held_ref[0:total, :]
    row = lax.broadcasted_iota(jnp.int32, (CORNER_ROWS, 2 * LANES), 0)
    lane = lax.broadcasted_iota(jnp.int32, (CORNER_ROWS, 2 * LANES), 1)
    first = jnp.where(lane < LANES, HEIGHT_CORNER_LANE, CORNER_LANE)
    spread = jnp.where((lane % HALF == row + first) & (row < 4), 1.0, 0.0).astype(jnp.bfloat16)
    corners = lax.dot_general(
        corners.astype(jnp.bfloat16), spread, (((0,), (0,)), ((), ())), preferred_element_type=jnp.float32
    )
    corners = corners[:total, :LANES] + corners[total:, LANES:]
    lane = lax.broadcasted_iota(jnp.int32, (total // 2, LANES), 1)
    rims = held_ref[2 * total : 3 * total, :]
    for step in range(arrivals):
        bands[step][0:total, :] = held_ref[total : 2 * total, :]
        bands[step][total : 2 * total, :] = held_ref[3 * total : 4 * total, :]
        receiver = look_up(tile_routes[step - 1], tile_ref[0]) if step else tile_ref[0]
        columns = pl.ds(pl.multiple_of(receiver * LANES, LANES), LANES)
        part = dot(rims, rim_map_ref[:, columns]) + corners
        packed = jnp.where(lane < HALF, part[: total // 2], part[total // 2 :])
        bands[step][2 * total :, :] = packed.astype(jnp.bfloat16)


def rim_lane(edge, position):
    return RIM_LANES[edge] + (position // 2 if edge in (NORTH, SOUTH) else position)


def rim_cell(edge, position):
    across = SIDE // 4
    if edge == NORTH:
        return position
    if edge == EAST:
        return position * across + across - 1
    if edge == SOUTH:
        return LANES - across + position
    return position * across


def turn(position, reverse):
    return position + reverse * (BLOCKS - 1 - 2 * position)


def fill_slots(ids_ref, near_ids_ref, codes_ref, slot_ref, near_ref, kept_codes_ref):
    slots = ids_ref.shape[0]

    def invert(slot, carry):
        slot_ref[ids_ref[slot]] = slot
        return carry

    def find(slot, carry):
        for edge in range(4):
            near_ref[slot, edge] = slot_ref[near_ids_ref[slot, edge]]
            kept_codes_ref[slot, edge] = codes_ref[slot, edge]
        return carry

    lax.fori_loop(0, slots, invert, 0, unroll=slots <= 8)
    lax.fori_loop(0, slots, find, 0, unroll=slots <= 8)


def edge_terms(slot, edge, near_ref, codes_ref):
    near = near_ref[slot, edge]
    code = codes_ref[slot, edge]
    touching, reverse = code % 4, code // 4
    beyond_code = codes_ref[near, touching]
    carried = (near, touching, reverse)
    summed = (near_ref[near, touching], beyond_code % 4, jnp.bitwise_xor(reverse, beyond_code // 4))
    ends = []
    for end in range(2):
        rim_edge = look_up([END_RIMS[option][end][0] for option in range(4)], touching)
        rim_end = look_up([END_RIMS[option][end][1] for option in range(4)], touching)
        other_code = codes_ref[near, rim_edge]
        other_end = jnp.bitwise_xor(rim_end, other_code // 4)
        corner = look_up([EDGE_CORNERS[i // 2][i % 2] for i in range(8)], other_code % 4 * 2 + other_end)
        ends.append((near_ref[near, rim_edge], corner, turn((BLOCKS - 1) * end, reverse)))
    return carried, summed, ends


def rim_map_kernel(tile_ref, near_ref, codes_ref, rim_map_ref, wide_ref):
    tile = tile_ref[0]
    wide_ref[...] = jnp.zeros_like(wide_ref)
    block = lax.broadcasted_iota(jnp.int32, (BLOCKS, LANES), 0)
    lane = lax.broadcasted_iota(jnp.int32, (BLOCKS, LANES), 1) % HALF

    def fill(slot, carry):
        columns = pl.ds(pl.multiple_of(slot * LANES, LANES), LANES)
        for edge in range(4):
            carried, summed, _ = edge_terms(slot, edge, near_ref, codes_ref)
            for base, (source, source_edge, reverse) in ((0, carried), (4 * BLOCKS, summed)):
                hit = (lane == rim_lane(edge, turn(block, reverse))) & (source == tile)
                start = pl.multiple_of(base + source_edge * BLOCKS, BLOCKS)
                wide_ref[pl.ds(start, BLOCKS), columns] += hit.astype(jnp.float32)
        return carry

    slots = near_ref.shape[0]
    lax.fori_loop(0, slots, fill, 0, unroll=slots <= 8)
    rim_map_ref[...] = wide_ref[...].astype(jnp.bfloat16)


def partner_map_kernel(
    routes,
    tile_ref,
    near_ref,
    codes_ref,
    partner_ref,
    velocity_map_ref,
    rim_map_ref,
    chosen_ref,
    arrival_ref,
    wide_ref,
    rim_ref,
):
    tile = tile_ref[0]
    row = lax.broadcasted_iota(jnp.int32, (LANES, LANES), 0) % HALF
    cell = lax.broadcasted_iota(jnp.int32, (LANES, LANES), 1)
    placed = jnp.zeros((LANES, LANES), jnp.bool_)
    for edge in range(4):
        count = SIDE // 4 if edge in (NORTH, SOUTH) else BLOCKS
        position = row - RIM_LANES[edge]
        placed |= (position >= 0) & (position < count) & (cell == rim_cell(edge, position))
    placed = placed.astype(jnp.float32)
    wide_ref[...] = jnp.zeros_like(wide_ref)
    rim_ref[...] = jnp.zeros_like(rim_ref)
    rim_ref[0:LANES, 0:LANES] = placed
    for step, route in enumerate(routes):
        sent = look_up([float(receiver != sender) for sender, receiver in enumerate(route)], tile, jnp.float32)
        rim_ref[(step + 1) * LANES : (step + 2) * LANES, 0:LANES] = placed * sent
    for sender in range(len(routes[0])):
        steps = [0] * len(routes[0])
        for step, route in enumerate(routes):
            if route[sender] != sender:
                steps[route[sender]] = step + 1
        arrival_ref[sender] = look_up(steps, tile)
    block = lax.broadcasted_iota(jnp.int32, (BLOCKS, LANES), 0)
    cell = lax.broadcasted_iota(jnp.int32, (BLOCKS, LANES), 1)
    corner_row = lax.broadcasted_iota(jnp.int32, (8, LANES), 0)
    corner_cell = lax.broadcasted_iota(jnp.int32, (8, LANES), 1)
    step = lax.broadcasted_iota(jnp.int32, (chosen_ref.shape[0], LANES), 0)

    def target(edge, position):
        return rim_cell(edge, position // 2 if edge in (NORTH, SOUTH) else position)

    def add_corners(ends, edge, first_lane, columns):
        for source, corner, position in ends:
            hit = (corner_row == corner) & (corner_cell == target(edge, position))
            for base in (first_lane, HALF + first_lane):
                start = pl.multiple_of(arrival_ref[source] * LANES + base, 8)
                rim_ref[pl.ds(start, 8), columns] += hit.astype(jnp.float32)

    for edge in range(4):
        _, _, ends = edge_terms(tile, edge, near_ref, codes_ref)
        add_corners(ends, edge, HEIGHT_CORNER_LANE, slice(0, LANES))
    for partner in range(partner_ref.shape[1]):
        slot = partner_ref[0, partner]
        columns = slice(partner * LANES, (partner + 1) * LANES)
        rim_columns = slice((partner + 1) * LANES, (partner + 2) * LANES)
        chosen_ref[:, columns] = (step == arrival_ref[slot]).astype(jnp.float32)
        for edge in range(4):
            carried, summed, ends = edge_terms(slot, edge, near_ref, codes_ref)
            for base, (source, source_edge, reverse) in ((0, carried), (4 * BLOCKS, summed)):
                hit = cell == target(edge, turn(block, reverse))
                start = pl.multiple_of(arrival_ref[source] * LANES + base + source_edge * BLOCKS, BLOCKS)
                wide_ref[pl.ds(start, BLOCKS), columns] += hit.astype(jnp.float32)
            add_corners(ends, edge, CORNER_LANE, rim_columns)
    velocity_map_ref[...] = wide_ref[...].astype(jnp.bfloat16)
    rim_map_ref[...] = rim_ref[...].astype(jnp.bfloat16)


def add_arrivals(height, velocity, first, bands, velocity_map_ref, rim_map_ref, chosen_ref):
    total = height.shape[0]
    partners = velocity.shape[1] // LANES
    rows = slice(first * LANES, (first + len(bands)) * LANES)
    rims = jnp.concatenate([band[2 * total :, :] for band in bands], axis=1)
    first_half = lax.broadcasted_iota(jnp.int32, rims.shape, 1) % LANES < HALF
    rims = rims.astype(jnp.float32)
    rims = jnp.concatenate([jnp.where(first_half, rims, 0.0), jnp.where(first_half, 0.0, rims)], axis=0)
    rims = dot(rims.astype(jnp.bfloat16), rim_map_ref[rows, :])
    pairs = jnp.concatenate([band[total : 2 * total, :] for band in bands], axis=1)
    velocity = velocity + dot(pairs, velocity_map_ref[rows, :]) + rims[:, LANES:]
    for step, band in enumerate(bands):
        own = band[0:total, :].astype(jnp.float32)
        chosen = chosen_ref[first + step : first + step + 1, :]
        velocity += jnp.concatenate([own] * partners, axis=1) * chosen
    return height + rims[:, :LANES], velocity


def early_kernel(height_ref, velocity_map_ref, rim_map_ref, chosen_ref, *rest):
    bands, (height_sum_ref, velocity_sum_ref) = rest[:-2], rest[-2:]
    height = height_ref[...].astype(jnp.float32)
    velocity = jnp.zeros(velocity_sum_ref.shape, jnp.float32)
    height, velocity = add_arrivals(height, velocity, 0, bands, velocity_map_ref, rim_map_ref, chosen_ref)
    height_sum_ref[...] = height
    velocity_sum_ref[...] = velocity


def density_kernel(
    early, partners, scale, per_band, height_ref, velocity_ref, velocity_map_ref, rim_map_ref, chosen_ref, *rest
):
    bands, (out_ref, cross_ref, sent) = rest[:-3], rest[-3:]
    total = height_ref.shape[0]
    height, velocity = add_arrivals(
        height_ref[...], velocity_ref[...], early, bands, velocity_map_ref, rim_map_ref, chosen_ref
    )
    velocity = velocity.astype(jnp.bfloat16)
    height = height.astype(jnp.bfloat16).astype(jnp.float32)
    row = lax.broadcasted_iota(jnp.int32, height.shape, 0)
    rotated = jnp.where(
        (row // per_band) % 2 == 0,
        pltpu.roll(height, total - per_band, 0),
        -pltpu.roll(height, per_band, 0),
    )
    turned = jnp.concatenate([height.T, rotated.T], axis=0)
    lane = lax.broadcasted_iota(jnp.int32, turned.shape, 1)
    copies = []
    for frequency in range(per_band):
        left = jnp.where(lane % per_band == frequency, turned, 0.0).astype(jnp.bfloat16)
        cross = dot(left, velocity) * scale
        for partner in range(partners):
            for part in range(2):
                index = (partner * 2 + part) * per_band + frequency
                rows = pl.ds(index * LANES, LANES)
                cross_ref[rows, :] = cross[
                    part * LANES : (part + 1) * LANES, partner * LANES : (partner + 1) * LANES
                ]
                copies.append(pltpu.make_async_copy(cross_ref.at[rows], out_ref.at[rows], sent.at[index]))
                copies[-1].start()
    for copy in copies:
        copy.wait()


SMEM = pl.BlockSpec(memory_space=pltpu.SMEM)
VMEM = pl.BlockSpec(memory_space=pltpu.VMEM)


def kept(shape, dtype):
    return pltpu.VMEM(shape, dtype)


def scalars(shape, dtype):
    return pltpu.SMEM(shape, dtype)


def near_scalars(value):
    return pltpu.with_memory_space_constraint(value, pltpu.SMEM)


def near(value):
    return pltpu.with_memory_space_constraint(value, pltpu.VMEM)


def shards(tiles, freqs, field_count, fields, slot_tile_ids, neighbour_tile_ids, neighbour_rotation_code, paired_tile_ids):
    field = fields.reshape(fields.shape[2], fields.shape[3])
    samples = field.shape[0]
    devices = freqs * field_count
    per_band = FREQS // devices
    rows = samples // SEGLEN * 2 * per_band
    total = freqs * rows
    partners = paired_tile_ids.shape[1]
    tile = lax.axis_index("tiles").astype(jnp.int32).reshape(1)
    place = (lax.axis_index("freq") * field_count + lax.axis_index("field")).astype(jnp.int32).reshape(1)

    band_routes = routes_for(devices, BAND_ROUTES)
    tile_routes = routes_for(tiles, TILE_ROUTES)
    arrivals = len(tile_routes) + 1

    piece = kept((2 * rows + CORNER_ROWS, LANES), jnp.bfloat16)
    slots = slot_tile_ids.shape[0]
    near_slots, codes, partner_slots, *pieces = pl.pallas_call(
        functools.partial(transform_kernel, band_routes),
        out_shape=[
            scalars((slots, 4), jnp.int32),
            scalars((slots, 4), jnp.int32),
            scalars((1, partners), jnp.int32),
        ]
        + [piece] * devices,
        in_specs=[SMEM] * 5 + [VMEM] * 3,
        out_specs=[SMEM] * 3 + [VMEM] * devices,
        scratch_shapes=[pltpu.SMEM((slots,), jnp.int32)],
        name="transform",
    )(
        place,
        slot_tile_ids,
        neighbour_tile_ids,
        neighbour_rotation_code,
        paired_tile_ids,
        field,
        cell_table(),
        time_table(devices, samples),
    )
    near_slots, codes, partner_slots = map(near_scalars, (near_slots, codes, partner_slots))
    pieces = [pieces[0]] + [
        lax.ppermute(piece, ("freq", "field"), list(enumerate(route)))
        for piece, route in zip(pieces[1:], band_routes)
    ]

    rim_map = pl.pallas_call(
        rim_map_kernel,
        out_shape=kept((LANES, slots * LANES), jnp.bfloat16),
        in_specs=[SMEM] * 3,
        out_specs=VMEM,
        scratch_shapes=[pltpu.VMEM((LANES, slots * LANES), jnp.float32)],
        name="rim_map",
    )(tile, near_slots, codes)

    *sent, height = pl.pallas_call(
        functools.partial(collect_kernel, band_routes, tile_routes),
        out_shape=[kept((5 * total // 2, LANES), jnp.bfloat16)] * arrivals + [kept((total, LANES), jnp.bfloat16)],
        in_specs=[SMEM] * 2 + [VMEM] * (1 + devices),
        out_specs=[VMEM] * (arrivals + 1),
        scratch_shapes=[pltpu.VMEM((4 * total, LANES), jnp.bfloat16)],
        name="collect",
    )(place, tile, *map(near, (rim_map, *pieces)))

    velocity_map, rim_map, chosen = pl.pallas_call(
        functools.partial(partner_map_kernel, tile_routes),
        out_shape=[
            kept((arrivals * LANES, partners * LANES), jnp.bfloat16),
            kept((arrivals * LANES, (1 + partners) * LANES), jnp.bfloat16),
            kept((arrivals + -arrivals % 8, partners * LANES), jnp.float32),
        ],
        in_specs=[SMEM] * 4,
        out_specs=[VMEM] * 3,
        scratch_shapes=[
            pltpu.SMEM((slots,), jnp.int32),
            pltpu.VMEM((arrivals * LANES, partners * LANES), jnp.float32),
            pltpu.VMEM((arrivals * LANES, (1 + partners) * LANES), jnp.float32),
        ],
        name="partner_map",
    )(tile, near_slots, codes, partner_slots)

    bands = [sent[0]]
    for band, route in zip(sent[1:], tile_routes):
        pairs = []
        for sender, receiver in enumerate(route):
            for core in range(field_count):
                there = receiver * field_count + (core if receiver != sender else field_count - 1 - core)
                pairs.append((sender * field_count + core, there))
        bands.append(lax.ppermute(band, ("tiles", "field"), pairs))

    early = arrivals - 2
    height, velocity = pl.pallas_call(
        early_kernel,
        out_shape=[kept((total, LANES), jnp.float32), kept((total, partners * LANES), jnp.float32)],
        in_specs=[VMEM] * (4 + early),
        out_specs=[VMEM] * 2,
        name="early",
    )(*map(near, (height, velocity_map, rim_map, chosen, *bands[:early])))

    segments = freqs * samples // SEGLEN
    scale = 1.0 / (segments * SEGLEN * 0.375)
    blocks = partners * 2 * per_band
    density = pl.pallas_call(
        functools.partial(density_kernel, early, partners, scale, per_band),
        out_shape=jax.ShapeDtypeStruct((blocks * LANES, LANES), jnp.float32),
        in_specs=[VMEM] * (5 + arrivals - early),
        out_specs=pl.BlockSpec(memory_space=pl.ANY),
        scratch_shapes=[
            pltpu.VMEM((blocks * LANES, LANES), jnp.float32),
            pltpu.SemaphoreType.DMA((blocks,)),
        ],
        name="density",
    )(*map(near, (height, velocity, velocity_map, rim_map, chosen, *bands[early:])))
    return density.reshape(1, partners, 2, per_band, LANES, LANES)


def solution(mesh):
    placed = (P("field", "tiles", ("groups", "freq"), None), P(), P(), P(), P("tiles", None))
    return jax.shard_map(
        functools.partial(shards, mesh.shape["tiles"], mesh.shape["freq"], mesh.shape["field"]),
        mesh=mesh,
        in_specs=placed,
        out_specs=P(("groups", "tiles"), None, None, ("freq", "field"), None, None),
        check_vma=False,
    )
```

```python
import functools
import math

import jax
import jax.numpy as jnp
import ml_dtypes
import numpy as np
from jax import lax
from jax.experimental import pallas as pl
from jax.experimental.pallas import tpu as pltpu
from jax.sharding import PartitionSpec as P

SIDE = 32
SEGLEN = 64
LANES = 128
BLOCKS = SIDE // 2
CORNER_ROWS = 16
FREQS = SEGLEN // 2

NORTH, EAST, SOUTH, WEST = range(4)
HALF = LANES // 2
RIM_LANES = (0, SIDE // 4, SIDE // 4 + BLOCKS, SIDE // 2 + BLOCKS)
CORNER_LANE = SIDE // 2 + 2 * BLOCKS
HEIGHT_CORNER_LANE = CORNER_LANE + 8
EDGE_CORNERS = ((0, 1), (1, 3), (2, 3), (0, 2))
END_RIMS = (
    ((WEST, 0), (EAST, 0)),
    ((NORTH, 1), (SOUTH, 1)),
    ((WEST, 1), (EAST, 1)),
    ((NORTH, 0), (SOUTH, 0)),
)

BAND_ROUTES = ((2, 3, 0, 1), (3, 2, 1, 0), (1, 0, 3, 2))
TILE_ROUTES = ((1, 3, 2, 0), (2, 1, 0, 3), (3, 0, 1, 2), (0, 2, 3, 1))


def routes_for(count, preferred):
    if len(preferred[0]) == count:
        return preferred
    return tuple(tuple(i ^ step for i in range(count)) for step in range(1, count))


def senders(route):
    return tuple(route.index(i) for i in range(len(route)))


def look_up(table, index, dtype=jnp.int32):
    value = dtype(table[0])
    for i in range(1, len(table)):
        value = jnp.where(index == i, dtype(table[i]), value)
    return value


def split_bf16(values):
    high = values.astype(ml_dtypes.bfloat16)
    low = (values - high.astype(np.float64)).astype(ml_dtypes.bfloat16)
    return high, low


@functools.lru_cache(maxsize=None)
def cell_table():
    cells = SIDE * SIDE

    def at(row, column):
        return row * SIDE + column

    near = np.zeros((cells, cells))
    pool = np.zeros((cells, LANES))
    for row in range(SIDE):
        for column in range(SIDE):
            pool[at(row, column), (row // 2) * (SIDE // 4) + column // 4] = 1
            for down, right in ((1, 0), (-1, 0), (0, 1), (0, -1)):
                if 0 <= row + down < SIDE and 0 <= column + right < SIDE:
                    near[at(row + down, column + right), at(row, column)] = 1
    last = SIDE - 1
    outer = [[at(0, i), at(i, last), at(last, i), at(i, 0)] for i in range(SIDE)]
    inner = [[at(1, i), at(i, last - 1), at(last - 1, i), at(i, 1)] for i in range(SIDE)]
    carried = np.zeros((cells, 4 * BLOCKS))
    sums = np.zeros((cells, 4 * BLOCKS))
    for edge in range(4):
        for i in range(SIDE):
            block = edge * BLOCKS + i // 2
            sums[outer[i][edge], block] += 1
            carried[outer[i][edge], block] += 1
            carried[inner[i][edge], block] += 1
            if i > 0:
                carried[outer[i - 1][edge], block] += 2
            if i < last:
                carried[outer[i + 1][edge], block] += 2
    cell_map = np.concatenate([near @ near @ pool, carried, sums], axis=1)
    return cell_map.astype(ml_dtypes.float8_e4m3fn)


@functools.lru_cache(maxsize=None)
def time_table(bands, samples):
    per_band = FREQS // bands
    segments = samples // SEGLEN
    time = np.arange(SEGLEN)
    frequency = np.arange(FREQS)
    angles = 2.0 * math.pi / SEGLEN * (frequency[:, None] * time[None, :] % SEGLEN)
    window = 0.5 - 0.5 * np.cos(2.0 * math.pi / SEGLEN * time)
    waves = np.stack([window * np.cos(angles), -window * np.sin(angles)]) / 16.0
    table = np.zeros((bands, segments, 2, per_band, segments, SEGLEN))
    for segment in range(segments):
        table[:, segment, :, :, segment, :] = waves.reshape(2, bands, per_band, SEGLEN).transpose(1, 0, 2, 3)
    table = table.reshape(bands * segments * 2 * per_band, samples)
    return np.concatenate(split_bf16(table), axis=0)


def dot(left, right):
    return jnp.dot(left, right, preferred_element_type=jnp.float32)


def transform_kernel(
    routes,
    place_ref,
    ids_ref,
    near_ids_ref,
    codes_ref,
    paired_ref,
    x_ref,
    cells_ref,
    waves_ref,
    near_ref,
    kept_codes_ref,
    partner_ref,
    *rest,
):
    outs, slot_ref = rest[:-1], rest[-1]
    place = place_ref[0]
    devices = len(outs)
    count = waves_ref.shape[0] // 2
    rows = count // devices
    x = x_ref[...]
    sums = dot(x, cells_ref[...].astype(jnp.bfloat16))
    bands = [place] + [look_up(route, place) for route in routes]
    starts = [pl.multiple_of(band * rows, rows) for band in bands]
    high = jnp.concatenate([waves_ref[pl.ds(start, rows), :] for start in starts], axis=0)
    low = jnp.concatenate([waves_ref[pl.ds(count + start, rows), :] for start in starts], axis=0)
    across = (((1,), (1,)), ((), ()))
    row = lax.broadcasted_iota(jnp.int32, (CORNER_ROWS, LANES), 0)
    lane = lax.broadcasted_iota(jnp.int32, (CORNER_ROWS, LANES), 1)
    first = ((row == 0) & (lane == 0)) | ((row == 1) & (lane == SIDE - 1))
    last = ((row == 2) & (lane == LANES - SIDE)) | ((row == 3) & (lane == LANES - 1))
    first, last = (jnp.where(hit, 1.0, 0.0).astype(jnp.bfloat16) for hit in (first, last))
    corners = lax.dot_general(first, x[:, :LANES], across, preferred_element_type=jnp.float32)
    corners += lax.dot_general(
        last, x[:, SIDE * SIDE - LANES :], across, preferred_element_type=jnp.float32
    )
    corners = corners.astype(jnp.bfloat16)
    corner_spectra = lax.dot_general(corners, high, across, preferred_element_type=jnp.float32)
    corner_spectra += lax.dot_general(corners, low, across, preferred_element_type=jnp.float32)
    sums_high = sums.astype(jnp.bfloat16)
    sums_low = (sums - sums_high.astype(jnp.float32)).astype(jnp.bfloat16)
    spectra = dot(
        jnp.concatenate([high, high, low], axis=1), jnp.concatenate([sums_high, sums_low, sums_high], axis=0)
    )
    spectra = spectra.astype(jnp.bfloat16)
    lane_start = (place % 2) * (LANES // 2) + (place // 2) * rows
    lane = lax.broadcasted_iota(jnp.int32, (CORNER_ROWS, LANES), 1)
    mine = (lane >= lane_start) & (lane < lane_start + rows)
    for step in range(devices):
        block = spectra[step * rows : (step + 1) * rows]
        outs[step][0:rows, :] = block[:, :LANES]
        outs[step][rows : 2 * rows, :] = block[:, LANES:]
        turned = pltpu.roll(corner_spectra, lax.rem(lane_start - step * rows + LANES, LANES), 1)
        outs[step][2 * rows : 2 * rows + CORNER_ROWS, :] = jnp.where(mine, turned, 0.0).astype(jnp.bfloat16)
    fill_slots(ids_ref, near_ids_ref, codes_ref, slot_ref, near_ref, kept_codes_ref)
    for partner in range(paired_ref.shape[1]):
        partner_ref[0, partner] = slot_ref[paired_ref[0, partner]]


def collect_kernel(band_routes, tile_routes, place_ref, tile_ref, rim_map_ref, *rest):
    devices, arrivals = len(band_routes) + 1, len(tile_routes) + 1
    blocks, rest = rest[:devices], rest[devices:]
    bands, (height_ref, held_ref) = rest[:arrivals], rest[arrivals:]
    place = place_ref[0]
    rows = (blocks[0].shape[0] - CORNER_ROWS) // 2
    total = height_ref.shape[0]
    corners = jnp.zeros((CORNER_ROWS, LANES), jnp.float32)
    for step in range(devices):
        source = look_up(senders(band_routes[step - 1]), place) if step else place
        field, half = source % 2, source // 2
        start = pl.multiple_of(field * total + half * rows, rows)
        held_ref[pl.ds(start, rows), :] = blocks[step][0:rows, :]
        held_ref[pl.ds(2 * total + start, rows), :] = blocks[step][rows : 2 * rows, :]
        corners += blocks[step][2 * rows :, :].astype(jnp.float32)
    height_ref[...] = held_ref[0:total, :]
    row = lax.broadcasted_iota(jnp.int32, (CORNER_ROWS, 2 * LANES), 0)
    lane = lax.broadcasted_iota(jnp.int32, (CORNER_ROWS, 2 * LANES), 1)
    first = jnp.where(lane < LANES, HEIGHT_CORNER_LANE, CORNER_LANE)
    spread = jnp.where((lane % HALF == row + first) & (row < 4), 1.0, 0.0).astype(jnp.bfloat16)
    corners = lax.dot_general(
        corners.astype(jnp.bfloat16), spread, (((0,), (0,)), ((), ())), preferred_element_type=jnp.float32
    )
    corners = corners[:total, :LANES] + corners[total:, LANES:]
    lane = lax.broadcasted_iota(jnp.int32, (total // 2, LANES), 1)
    rims = held_ref[2 * total : 3 * total, :]
    for step in range(arrivals):
        bands[step][0:total, :] = held_ref[total : 2 * total, :]
        bands[step][total : 2 * total, :] = held_ref[3 * total : 4 * total, :]
        receiver = look_up(tile_routes[step - 1], tile_ref[0]) if step else tile_ref[0]
        columns = pl.ds(pl.multiple_of(receiver * LANES, LANES), LANES)
        part = dot(rims, rim_map_ref[:, columns]) + corners
        packed = jnp.where(lane < HALF, part[: total // 2], part[total // 2 :])
        bands[step][2 * total :, :] = packed.astype(jnp.bfloat16)


def rim_lane(edge, position):
    return RIM_LANES[edge] + (position // 2 if edge in (NORTH, SOUTH) else position)


def rim_cell(edge, position):
    across = SIDE // 4
    if edge == NORTH:
        return position
    if edge == EAST:
        return position * across + across - 1
    if edge == SOUTH:
        return LANES - across + position
    return position * across


def turn(position, reverse):
    return position + reverse * (BLOCKS - 1 - 2 * position)


def fill_slots(ids_ref, near_ids_ref, codes_ref, slot_ref, near_ref, kept_codes_ref):
    slots = ids_ref.shape[0]

    def invert(slot, carry):
        slot_ref[ids_ref[slot]] = slot
        return carry

    def find(slot, carry):
        for edge in range(4):
            near_ref[slot, edge] = slot_ref[near_ids_ref[slot, edge]]
            kept_codes_ref[slot, edge] = codes_ref[slot, edge]
        return carry

    lax.fori_loop(0, slots, invert, 0, unroll=slots <= 8)
    lax.fori_loop(0, slots, find, 0, unroll=slots <= 8)


def edge_terms(slot, edge, near_ref, codes_ref):
    near = near_ref[slot, edge]
    code = codes_ref[slot, edge]
    touching, reverse = code % 4, code // 4
    beyond_code = codes_ref[near, touching]
    carried = (near, touching, reverse)
    summed = (near_ref[near, touching], beyond_code % 4, jnp.bitwise_xor(reverse, beyond_code // 4))
    ends = []
    for end in range(2):
        rim_edge = look_up([END_RIMS[option][end][0] for option in range(4)], touching)
        rim_end = look_up([END_RIMS[option][end][1] for option in range(4)], touching)
        other_code = codes_ref[near, rim_edge]
        other_end = jnp.bitwise_xor(rim_end, other_code // 4)
        corner = look_up([EDGE_CORNERS[i // 2][i % 2] for i in range(8)], other_code % 4 * 2 + other_end)
        ends.append((near_ref[near, rim_edge], corner, turn((BLOCKS - 1) * end, reverse)))
    return carried, summed, ends


def rim_map_kernel(tile_ref, near_ref, codes_ref, rim_map_ref, wide_ref):
    tile = tile_ref[0]
    wide_ref[...] = jnp.zeros_like(wide_ref)
    block = lax.broadcasted_iota(jnp.int32, (BLOCKS, LANES), 0)
    lane = lax.broadcasted_iota(jnp.int32, (BLOCKS, LANES), 1) % HALF

    def fill(slot, carry):
        columns = pl.ds(pl.multiple_of(slot * LANES, LANES), LANES)
        for edge in range(4):
            carried, summed, _ = edge_terms(slot, edge, near_ref, codes_ref)
            for base, (source, source_edge, reverse) in ((0, carried), (4 * BLOCKS, summed)):
                hit = (lane == rim_lane(edge, turn(block, reverse))) & (source == tile)
                start = pl.multiple_of(base + source_edge * BLOCKS, BLOCKS)
                wide_ref[pl.ds(start, BLOCKS), columns] += hit.astype(jnp.float32)
        return carry

    slots = near_ref.shape[0]
    lax.fori_loop(0, slots, fill, 0, unroll=slots <= 8)
    rim_map_ref[...] = wide_ref[...].astype(jnp.bfloat16)


def partner_map_kernel(
    routes,
    tile_ref,
    near_ref,
    codes_ref,
    partner_ref,
    velocity_map_ref,
    rim_map_ref,
    chosen_ref,
    arrival_ref,
    wide_ref,
    rim_ref,
):
    tile = tile_ref[0]
    row = lax.broadcasted_iota(jnp.int32, (LANES, LANES), 0) % HALF
    cell = lax.broadcasted_iota(jnp.int32, (LANES, LANES), 1)
    placed = jnp.zeros((LANES, LANES), jnp.bool_)
    for edge in range(4):
        count = SIDE // 4 if edge in (NORTH, SOUTH) else BLOCKS
        position = row - RIM_LANES[edge]
        placed |= (position >= 0) & (position < count) & (cell == rim_cell(edge, position))
    placed = placed.astype(jnp.float32)
    wide_ref[...] = jnp.zeros_like(wide_ref)
    rim_ref[...] = jnp.zeros_like(rim_ref)
    rim_ref[0:LANES, 0:LANES] = placed
    for step, route in enumerate(routes):
        sent = look_up([float(receiver != sender) for sender, receiver in enumerate(route)], tile, jnp.float32)
        rim_ref[(step + 1) * LANES : (step + 2) * LANES, 0:LANES] = placed * sent
    for sender in range(len(routes[0])):
        steps = [0] * len(routes[0])
        for step, route in enumerate(routes):
            if route[sender] != sender:
                steps[route[sender]] = step + 1
        arrival_ref[sender] = look_up(steps, tile)
    block = lax.broadcasted_iota(jnp.int32, (BLOCKS, LANES), 0)
    cell = lax.broadcasted_iota(jnp.int32, (BLOCKS, LANES), 1)
    corner_row = lax.broadcasted_iota(jnp.int32, (8, LANES), 0)
    corner_cell = lax.broadcasted_iota(jnp.int32, (8, LANES), 1)
    step = lax.broadcasted_iota(jnp.int32, (chosen_ref.shape[0], LANES), 0)

    def target(edge, position):
        return rim_cell(edge, position // 2 if edge in (NORTH, SOUTH) else position)

    def add_corners(ends, edge, first_lane, columns):
        for source, corner, position in ends:
            hit = (corner_row == corner) & (corner_cell == target(edge, position))
            for base in (first_lane, HALF + first_lane):
                start = pl.multiple_of(arrival_ref[source] * LANES + base, 8)
                rim_ref[pl.ds(start, 8), columns] += hit.astype(jnp.float32)

    for edge in range(4):
        _, _, ends = edge_terms(tile, edge, near_ref, codes_ref)
        add_corners(ends, edge, HEIGHT_CORNER_LANE, slice(0, LANES))
    for partner in range(partner_ref.shape[1]):
        slot = partner_ref[0, partner]
        columns = slice(partner * LANES, (partner + 1) * LANES)
        rim_columns = slice((partner + 1) * LANES, (partner + 2) * LANES)
        chosen_ref[:, columns] = (step == arrival_ref[slot]).astype(jnp.float32)
        for edge in range(4):
            carried, summed, ends = edge_terms(slot, edge, near_ref, codes_ref)
            for base, (source, source_edge, reverse) in ((0, carried), (4 * BLOCKS, summed)):
                hit = cell == target(edge, turn(block, reverse))
                start = pl.multiple_of(arrival_ref[source] * LANES + base + source_edge * BLOCKS, BLOCKS)
                wide_ref[pl.ds(start, BLOCKS), columns] += hit.astype(jnp.float32)
            add_corners(ends, edge, CORNER_LANE, rim_columns)
    velocity_map_ref[...] = wide_ref[...].astype(jnp.bfloat16)
    rim_map_ref[...] = rim_ref[...].astype(jnp.bfloat16)


def add_arrivals(height, velocity, first, bands, velocity_map_ref, rim_map_ref, chosen_ref):
    total = height.shape[0]
    partners = velocity.shape[1] // LANES
    rows = slice(first * LANES, (first + len(bands)) * LANES)
    rims = jnp.concatenate([band[2 * total :, :] for band in bands], axis=1)
    first_half = lax.broadcasted_iota(jnp.int32, rims.shape, 1) % LANES < HALF
    rims = rims.astype(jnp.float32)
    rims = jnp.concatenate([jnp.where(first_half, rims, 0.0), jnp.where(first_half, 0.0, rims)], axis=0)
    rims = dot(rims.astype(jnp.bfloat16), rim_map_ref[rows, :])
    pairs = jnp.concatenate([band[total : 2 * total, :] for band in bands], axis=1)
    velocity = velocity + dot(pairs, velocity_map_ref[rows, :]) + rims[:, LANES:]
    for step, band in enumerate(bands):
        own = band[0:total, :].astype(jnp.float32)
        chosen = chosen_ref[first + step : first + step + 1, :]
        velocity += jnp.concatenate([own] * partners, axis=1) * chosen
    return height + rims[:, :LANES], velocity


def early_kernel(height_ref, velocity_map_ref, rim_map_ref, chosen_ref, *rest):
    bands, (height_sum_ref, velocity_sum_ref) = rest[:-2], rest[-2:]
    height = height_ref[...].astype(jnp.float32)
    velocity = jnp.zeros(velocity_sum_ref.shape, jnp.float32)
    height, velocity = add_arrivals(height, velocity, 0, bands, velocity_map_ref, rim_map_ref, chosen_ref)
    height_sum_ref[...] = height
    velocity_sum_ref[...] = velocity


def density_kernel(
    early, partners, scale, per_band, height_ref, velocity_ref, velocity_map_ref, rim_map_ref, chosen_ref, *rest
):
    bands, (out_ref, cross_ref, sent) = rest[:-3], rest[-3:]
    total = height_ref.shape[0]
    height, velocity = add_arrivals(
        height_ref[...], velocity_ref[...], early, bands, velocity_map_ref, rim_map_ref, chosen_ref
    )
    velocity = velocity.astype(jnp.bfloat16)
    height = height.astype(jnp.bfloat16).astype(jnp.float32)
    row = lax.broadcasted_iota(jnp.int32, height.shape, 0)
    rotated = jnp.where(
        (row // per_band) % 2 == 0,
        pltpu.roll(height, total - per_band, 0),
        -pltpu.roll(height, per_band, 0),
    )
    turned = jnp.concatenate([height.T, rotated.T], axis=0)
    lane = lax.broadcasted_iota(jnp.int32, turned.shape, 1)
    copies = []
    for frequency in range(per_band):
        left = jnp.where(lane % per_band == frequency, turned, 0.0).astype(jnp.bfloat16)
        cross = dot(left, velocity) * scale
        for partner in range(partners):
            for part in range(2):
                index = (partner * 2 + part) * per_band + frequency
                rows = pl.ds(index * LANES, LANES)
                cross_ref[rows, :] = cross[
                    part * LANES : (part + 1) * LANES, partner * LANES : (partner + 1) * LANES
                ]
                copies.append(pltpu.make_async_copy(cross_ref.at[rows], out_ref.at[rows], sent.at[index]))
                copies[-1].start()
    for copy in copies:
        copy.wait()


SMEM = pl.BlockSpec(memory_space=pltpu.SMEM)
VMEM = pl.BlockSpec(memory_space=pltpu.VMEM)


def kept(shape, dtype):
    return pltpu.VMEM(shape, dtype)


def scalars(shape, dtype):
    return pltpu.SMEM(shape, dtype)


def near_scalars(value):
    return pltpu.with_memory_space_constraint(value, pltpu.SMEM)


def near(value):
    return pltpu.with_memory_space_constraint(value, pltpu.VMEM)


def shards(tiles, freqs, field_count, fields, slot_tile_ids, neighbour_tile_ids, neighbour_rotation_code, paired_tile_ids):
    field = fields.reshape(fields.shape[2], fields.shape[3])
    samples = field.shape[0]
    devices = freqs * field_count
    per_band = FREQS // devices
    rows = samples // SEGLEN * 2 * per_band
    total = freqs * rows
    partners = paired_tile_ids.shape[1]
    tile = lax.axis_index("tiles").astype(jnp.int32).reshape(1)
    place = (lax.axis_index("freq") * field_count + lax.axis_index("field")).astype(jnp.int32).reshape(1)

    band_routes = routes_for(devices, BAND_ROUTES)
    tile_routes = routes_for(tiles, TILE_ROUTES)
    arrivals = len(tile_routes) + 1

    piece = kept((2 * rows + CORNER_ROWS, LANES), jnp.bfloat16)
    slots = slot_tile_ids.shape[0]
    near_slots, codes, partner_slots, *pieces = pl.pallas_call(
        functools.partial(transform_kernel, band_routes),
        out_shape=[
            scalars((slots, 4), jnp.int32),
            scalars((slots, 4), jnp.int32),
            scalars((1, partners), jnp.int32),
        ]
        + [piece] * devices,
        in_specs=[SMEM] * 5 + [VMEM] * 3,
        out_specs=[SMEM] * 3 + [VMEM] * devices,
        scratch_shapes=[pltpu.SMEM((slots,), jnp.int32)],
        name="transform",
    )(
        place,
        slot_tile_ids,
        neighbour_tile_ids,
        neighbour_rotation_code,
        paired_tile_ids,
        field,
        cell_table(),
        time_table(devices, samples),
    )
    near_slots, codes, partner_slots = map(near_scalars, (near_slots, codes, partner_slots))
    pieces = [pieces[0]] + [
        lax.ppermute(piece, ("freq", "field"), list(enumerate(route)))
        for piece, route in zip(pieces[1:], band_routes)
    ]

    rim_map = pl.pallas_call(
        rim_map_kernel,
        out_shape=kept((LANES, slots * LANES), jnp.bfloat16),
        in_specs=[SMEM] * 3,
        out_specs=VMEM,
        scratch_shapes=[pltpu.VMEM((LANES, slots * LANES), jnp.float32)],
        name="rim_map",
    )(tile, near_slots, codes)

    *sent, height = pl.pallas_call(
        functools.partial(collect_kernel, band_routes, tile_routes),
        out_shape=[kept((5 * total // 2, LANES), jnp.bfloat16)] * arrivals + [kept((total, LANES), jnp.bfloat16)],
        in_specs=[SMEM] * 2 + [VMEM] * (1 + devices),
        out_specs=[VMEM] * (arrivals + 1),
        scratch_shapes=[pltpu.VMEM((4 * total, LANES), jnp.bfloat16)],
        name="collect",
    )(place, tile, *map(near, (rim_map, *pieces)))

    velocity_map, rim_map, chosen = pl.pallas_call(
        functools.partial(partner_map_kernel, tile_routes),
        out_shape=[
            kept((arrivals * LANES, partners * LANES), jnp.bfloat16),
            kept((arrivals * LANES, (1 + partners) * LANES), jnp.bfloat16),
            kept((arrivals + -arrivals % 8, partners * LANES), jnp.float32),
        ],
        in_specs=[SMEM] * 4,
        out_specs=[VMEM] * 3,
        scratch_shapes=[
            pltpu.SMEM((slots,), jnp.int32),
            pltpu.VMEM((arrivals * LANES, partners * LANES), jnp.float32),
            pltpu.VMEM((arrivals * LANES, (1 + partners) * LANES), jnp.float32),
        ],
        name="partner_map",
    )(tile, near_slots, codes, partner_slots)

    bands = [sent[0]]
    for band, route in zip(sent[1:], tile_routes):
        pairs = []
        for sender, receiver in enumerate(route):
            for core in range(field_count):
                there = receiver * field_count + (core if receiver != sender else field_count - 1 - core)
                pairs.append((sender * field_count + core, there))
        bands.append(lax.ppermute(band, ("tiles", "field"), pairs))

    early = arrivals - 3
    height, velocity = pl.pallas_call(
        early_kernel,
        out_shape=[kept((total, LANES), jnp.float32), kept((total, partners * LANES), jnp.float32)],
        in_specs=[VMEM] * (4 + early),
        out_specs=[VMEM] * 2,
        name="early",
    )(*map(near, (height, velocity_map, rim_map, chosen, *bands[:early])))

    segments = freqs * samples // SEGLEN
    scale = 1.0 / (segments * SEGLEN * 0.375)
    blocks = partners * 2 * per_band
    density = pl.pallas_call(
        functools.partial(density_kernel, early, partners, scale, per_band),
        out_shape=jax.ShapeDtypeStruct((blocks * LANES, LANES), jnp.float32),
        in_specs=[VMEM] * (5 + arrivals - early),
        out_specs=pl.BlockSpec(memory_space=pl.ANY),
        scratch_shapes=[
            pltpu.VMEM((blocks * LANES, LANES), jnp.float32),
            pltpu.SemaphoreType.DMA((blocks,)),
        ],
        name="density",
    )(*map(near, (height, velocity, velocity_map, rim_map, chosen, *bands[early:])))
    return density.reshape(1, partners, 2, per_band, LANES, LANES)


def solution(mesh):
    placed = (P("field", "tiles", ("groups", "freq"), None), P(), P(), P(), P("tiles", None))
    return jax.shard_map(
        functools.partial(shards, mesh.shape["tiles"], mesh.shape["freq"], mesh.shape["field"]),
        mesh=mesh,
        in_specs=placed,
        out_specs=P(("groups", "tiles"), None, None, ("freq", "field"), None, None),
        check_vma=False,
    )
```

```python
import functools
import math

import jax
import jax.numpy as jnp
import ml_dtypes
import numpy as np
from jax import lax
from jax.experimental import pallas as pl
from jax.experimental.pallas import tpu as pltpu
from jax.sharding import PartitionSpec as P

SIDE = 32
SEGLEN = 64
LANES = 128
BLOCKS = SIDE // 2
CORNER_ROWS = 16
FREQS = SEGLEN // 2

NORTH, EAST, SOUTH, WEST = range(4)
HALF = LANES // 2
RIM_LANES = (0, SIDE // 4, SIDE // 4 + BLOCKS, SIDE // 2 + BLOCKS)
CORNER_LANE = SIDE // 2 + 2 * BLOCKS
HEIGHT_CORNER_LANE = CORNER_LANE + 8
EDGE_CORNERS = ((0, 1), (1, 3), (2, 3), (0, 2))
END_RIMS = (
    ((WEST, 0), (EAST, 0)),
    ((NORTH, 1), (SOUTH, 1)),
    ((WEST, 1), (EAST, 1)),
    ((NORTH, 0), (SOUTH, 0)),
)

BAND_ROUTES = ((3, 2, 1, 0), (2, 3, 0, 1), (1, 0, 3, 2))
TILE_ROUTES = ((1, 3, 2, 0), (2, 1, 0, 3), (3, 0, 1, 2), (0, 2, 3, 1))


def routes_for(count, preferred):
    if len(preferred[0]) == count:
        return preferred
    return tuple(tuple(i ^ step for i in range(count)) for step in range(1, count))


def senders(route):
    return tuple(route.index(i) for i in range(len(route)))


def look_up(table, index, dtype=jnp.int32):
    value = dtype(table[0])
    for i in range(1, len(table)):
        value = jnp.where(index == i, dtype(table[i]), value)
    return value


def split_bf16(values):
    high = values.astype(ml_dtypes.bfloat16)
    low = (values - high.astype(np.float64)).astype(ml_dtypes.bfloat16)
    return high, low


@functools.lru_cache(maxsize=None)
def cell_table():
    cells = SIDE * SIDE

    def at(row, column):
        return row * SIDE + column

    near = np.zeros((cells, cells))
    pool = np.zeros((cells, LANES))
    for row in range(SIDE):
        for column in range(SIDE):
            pool[at(row, column), (row // 2) * (SIDE // 4) + column // 4] = 1
            for down, right in ((1, 0), (-1, 0), (0, 1), (0, -1)):
                if 0 <= row + down < SIDE and 0 <= column + right < SIDE:
                    near[at(row + down, column + right), at(row, column)] = 1
    last = SIDE - 1
    outer = [[at(0, i), at(i, last), at(last, i), at(i, 0)] for i in range(SIDE)]
    inner = [[at(1, i), at(i, last - 1), at(last - 1, i), at(i, 1)] for i in range(SIDE)]
    carried = np.zeros((cells, 4 * BLOCKS))
    sums = np.zeros((cells, 4 * BLOCKS))
    for edge in range(4):
        for i in range(SIDE):
            block = edge * BLOCKS + i // 2
            sums[outer[i][edge], block] += 1
            carried[outer[i][edge], block] += 1
            carried[inner[i][edge], block] += 1
            if i > 0:
                carried[outer[i - 1][edge], block] += 2
            if i < last:
                carried[outer[i + 1][edge], block] += 2
    cell_map = np.concatenate([near @ near @ pool, carried, sums], axis=1)
    return cell_map.astype(ml_dtypes.float8_e4m3fn)


@functools.lru_cache(maxsize=None)
def time_table(bands, samples):
    per_band = FREQS // bands
    segments = samples // SEGLEN
    time = np.arange(SEGLEN)
    frequency = np.arange(FREQS)
    angles = 2.0 * math.pi / SEGLEN * (frequency[:, None] * time[None, :] % SEGLEN)
    window = 0.5 - 0.5 * np.cos(2.0 * math.pi / SEGLEN * time)
    waves = np.stack([window * np.cos(angles), -window * np.sin(angles)]) / 16.0
    table = np.zeros((bands, segments, 2, per_band, segments, SEGLEN))
    for segment in range(segments):
        table[:, segment, :, :, segment, :] = waves.reshape(2, bands, per_band, SEGLEN).transpose(1, 0, 2, 3)
    table = table.reshape(bands * segments * 2 * per_band, samples)
    return np.concatenate(split_bf16(table), axis=0)


def dot(left, right):
    return jnp.dot(left, right, preferred_element_type=jnp.float32)


def transform_kernel(
    routes,
    place_ref,
    ids_ref,
    near_ids_ref,
    codes_ref,
    paired_ref,
    x_ref,
    cells_ref,
    waves_ref,
    near_ref,
    kept_codes_ref,
    partner_ref,
    *rest,
):
    outs, slot_ref = rest[:-1], rest[-1]
    place = place_ref[0]
    devices = len(outs)
    count = waves_ref.shape[0] // 2
    rows = count // devices
    x = x_ref[...]
    sums = dot(x, cells_ref[...].astype(jnp.bfloat16))
    bands = [place] + [look_up(route, place) for route in routes]
    starts = [pl.multiple_of(band * rows, rows) for band in bands]
    high = jnp.concatenate([waves_ref[pl.ds(start, rows), :] for start in starts], axis=0)
    low = jnp.concatenate([waves_ref[pl.ds(count + start, rows), :] for start in starts], axis=0)
    across = (((1,), (1,)), ((), ()))
    row = lax.broadcasted_iota(jnp.int32, (CORNER_ROWS, LANES), 0)
    lane = lax.broadcasted_iota(jnp.int32, (CORNER_ROWS, LANES), 1)
    first = ((row == 0) & (lane == 0)) | ((row == 1) & (lane == SIDE - 1))
    last = ((row == 2) & (lane == LANES - SIDE)) | ((row == 3) & (lane == LANES - 1))
    first, last = (jnp.where(hit, 1.0, 0.0).astype(jnp.bfloat16) for hit in (first, last))
    corners = lax.dot_general(first, x[:, :LANES], across, preferred_element_type=jnp.float32)
    corners += lax.dot_general(
        last, x[:, SIDE * SIDE - LANES :], across, preferred_element_type=jnp.float32
    )
    corners = corners.astype(jnp.bfloat16)
    corner_spectra = lax.dot_general(corners, high, across, preferred_element_type=jnp.float32)
    corner_spectra += lax.dot_general(corners, low, across, preferred_element_type=jnp.float32)
    sums_high = sums.astype(jnp.bfloat16)
    sums_low = (sums - sums_high.astype(jnp.float32)).astype(jnp.bfloat16)
    spectra = dot(
        jnp.concatenate([high, high, low], axis=1), jnp.concatenate([sums_high, sums_low, sums_high], axis=0)
    )
    spectra = spectra.astype(jnp.bfloat16)
    lane_start = (place % 2) * (LANES // 2) + (place // 2) * rows
    lane = lax.broadcasted_iota(jnp.int32, (CORNER_ROWS, LANES), 1)
    mine = (lane >= lane_start) & (lane < lane_start + rows)
    for step in range(devices):
        block = spectra[step * rows : (step + 1) * rows]
        outs[step][0:rows, :] = block[:, :LANES]
        outs[step][rows : 2 * rows, :] = block[:, LANES:]
        turned = pltpu.roll(corner_spectra, lax.rem(lane_start - step * rows + LANES, LANES), 1)
        outs[step][2 * rows : 2 * rows + CORNER_ROWS, :] = jnp.where(mine, turned, 0.0).astype(jnp.bfloat16)
    fill_slots(ids_ref, near_ids_ref, codes_ref, slot_ref, near_ref, kept_codes_ref)
    for partner in range(paired_ref.shape[1]):
        partner_ref[0, partner] = slot_ref[paired_ref[0, partner]]


def collect_kernel(band_routes, tile_routes, place_ref, tile_ref, rim_map_ref, *rest):
    devices, arrivals = len(band_routes) + 1, len(tile_routes) + 1
    blocks, rest = rest[:devices], rest[devices:]
    bands, (height_ref, held_ref) = rest[:arrivals], rest[arrivals:]
    place = place_ref[0]
    rows = (blocks[0].shape[0] - CORNER_ROWS) // 2
    total = height_ref.shape[0]
    corners = jnp.zeros((CORNER_ROWS, LANES), jnp.float32)
    for step in range(devices):
        source = look_up(senders(band_routes[step - 1]), place) if step else place
        field, half = source % 2, source // 2
        start = pl.multiple_of(field * total + half * rows, rows)
        held_ref[pl.ds(start, rows), :] = blocks[step][0:rows, :]
        held_ref[pl.ds(2 * total + start, rows), :] = blocks[step][rows : 2 * rows, :]
        corners += blocks[step][2 * rows :, :].astype(jnp.float32)
    height_ref[...] = held_ref[0:total, :]
    row = lax.broadcasted_iota(jnp.int32, (CORNER_ROWS, 2 * LANES), 0)
    lane = lax.broadcasted_iota(jnp.int32, (CORNER_ROWS, 2 * LANES), 1)
    first = jnp.where(lane < LANES, HEIGHT_CORNER_LANE, CORNER_LANE)
    spread = jnp.where((lane % HALF == row + first) & (row < 4), 1.0, 0.0).astype(jnp.bfloat16)
    corners = lax.dot_general(
        corners.astype(jnp.bfloat16), spread, (((0,), (0,)), ((), ())), preferred_element_type=jnp.float32
    )
    corners = corners[:total, :LANES] + corners[total:, LANES:]
    lane = lax.broadcasted_iota(jnp.int32, (total // 2, LANES), 1)
    rims = held_ref[2 * total : 3 * total, :]
    for step in range(arrivals):
        bands[step][0:total, :] = held_ref[total : 2 * total, :]
        bands[step][total : 2 * total, :] = held_ref[3 * total : 4 * total, :]
        receiver = look_up(tile_routes[step - 1], tile_ref[0]) if step else tile_ref[0]
        columns = pl.ds(pl.multiple_of(receiver * LANES, LANES), LANES)
        part = dot(rims, rim_map_ref[:, columns]) + corners
        packed = jnp.where(lane < HALF, part[: total // 2], part[total // 2 :])
        bands[step][2 * total :, :] = packed.astype(jnp.bfloat16)


def rim_lane(edge, position):
    return RIM_LANES[edge] + (position // 2 if edge in (NORTH, SOUTH) else position)


def rim_cell(edge, position):
    across = SIDE // 4
    if edge == NORTH:
        return position
    if edge == EAST:
        return position * across + across - 1
    if edge == SOUTH:
        return LANES - across + position
    return position * across


def turn(position, reverse):
    return position + reverse * (BLOCKS - 1 - 2 * position)


def fill_slots(ids_ref, near_ids_ref, codes_ref, slot_ref, near_ref, kept_codes_ref):
    slots = ids_ref.shape[0]

    def invert(slot, carry):
        slot_ref[ids_ref[slot]] = slot
        return carry

    def find(slot, carry):
        for edge in range(4):
            near_ref[slot, edge] = slot_ref[near_ids_ref[slot, edge]]
            kept_codes_ref[slot, edge] = codes_ref[slot, edge]
        return carry

    lax.fori_loop(0, slots, invert, 0, unroll=slots <= 8)
    lax.fori_loop(0, slots, find, 0, unroll=slots <= 8)


def edge_terms(slot, edge, near_ref, codes_ref):
    near = near_ref[slot, edge]
    code = codes_ref[slot, edge]
    touching, reverse = code % 4, code // 4
    beyond_code = codes_ref[near, touching]
    carried = (near, touching, reverse)
    summed = (near_ref[near, touching], beyond_code % 4, jnp.bitwise_xor(reverse, beyond_code // 4))
    ends = []
    for end in range(2):
        rim_edge = look_up([END_RIMS[option][end][0] for option in range(4)], touching)
        rim_end = look_up([END_RIMS[option][end][1] for option in range(4)], touching)
        other_code = codes_ref[near, rim_edge]
        other_end = jnp.bitwise_xor(rim_end, other_code // 4)
        corner = look_up([EDGE_CORNERS[i // 2][i % 2] for i in range(8)], other_code % 4 * 2 + other_end)
        ends.append((near_ref[near, rim_edge], corner, turn((BLOCKS - 1) * end, reverse)))
    return carried, summed, ends


def rim_map_kernel(tile_ref, near_ref, codes_ref, rim_map_ref, wide_ref):
    tile = tile_ref[0]
    wide_ref[...] = jnp.zeros_like(wide_ref)
    block = lax.broadcasted_iota(jnp.int32, (BLOCKS, LANES), 0)
    lane = lax.broadcasted_iota(jnp.int32, (BLOCKS, LANES), 1) % HALF

    def fill(slot, carry):
        columns = pl.ds(pl.multiple_of(slot * LANES, LANES), LANES)
        for edge in range(4):
            carried, summed, _ = edge_terms(slot, edge, near_ref, codes_ref)
            for base, (source, source_edge, reverse) in ((0, carried), (4 * BLOCKS, summed)):
                hit = (lane == rim_lane(edge, turn(block, reverse))) & (source == tile)
                start = pl.multiple_of(base + source_edge * BLOCKS, BLOCKS)
                wide_ref[pl.ds(start, BLOCKS), columns] += hit.astype(jnp.float32)
        return carry

    slots = near_ref.shape[0]
    lax.fori_loop(0, slots, fill, 0, unroll=slots <= 8)
    rim_map_ref[...] = wide_ref[...].astype(jnp.bfloat16)


def partner_map_kernel(
    routes,
    tile_ref,
    near_ref,
    codes_ref,
    partner_ref,
    velocity_map_ref,
    rim_map_ref,
    chosen_ref,
    arrival_ref,
    wide_ref,
    rim_ref,
):
    tile = tile_ref[0]
    row = lax.broadcasted_iota(jnp.int32, (LANES, LANES), 0) % HALF
    cell = lax.broadcasted_iota(jnp.int32, (LANES, LANES), 1)
    placed = jnp.zeros((LANES, LANES), jnp.bool_)
    for edge in range(4):
        count = SIDE // 4 if edge in (NORTH, SOUTH) else BLOCKS
        position = row - RIM_LANES[edge]
        placed |= (position >= 0) & (position < count) & (cell == rim_cell(edge, position))
    placed = placed.astype(jnp.float32)
    wide_ref[...] = jnp.zeros_like(wide_ref)
    rim_ref[...] = jnp.zeros_like(rim_ref)
    rim_ref[0:LANES, 0:LANES] = placed
    for step, route in enumerate(routes):
        sent = look_up([float(receiver != sender) for sender, receiver in enumerate(route)], tile, jnp.float32)
        rim_ref[(step + 1) * LANES : (step + 2) * LANES, 0:LANES] = placed * sent
    for sender in range(len(routes[0])):
        steps = [0] * len(routes[0])
        for step, route in enumerate(routes):
            if route[sender] != sender:
                steps[route[sender]] = step + 1
        arrival_ref[sender] = look_up(steps, tile)
    block = lax.broadcasted_iota(jnp.int32, (BLOCKS, LANES), 0)
    cell = lax.broadcasted_iota(jnp.int32, (BLOCKS, LANES), 1)
    corner_row = lax.broadcasted_iota(jnp.int32, (8, LANES), 0)
    corner_cell = lax.broadcasted_iota(jnp.int32, (8, LANES), 1)
    step = lax.broadcasted_iota(jnp.int32, (chosen_ref.shape[0], LANES), 0)

    def target(edge, position):
        return rim_cell(edge, position // 2 if edge in (NORTH, SOUTH) else position)

    def add_corners(ends, edge, first_lane, columns):
        for source, corner, position in ends:
            hit = (corner_row == corner) & (corner_cell == target(edge, position))
            for base in (first_lane, HALF + first_lane):
                start = pl.multiple_of(arrival_ref[source] * LANES + base, 8)
                rim_ref[pl.ds(start, 8), columns] += hit.astype(jnp.float32)

    for edge in range(4):
        _, _, ends = edge_terms(tile, edge, near_ref, codes_ref)
        add_corners(ends, edge, HEIGHT_CORNER_LANE, slice(0, LANES))
    for partner in range(partner_ref.shape[1]):
        slot = partner_ref[0, partner]
        columns = slice(partner * LANES, (partner + 1) * LANES)
        rim_columns = slice((partner + 1) * LANES, (partner + 2) * LANES)
        chosen_ref[:, columns] = (step == arrival_ref[slot]).astype(jnp.float32)
        for edge in range(4):
            carried, summed, ends = edge_terms(slot, edge, near_ref, codes_ref)
            for base, (source, source_edge, reverse) in ((0, carried), (4 * BLOCKS, summed)):
                hit = cell == target(edge, turn(block, reverse))
                start = pl.multiple_of(arrival_ref[source] * LANES + base + source_edge * BLOCKS, BLOCKS)
                wide_ref[pl.ds(start, BLOCKS), columns] += hit.astype(jnp.float32)
            add_corners(ends, edge, CORNER_LANE, rim_columns)
    velocity_map_ref[...] = wide_ref[...].astype(jnp.bfloat16)
    rim_map_ref[...] = rim_ref[...].astype(jnp.bfloat16)


def add_arrivals(height, velocity, first, bands, velocity_map_ref, rim_map_ref, chosen_ref):
    total = height.shape[0]
    partners = velocity.shape[1] // LANES
    rows = slice(first * LANES, (first + len(bands)) * LANES)
    rims = jnp.concatenate([band[2 * total :, :] for band in bands], axis=1)
    first_half = lax.broadcasted_iota(jnp.int32, rims.shape, 1) % LANES < HALF
    rims = rims.astype(jnp.float32)
    rims = jnp.concatenate([jnp.where(first_half, rims, 0.0), jnp.where(first_half, 0.0, rims)], axis=0)
    rims = dot(rims.astype(jnp.bfloat16), rim_map_ref[rows, :])
    pairs = jnp.concatenate([band[total : 2 * total, :] for band in bands], axis=1)
    velocity = velocity + dot(pairs, velocity_map_ref[rows, :]) + rims[:, LANES:]
    for step, band in enumerate(bands):
        own = band[0:total, :].astype(jnp.float32)
        chosen = chosen_ref[first + step : first + step + 1, :]
        velocity += jnp.concatenate([own] * partners, axis=1) * chosen
    return height + rims[:, :LANES], velocity


def early_kernel(height_ref, velocity_map_ref, rim_map_ref, chosen_ref, *rest):
    bands, (height_sum_ref, velocity_sum_ref) = rest[:-2], rest[-2:]
    height = height_ref[...].astype(jnp.float32)
    velocity = jnp.zeros(velocity_sum_ref.shape, jnp.float32)
    height, velocity = add_arrivals(height, velocity, 0, bands, velocity_map_ref, rim_map_ref, chosen_ref)
    height_sum_ref[...] = height
    velocity_sum_ref[...] = velocity


def density_kernel(
    early, partners, scale, per_band, height_ref, velocity_ref, velocity_map_ref, rim_map_ref, chosen_ref, *rest
):
    bands, (out_ref, cross_ref, sent) = rest[:-3], rest[-3:]
    total = height_ref.shape[0]
    height, velocity = add_arrivals(
        height_ref[...], velocity_ref[...], early, bands, velocity_map_ref, rim_map_ref, chosen_ref
    )
    velocity = velocity.astype(jnp.bfloat16)
    height = height.astype(jnp.bfloat16).astype(jnp.float32)
    row = lax.broadcasted_iota(jnp.int32, height.shape, 0)
    rotated = jnp.where(
        (row // per_band) % 2 == 0,
        pltpu.roll(height, total - per_band, 0),
        -pltpu.roll(height, per_band, 0),
    )
    turned = jnp.concatenate([height.T, rotated.T], axis=0)
    lane = lax.broadcasted_iota(jnp.int32, turned.shape, 1)
    copies = []
    for frequency in range(per_band):
        left = jnp.where(lane % per_band == frequency, turned, 0.0).astype(jnp.bfloat16)
        cross = dot(left, velocity) * scale
        for partner in range(partners):
            for part in range(2):
                index = (partner * 2 + part) * per_band + frequency
                rows = pl.ds(index * LANES, LANES)
                cross_ref[rows, :] = cross[
                    part * LANES : (part + 1) * LANES, partner * LANES : (partner + 1) * LANES
                ]
                copies.append(pltpu.make_async_copy(cross_ref.at[rows], out_ref.at[rows], sent.at[index]))
                copies[-1].start()
    for copy in copies:
        copy.wait()


SMEM = pl.BlockSpec(memory_space=pltpu.SMEM)
VMEM = pl.BlockSpec(memory_space=pltpu.VMEM)


def kept(shape, dtype):
    return pltpu.VMEM(shape, dtype)


def scalars(shape, dtype):
    return pltpu.SMEM(shape, dtype)


def near_scalars(value):
    return pltpu.with_memory_space_constraint(value, pltpu.SMEM)


def near(value):
    return pltpu.with_memory_space_constraint(value, pltpu.VMEM)


def shards(tiles, freqs, field_count, fields, slot_tile_ids, neighbour_tile_ids, neighbour_rotation_code, paired_tile_ids):
    field = fields.reshape(fields.shape[2], fields.shape[3])
    samples = field.shape[0]
    devices = freqs * field_count
    per_band = FREQS // devices
    rows = samples // SEGLEN * 2 * per_band
    total = freqs * rows
    partners = paired_tile_ids.shape[1]
    tile = lax.axis_index("tiles").astype(jnp.int32).reshape(1)
    place = (lax.axis_index("freq") * field_count + lax.axis_index("field")).astype(jnp.int32).reshape(1)

    band_routes = routes_for(devices, BAND_ROUTES)
    tile_routes = routes_for(tiles, TILE_ROUTES)
    arrivals = len(tile_routes) + 1

    piece = kept((2 * rows + CORNER_ROWS, LANES), jnp.bfloat16)
    slots = slot_tile_ids.shape[0]
    near_slots, codes, partner_slots, *pieces = pl.pallas_call(
        functools.partial(transform_kernel, band_routes),
        out_shape=[
            scalars((slots, 4), jnp.int32),
            scalars((slots, 4), jnp.int32),
            scalars((1, partners), jnp.int32),
        ]
        + [piece] * devices,
        in_specs=[SMEM] * 5 + [VMEM] * 3,
        out_specs=[SMEM] * 3 + [VMEM] * devices,
        scratch_shapes=[pltpu.SMEM((slots,), jnp.int32)],
        name="transform",
    )(
        place,
        slot_tile_ids,
        neighbour_tile_ids,
        neighbour_rotation_code,
        paired_tile_ids,
        field,
        cell_table(),
        time_table(devices, samples),
    )
    near_slots, codes, partner_slots = map(near_scalars, (near_slots, codes, partner_slots))
    pieces = [pieces[0]] + [
        lax.ppermute(piece, ("freq", "field"), list(enumerate(route)))
        for piece, route in zip(pieces[1:], band_routes)
    ]

    rim_map = pl.pallas_call(
        rim_map_kernel,
        out_shape=kept((LANES, slots * LANES), jnp.bfloat16),
        in_specs=[SMEM] * 3,
        out_specs=VMEM,
        scratch_shapes=[pltpu.VMEM((LANES, slots * LANES), jnp.float32)],
        name="rim_map",
    )(tile, near_slots, codes)

    *sent, height = pl.pallas_call(
        functools.partial(collect_kernel, band_routes, tile_routes),
        out_shape=[kept((5 * total // 2, LANES), jnp.bfloat16)] * arrivals + [kept((total, LANES), jnp.bfloat16)],
        in_specs=[SMEM] * 2 + [VMEM] * (1 + devices),
        out_specs=[VMEM] * (arrivals + 1),
        scratch_shapes=[pltpu.VMEM((4 * total, LANES), jnp.bfloat16)],
        name="collect",
    )(place, tile, *map(near, (rim_map, *pieces)))

    velocity_map, rim_map, chosen = pl.pallas_call(
        functools.partial(partner_map_kernel, tile_routes),
        out_shape=[
            kept((arrivals * LANES, partners * LANES), jnp.bfloat16),
            kept((arrivals * LANES, (1 + partners) * LANES), jnp.bfloat16),
            kept((arrivals + -arrivals % 8, partners * LANES), jnp.float32),
        ],
        in_specs=[SMEM] * 4,
        out_specs=[VMEM] * 3,
        scratch_shapes=[
            pltpu.SMEM((slots,), jnp.int32),
            pltpu.VMEM((arrivals * LANES, partners * LANES), jnp.float32),
            pltpu.VMEM((arrivals * LANES, (1 + partners) * LANES), jnp.float32),
        ],
        name="partner_map",
    )(tile, near_slots, codes, partner_slots)

    bands = [sent[0]]
    for band, route in zip(sent[1:], tile_routes):
        pairs = []
        for sender, receiver in enumerate(route):
            for core in range(field_count):
                there = receiver * field_count + (core if receiver != sender else field_count - 1 - core)
                pairs.append((sender * field_count + core, there))
        bands.append(lax.ppermute(band, ("tiles", "field"), pairs))

    early = arrivals - 2
    height, velocity = pl.pallas_call(
        early_kernel,
        out_shape=[kept((total, LANES), jnp.float32), kept((total, partners * LANES), jnp.float32)],
        in_specs=[VMEM] * (4 + early),
        out_specs=[VMEM] * 2,
        name="early",
    )(*map(near, (height, velocity_map, rim_map, chosen, *bands[:early])))

    segments = freqs * samples // SEGLEN
    scale = 1.0 / (segments * SEGLEN * 0.375)
    blocks = partners * 2 * per_band
    density = pl.pallas_call(
        functools.partial(density_kernel, early, partners, scale, per_band),
        out_shape=jax.ShapeDtypeStruct((blocks * LANES, LANES), jnp.float32),
        in_specs=[VMEM] * (5 + arrivals - early),
        out_specs=pl.BlockSpec(memory_space=pl.ANY),
        scratch_shapes=[
            pltpu.VMEM((blocks * LANES, LANES), jnp.float32),
            pltpu.SemaphoreType.DMA((blocks,)),
        ],
        name="density",
    )(*map(near, (height, velocity, velocity_map, rim_map, chosen, *bands[early:])))
    return density.reshape(1, partners, 2, per_band, LANES, LANES)


def solution(mesh):
    placed = (P("field", "tiles", ("groups", "freq"), None), P(), P(), P(), P("tiles", None))
    return jax.shard_map(
        functools.partial(shards, mesh.shape["tiles"], mesh.shape["freq"], mesh.shape["field"]),
        mesh=mesh,
        in_specs=placed,
        out_specs=P(("groups", "tiles"), None, None, ("freq", "field"), None, None),
        check_vma=False,
    )
```
